32 devices in a mesh: op: 8 (over y, x, core), sec: 4 (over z).
Axes of the slice: x: 2, y: 2, z: 4, core: 2. Of those that a mesh axis runs over, the one named last changes fastest.
Arguments:
- wavefunction: bfloat16 [16, 256, 256], P('sec'), may hold values from -6 to 6
- left_operators: bfloat16 [32, 16, 256, 256], P('op', 'sec'), may hold values from -0.375 to 0.375
- right_operators: bfloat16 [32, 16, 256, 256], P('op', 'sec'), may hold values from -0.375 to 0.375
- rotations: bfloat16 [16, 256, 256], P('sec'), may hold values from -0.375 to 0.375
- charges: int32 [32], P('op'), may hold values from -1 to 1
- present_blocks: int32 [32, 16], P('op', 'sec'), may hold values 0 or 1
- directions: int32 [32, 1], P('op'), may hold values from 0 to 3, as said below
Outputs:
- sigma_vector: float32 [16, 256, 256], P('sec', 'op')
- regrouped: bfloat16 [64, 16, 256, 256], P('op', 'sec')
The draws below stay inside these ranges and needn't reach their ends.
Inputs may be any that keep to these rules, and one draw needn't show every extreme that they name: `directions`: among the pairs of one index of op, each direction is named by at most 2 pairs, some direction is named by exactly 2, and every direction other than 0 is named at least once.
All inputs are finite; a program needn't handle non-finite values. No bound on the sum of `present_blocks` on one device may be relied on, other than what follows from the above.
Results may differ from the reference program's by a relative error of at most 0.0049.
Values may be sent and summed in bfloat16 or wider, within the bound.
No kernel may reach another device: no remote copies, remote signals or barrier semaphores. Data moves between devices by JAX's collectives and lax.ppermute only.
A program may use at most 64 MiB of HBM per device.

```python
import math
import jax
import jax.numpy as jnp
from jax import lax

MB = 256
P_DEV = 4
DIRS = 4
CAPS = 2
NSEC = 16
PAIRS = 32
N_OP = 8


def draw_directions(key, part):
    owners = PAIRS // P_DEV
    first_key = jax.random.fold_in(key, 71)
    second_key = jax.random.fold_in(key, 72)
    extra = jax.random.randint(first_key, (owners,), 1, DIRS).astype(jnp.int32)
    base = (jnp.arange(P_DEV, dtype=jnp.int32) % DIRS).astype(jnp.int32)
    column = jnp.arange(P_DEV, dtype=jnp.int32)[None, :]
    layout = jnp.where(column == 0, extra[:, None], base[None, :]).astype(jnp.int32)
    row_keys = jax.random.split(second_key, owners)
    shuffled = jax.vmap(lambda row_key, row: jax.random.permutation(row_key, row))(row_keys, layout)
    return shuffled.reshape(PAIRS, 1).astype(jnp.int32)


def plant(drawn, rng, smallest, largest):
    index_at = [jax.random.randint(jax.random.fold_in(rng, axis), (), 0, length) for axis, length in enumerate(drawn.shape)]
    widest = drawn.shape.index(max(drawn.shape))
    next_to = index_at[:widest] + [(index_at[widest] + 1) % drawn.shape[widest]] + index_at[widest + 1:]
    return drawn.at[tuple(index_at)].set(smallest).at[tuple(next_to)].set(largest)


def level_of(rng, extent, shards, smallest, top_value):
    def one(dim, parts):
        heights = jax.random.uniform(jax.random.fold_in(jax.random.fold_in(rng, 6), dim), (parts,), jnp.float32, smallest / len(shards), top_value / len(shards))
        return jnp.repeat(jnp.exp(heights), extent[dim] // parts).reshape((-1,) + (1,) * (len(extent) - dim - 1))

    factor_of = one(*shards[0])
    for cut in shards[1:]:
        factor_of = factor_of * one(*cut)
    return factor_of


def noise(stream_key, dims, width, reach, cuts=(), kind=jnp.bfloat16):
    result = width * jax.random.normal(stream_key, dims, jnp.float32)
    if cuts:
        result = result * level_of(stream_key, dims, cuts, -0.22, 0.18)
    return jnp.clip(result, -reach, reach).astype(kind)


def setup_inputs(seed: int = 0) -> dict:
    keys = jax.random.split(jax.random.key(seed), 8)
    return {
        "wavefunction": noise(keys[0], (NSEC, MB, MB), 1.0, 6.0, ((0, 4),)),
        "left_operators": noise(keys[1], (PAIRS, NSEC, MB, MB), MB ** -0.5, 0.375, ((0, 8), (1, 4))),
        "right_operators": noise(keys[2], (PAIRS, NSEC, MB, MB), MB ** -0.5, 0.375, ((0, 8), (1, 4))),
        "rotations": noise(keys[3], (NSEC, MB, MB), MB ** -0.5, 0.375, ((0, 4),)),
        "charges": plant(jax.random.randint(keys[4], (PAIRS,), -1, 2), jax.random.fold_in(keys[4], 1), -1, 1).astype(jnp.int32),
        "present_blocks": plant((jax.random.randint(keys[5], (PAIRS, NSEC), 0, 4) < 3).astype(jnp.int32), jax.random.fold_in(keys[5], 1), 0, 1),
        "directions": draw_directions(jax.random.fold_in(keys[7], 71), 0),
    }


def reference(wavefunction, left_operators, right_operators, rotations, charges, present_blocks, directions):
    psi_full = wavefunction.astype(jnp.float32)
    rot_full = rotations.astype(jnp.float32)
    rot_padded = jnp.pad(rot_full, ((1, 1), (0, 0), (0, 0)))
    sectors = jnp.arange(NSEC, dtype=jnp.int32)

    def per_pair(carry, inputs):
        left, right, charge, present = inputs
        weight = present.astype(jnp.float32)[:, None, None]
        halfway = jnp.einsum('sij,sjk->sik', left.astype(jnp.float32), psi_full).astype(jnp.bfloat16)
        products = jnp.einsum('sik,smk->sim', halfway.astype(jnp.float32), right.astype(jnp.float32)) * weight
        indices = (sectors + 1 + charge).astype(jnp.int32)
        carry = carry.at[indices].add(products)
        rotated = jnp.einsum('sij,sjk->sik', left.astype(jnp.float32), rot_full).astype(jnp.bfloat16)
        target = rot_padded[indices]
        renormed = (jnp.einsum('sji,sjk->sik', target, rotated.astype(jnp.float32)) * weight).astype(jnp.bfloat16)
        return (carry, renormed)
    start = jnp.zeros((NSEC + 2, MB, MB), jnp.float32)
    extended, renormed = lax.scan(per_pair, start, (left_operators, right_operators, charges, present_blocks))
    sigma_vector = extended[1:NSEC + 1] / math.sqrt(PAIRS)
    kinds = directions[:, 0].reshape(N_OP, P_DEV)
    matching = kinds[:, :, None] == kinds[:, None, :]
    earlier = jnp.arange(P_DEV)[None, :] < jnp.arange(P_DEV)[:, None]
    position = lax.optimization_barrier(jnp.sum(jnp.logical_and(matching, earlier[None]), axis=2)).astype(jnp.int32).reshape(PAIRS)
    offsets = jnp.array([0, 1, -1, N_OP // 2], dtype=jnp.int32)
    kind_flat = directions[:, 0].astype(jnp.int32)
    device = (jnp.arange(PAIRS, dtype=jnp.int32) // P_DEV).astype(jnp.int32)
    destination = (device + offsets[kind_flat]) % N_OP
    slot_index = (destination * DIRS * CAPS + kind_flat * CAPS + position).astype(jnp.int32)
    regrouped = jnp.zeros((N_OP * DIRS * CAPS, NSEC, MB, MB), jnp.bfloat16).at[slot_index].set(renormed)
    return (sigma_vector, regrouped)
```

```python
import functools
import math

import jax
import jax.numpy as jnp
from jax import lax
from jax.experimental import pallas as pl
from jax.experimental.pallas import tpu as pltpu
from jax.sharding import PartitionSpec as P

DIRS = 4
CAPS = 2
META = 16
VMEM_LIMIT = 28 * 1024 * 1024

BF16 = jnp.bfloat16
F32 = jnp.float32
ANY = pl.BlockSpec(memory_space=pl.ANY)
SMEM = pl.BlockSpec(memory_space=pltpu.SMEM)
VMEM = pl.BlockSpec(memory_space=pltpu.VMEM)


def params():
    return pltpu.CompilerParams(vmem_limit_bytes=VMEM_LIMIT)


def cost(flops, moved):
    return pl.CostEstimate(flops=flops, bytes_accessed=moved, transcendentals=0)


def ranks(directions_ref, count):
    kinds = [directions_ref[p, 0] for p in range(count)]
    places = []
    for p in range(count):
        place = jnp.int32(0)
        for q in range(p):
            place = place + jnp.where(kinds[q] == kinds[p], 1, 0)
        places.append(place)
    return kinds, places


def pick(kinds, places, kind, place):
    index = jnp.int32(0)
    for p, (own, at) in enumerate(zip(kinds, places)):
        match = at == place if kind is None else jnp.logical_and(at == place, own == kind)
        index = index + jnp.where(match, p, 0)
    return index


def gather_kernel(roles, directions_ref, charges_ref, present_ref, left_ref, *refs):
    outs, (meta, sem) = refs[: len(roles)], refs[len(roles) :]
    count, sectors, width, _ = left_ref.shape
    kinds, places = ranks(directions_ref, count)
    odd = lax.rem(lax.axis_index("op"), 2)
    copies = []
    slot = 0
    chosen = []
    for out, wanted in zip(outs, roles):
        base = 0
        for role in wanted:
            if role == "extra":
                index = pick(kinds, places, None, 1)
            elif role == "half":
                index = pick(kinds, places, 3, 0)
            elif role == "core":
                index = pick(kinds, places, 1 + odd, 0)
            else:
                index = pick(kinds, places, 2 - odd, 0)
            for s in range(sectors):
                copy = pltpu.make_async_copy(
                    left_ref.at[index, s], out.at[pl.ds(base + s * width, width)], sem
                )
                copy.start()
                copies.append(copy)
            chosen.append((index, out, base + sectors * width, slot))
            slot += 1
            base += sectors * width + META
    for index, out, base, slot in chosen:
        row = lax.broadcasted_iota(jnp.int32, (META, width), 0)
        kind = jnp.int32(0)
        for p in range(count):
            kind = kind + jnp.where(index == p, kinds[p], 0)
        values = jnp.where(row == 0, charges_ref[index], jnp.where(row == 1, kind, 0))
        for s in range(sectors):
            values = jnp.where(row == 2 + s, present_ref[index, s], values)
        meta[slot] = values.astype(F32).astype(BF16)
        copy = pltpu.make_async_copy(meta.at[slot], out.at[pl.ds(base, META)], sem)
        copy.start()
        copies.append(copy)
    for copy in copies:
        copy.wait()


def gathered(roles, directions, charges, present, left):
    _, sectors, width, _ = left.shape
    rows = sectors * width + META
    pieces = sum(len(wanted) for wanted in roles)
    return pl.pallas_call(
        functools.partial(gather_kernel, roles),
        out_shape=[jax.ShapeDtypeStruct((rows * len(wanted), width), BF16) for wanted in roles],
        in_specs=[SMEM, SMEM, SMEM, ANY],
        out_specs=[ANY] * len(roles),
        scratch_shapes=[pltpu.VMEM((pieces, META, width), BF16), pltpu.SemaphoreType.DMA],
        compiler_params=params(),
        cost_estimate=cost(0, 4 * rows * width * pieces),
        name="gather_" + "_".join(wanted[0] for wanted in roles),
    )(directions, charges, present, left)


def sigma_kernel(split, chunk, charges_ref, present_ref, left, right, wave, rotations, *refs):
    outs, acc = refs[:-1], refs[-1]
    pair = pl.program_id(0)
    sectors, width = wave.shape[0], wave.shape[1]

    @pl.when(pair == 0)
    def _():
        acc[...] = jnp.zeros_like(acc)
        for s in range(sectors):
            outs[-1][s] = rotations[s].T

    charge = charges_ref[pair]
    for s in range(sectors):
        halfway = jnp.dot(left[0, s], wave[s], preferred_element_type=F32)
        halfway = (halfway * present_ref[pair, s].astype(F32)).astype(BF16)
        term = lax.dot_general(
            halfway, right[0, s], (((1,), (1,)), ((), ())), preferred_element_type=F32
        )
        at = jnp.clip(s + 1 + charge, 0, sectors + 1)
        acc[at] += term

    @pl.when(pair == pl.num_programs(0) - 1)
    def _():
        if not split:
            outs[0][...] = acc[...]
            return
        bit = lax.rem(lax.axis_index("op"), 2)
        for q in range(width // chunk // 2):
            to = slice(q * chunk, (q + 1) * chunk)
            for t in range(sectors + 2):
                outs[0][t, to] = acc[t, pl.ds((2 * q + 1 - bit) * chunk, chunk)].astype(BF16)
                outs[1][t, to] = acc[t, pl.ds((2 * q + bit) * chunk, chunk)]


def sigma_terms(split, chunk, charges, present, left, right, wave, rotations):
    count, sectors, width, _ = left.shape
    whole = pl.BlockSpec((sectors, width, width), lambda p: (0, 0, 0))
    by_pair = pl.BlockSpec((1, sectors, width, width), lambda p: (p, 0, 0, 0))
    if split:
        shapes = [((sectors + 2, width // 2, width), BF16), ((sectors + 2, width // 2, width), F32)]
    else:
        shapes = [((sectors + 2, width, width), F32)]
    shapes.append(((sectors, width, width), BF16))
    return pl.pallas_call(
        functools.partial(sigma_kernel, split, chunk),
        grid=(count,),
        out_shape=[jax.ShapeDtypeStruct(*shape) for shape in shapes],
        in_specs=[SMEM, SMEM, by_pair, by_pair, whole, whole],
        out_specs=[pl.BlockSpec(shape, lambda p: (0, 0, 0)) for shape, _ in shapes],
        scratch_shapes=[pltpu.VMEM((sectors + 2, width, width), F32)],
        compiler_params=params(),
        cost_estimate=cost(4 * count * sectors * width**3, 4 * left.size + 4 * left.size),
        name="sigma_terms",
    )(charges, present, left, right, wave, rotations)


def edges_kernel(keep, got, turned, up, down, mid):
    height = keep.shape[1]
    sectors = mid.shape[0]
    up[:height] = (keep[sectors + 1] + got[sectors + 1].astype(F32)).astype(BF16)
    up[height:] = turned[sectors - 1]
    down[:height] = (keep[0] + got[0].astype(F32)).astype(BF16)
    down[height:] = turned[0]
    for s in range(sectors):
        mid[s] = keep[s + 1] + got[s + 1].astype(F32)


def edges(keep, got, turned):
    outer, height, width = keep.shape
    rows = height + turned.shape[1]
    return pl.pallas_call(
        edges_kernel,
        out_shape=[
            jax.ShapeDtypeStruct((rows, width), BF16),
            jax.ShapeDtypeStruct((rows, width), BF16),
            jax.ShapeDtypeStruct((outer - 2, height, width), F32),
        ],
        in_specs=[VMEM] * 3,
        out_specs=[VMEM] * 3,
        compiler_params=params(),
        cost_estimate=cost(keep.size, 12 * keep.size),
        name="edges",
    )(keep, got, turned)


def split_kernel(bit, chunk, first, *refs):
    if first:
        mid, below, above, send, keep = refs
    else:
        mid, got, send, keep = refs
    sectors, height, _ = mid.shape
    own = lax.rem(lax.axis_index("op") // bit, 2)

    def total(s, rows):
        value = mid[s, rows]
        if not first:
            return value + got[s, rows].astype(F32)
        if s == 0:
            value = value + below[rows].astype(F32)
        if s == sectors - 1:
            value = value + above[rows].astype(F32)
        return value

    for q in range(height // chunk // 2):
        to = slice(q * chunk, (q + 1) * chunk)
        for s in range(sectors):
            send[s, to] = total(s, pl.ds((2 * q + 1 - own) * chunk, chunk)).astype(BF16)
            keep[s, to] = total(s, pl.ds((2 * q + own) * chunk, chunk))


def split(bit, chunk, first, mid, *more):
    sectors, height, width = mid.shape
    return pl.pallas_call(
        functools.partial(split_kernel, bit, chunk, first),
        out_shape=[
            jax.ShapeDtypeStruct((sectors, height // 2, width), BF16),
            jax.ShapeDtypeStruct((sectors, height // 2, width), F32),
        ],
        in_specs=[VMEM] * (1 + len(more)),
        out_specs=[VMEM] * 2,
        compiler_params=params(),
        cost_estimate=cost(mid.size, 10 * mid.size),
        name="split",
    )(mid, *more)


def renorm_kernel(items, zero, offset, turned_ref, rotations_ref, below_ref, above_ref, *refs):
    buffers = refs[: 1 + max(item[0] for item in items)]
    rest = refs[len(buffers) :]
    if not zero:
        rest = rest[1:]
    out, rot, turned, blocks, results, metas, sems, done = rest
    sectors, width, _ = rotations_ref.shape
    odd = lax.rem(lax.axis_index("op"), 2)
    last = sems.shape[0] - 1
    first = [
        pltpu.make_async_copy(rotations_ref, rot, sems.at[last]),
        pltpu.make_async_copy(turned_ref, turned.at[pl.ds(1, sectors)], sems.at[last]),
        pltpu.make_async_copy(below_ref.at[pl.ds(offset, width)], turned.at[0], sems.at[last]),
        pltpu.make_async_copy(
            above_ref.at[pl.ds(offset, width)], turned.at[sectors + 1], sems.at[last]
        ),
    ]
    for copy in first:
        copy.start()
    loads = []
    for i, (buffer, base, _, _) in enumerate(items):
        source = buffers[buffer]
        copies = [
            pltpu.make_async_copy(
                source.at[pl.ds(base + sectors * width, META)], metas.at[i], sems.at[i]
            )
        ]
        for s in range(sectors):
            copies.append(
                pltpu.make_async_copy(
                    source.at[pl.ds(base + s * width, width)], blocks.at[i, s], sems.at[i]
                )
            )
        for copy in copies:
            copy.start()
        loads.append(copies)
    stores = []
    for copy in first:
        copy.wait()
    for i, (_, _, kind, place) in enumerate(items):
        for copy in loads[i]:
            copy.wait()
        values = metas[i].astype(F32)

        def scalar(row):
            return jnp.max(values[row : row + 1, :])

        charge = scalar(0).astype(jnp.int32)
        if kind == "core":
            kind = 2 - odd
        elif kind == "side":
            kind = 1 + odd
        if place == 1:
            wanted = jnp.where(scalar(1).astype(jnp.int32) == kind, 1.0, 0.0)
        else:
            wanted = jnp.float32(1.0)
        for s in range(sectors):
            weight = scalar(2 + s) * wanted
            rotated = jnp.dot(blocks[i, s], rot[s], preferred_element_type=F32).astype(BF16)
            target = turned[jnp.clip(s + 1 + charge, 0, sectors + 1)]
            value = jnp.dot(target, rotated, preferred_element_type=F32) * weight
            results[i, s] = value.astype(BF16)
        copy = pltpu.make_async_copy(results.at[i], out.at[kind * CAPS + place], done)
        copy.start()
        stores.append(copy)
    if zero:
        results[len(items)] = jnp.zeros_like(results[len(items)])
        for place in range(CAPS):
            copy = pltpu.make_async_copy(results.at[len(items)], out.at[place], done)
            copy.start()
            stores.append(copy)
    for copy in stores:
        copy.wait()


def renorm(name, items, buffers, out, offset, turned, rotations, below, above):
    sectors, width, _ = rotations.shape
    zero = out is None
    operands = [turned, rotations, below, above, *buffers] + ([] if zero else [out])
    count = len(items)
    block = (sectors, width, width)
    return pl.pallas_call(
        functools.partial(renorm_kernel, items, zero, offset),
        out_shape=jax.ShapeDtypeStruct((DIRS * CAPS, *block), BF16),
        in_specs=[ANY] * len(operands),
        out_specs=ANY,
        input_output_aliases={} if zero else {len(operands) - 1: 0},
        scratch_shapes=[
            pltpu.VMEM(block, BF16),
            pltpu.VMEM((sectors + 2, width, width), BF16),
            pltpu.VMEM((count, *block), BF16),
            pltpu.VMEM((count + (1 if zero else 0), *block), BF16),
            pltpu.VMEM((count, META, width), BF16),
            pltpu.SemaphoreType.DMA((count + 1,)),
            pltpu.SemaphoreType.DMA,
        ],
        compiler_params=params(),
        cost_estimate=cost(
            4 * count * sectors * width**3, 4 * (count + 2) * sectors * width * width
        ),
        name=name,
    )(*operands)


def body(
    wavefunction, left_operators, right_operators, rotations, charges, present_blocks, directions
):
    sectors, width, _ = wavefunction.shape
    pairs = left_operators.shape[0]
    n = lax.axis_size("op")
    levels = lax.axis_size("sec")
    half = n // 2
    chunk = width // n
    halving = n & (n - 1) == 0 and chunk % 16 == 0
    rows = sectors * width + META

    def over_op(value, target):
        return lax.ppermute(value, "op", [(i, target(i)) for i in range(n)])

    def up(value):
        return lax.ppermute(value, "sec", [(i, i + 1) for i in range(levels - 1)])

    def down(value):
        return lax.ppermute(value, "sec", [(i + 1, i) for i in range(levels - 1)])

    def side(i):
        return (i + 1) % n if i % 2 else (i - 1) % n

    def side_or_across(i):
        place = i % half
        if place == half - 1:
            return i - place
        if place == 0:
            return i + half - 1
        return side(i)

    small = (directions, charges, present_blocks, left_operators)
    (extra,) = gathered((("extra",),), *small)
    extra_half = over_op(extra, lambda i: (i + half) % n)
    first_core, first_side, first_half = gathered(
        (("extra", "core"), ("side",), ("half",)), *small
    )
    from_core = over_op(first_core, lambda i: i ^ 1)
    from_side = over_op(first_side, side)
    from_half = over_op(first_half, lambda i: (i + half) % n)

    *terms, turned = sigma_terms(
        halving,
        chunk,
        charges,
        present_blocks,
        left_operators,
        right_operators,
        wavefunction,
        rotations,
    )
    if halving:
        send, keep = terms
        got = over_op(send, lambda i: i ^ 1)
        above_edge, below_edge, mid = edges(keep, got, turned)
        below, above = up(above_edge), down(below_edge)
        offset = width // 2
        bit = 2
        send, keep = split(bit, chunk, True, mid, below, above)
        got = over_op(send, lambda i: i ^ 2)
        while 2 * bit < n:
            bit *= 2
            send, keep = split(bit, chunk, False, keep, got)
            got = over_op(send, lambda i: i ^ bit)
        summed = keep + got.astype(F32)
    else:
        (terms,) = terms
        offset = width
        below = up(jnp.concatenate([terms[sectors + 1].astype(BF16), turned[sectors - 1]]))
        above = down(jnp.concatenate([terms[0].astype(BF16), turned[0]]))
        mid = terms[1 : sectors + 1]
        mid = mid.at[0].add(below[:width].astype(F32))
        mid = mid.at[sectors - 1].add(above[:width].astype(F32))
        summed = lax.psum_scatter(mid, "op", scatter_dimension=1, tiled=True)
    sigma_vector = summed / math.sqrt(pairs * n)

    place = lax.axis_index("op") % half
    cut = jnp.logical_or(place == 0, place == half - 1)
    relayed = jnp.where(cut, extra_half, extra)
    extra_side = over_op(relayed, side_or_across)

    fixed = (offset, turned, rotations, below, above)
    out = renorm(
        "renorm_core",
        ((0, 0, "core", 1), (0, rows, "core", 0), (1, 0, 3, 1)),
        (from_core, extra_half),
        None,
        *fixed,
    )
    out = renorm("renorm_side", ((0, 0, "side", 0),), (from_side,), out, *fixed)
    out = renorm("renorm_extra", ((0, 0, "side", 1),), (extra_side,), out, *fixed)
    out = renorm("renorm_half", ((0, 0, 3, 0),), (from_half,), out, *fixed)
    return sigma_vector, out


def solution(mesh):
    placed = (
        P("sec", None, None),
        P("op", "sec", None, None),
        P("op", "sec", None, None),
        P("sec", None, None),
        P("op"),
        P("op", "sec"),
        P("op", None),
    )
    return jax.shard_map(
        body,
        mesh=mesh,
        in_specs=placed,
        out_specs=(P("sec", "op", None), P("op", "sec", None, None)),
        check_vma=False,
    )
```

```python
import functools
import math

import jax
import jax.numpy as jnp
from jax import lax
from jax.experimental import pallas as pl
from jax.experimental.pallas import tpu as pltpu
from jax.sharding import PartitionSpec as P

DIRS = 4
CAPS = 2
META = 16

BF16 = jnp.bfloat16
F32 = jnp.float32
ANY = pl.BlockSpec(memory_space=pl.ANY)
HBM = pl.BlockSpec(memory_space=pltpu.HBM)
VMEM = pl.BlockSpec(memory_space=pltpu.VMEM)


def kernel_call(kernel, token, operands, in_specs, out_shape, out_specs, **options):
    mib = options.pop("mib")
    aliases = options.pop("aliases", {})
    grid = options.pop("grid", ())
    ahead = 0 if token is None else 1
    taken = len(operands) + ahead

    def run(*refs):
        refs = list(refs)
        del refs[taken]
        kernel(*refs[ahead:])

    outs = pl.pallas_call(
        run,
        grid=grid,
        out_shape=[jax.ShapeDtypeStruct((8, 128), F32), *out_shape],
        in_specs=[HBM] * ahead + list(in_specs),
        out_specs=[HBM, *out_specs],
        input_output_aliases={i + ahead: o + 1 for i, o in aliases.items()},
        compiler_params=pltpu.CompilerParams(vmem_limit_bytes=mib * 1024 * 1024),
        **options,
    )(*([] if token is None else [token]), *operands)
    return outs[0], list(outs[1:])


def in_hbm(value):
    return pltpu.with_memory_space_constraint(value, pltpu.HBM)


def estimate(flops, moved):
    return pl.CostEstimate(flops=flops, bytes_accessed=moved, transcendentals=0)


def fetch_scalars(pairs, sem):
    copies = [pltpu.make_async_copy(source, kept, sem) for source, kept in pairs]
    for copy in copies:
        copy.start()
    for copy in copies:
        copy.wait()


def pick(kinds, places, kind, place):
    index = jnp.int32(0)
    for p, (own, at) in enumerate(zip(kinds, places)):
        match = at == place if kind is None else jnp.logical_and(at == place, own == kind)
        index = index + jnp.where(match, p, 0)
    return index


def stage_kernel(roles, directions_ref, charges_ref, present_ref, left_ref, wave_ref, rot_ref, *refs):
    outs = refs[: len(roles)]
    left, wave, rot, directions, charges, present, few, sems = refs[len(roles) :]
    bulk = [
        pltpu.make_async_copy(left_ref, left, sems.at[0]),
        pltpu.make_async_copy(wave_ref, wave, sems.at[1]),
        pltpu.make_async_copy(rot_ref, rot, sems.at[2]),
    ]
    for copy in bulk:
        copy.start()
    fetch_scalars(
        [(directions_ref, directions), (charges_ref, charges), (present_ref, present)], few
    )
    count, sectors, width, _ = left_ref.shape
    kinds = [directions[p] for p in range(count)]
    places = []
    for p in range(count):
        place = jnp.int32(0)
        for q in range(p):
            place = place + jnp.where(kinds[q] == kinds[p], 1, 0)
        places.append(place)
    odd = lax.rem(lax.axis_index("op"), 2)
    row = lax.broadcasted_iota(jnp.int32, (META, width), 0)
    bulk[0].wait()
    for out, wanted in zip(outs, roles):
        base = 0
        for role in wanted:
            if role == "extra":
                index = pick(kinds, places, None, 1)
            elif role == "half":
                index = pick(kinds, places, 3, 0)
            elif role == "core":
                index = pick(kinds, places, 1 + odd, 0)
            else:
                index = pick(kinds, places, 2 - odd, 0)
            for s in range(sectors):
                out[base + s * width : base + (s + 1) * width] = left[index, s]
            kind = jnp.int32(0)
            for p in range(count):
                kind = kind + jnp.where(index == p, kinds[p], 0)
            values = jnp.where(row == 0, charges[index], jnp.where(row == 1, kind, 0))
            for s in range(sectors):
                values = jnp.where(row == 2 + s, present[index, s], values)
            base += sectors * width
            out[base : base + META] = values.astype(F32).astype(BF16)
            base += META
    for copy in bulk[1:]:
        copy.wait()


def staged(roles, directions, charges, present, left, wave, rotations):
    count, sectors, width, _ = left.shape
    rows = sectors * width + META
    shapes = [(rows * len(wanted), width) for wanted in roles]
    shapes += [left.shape, wave.shape, rotations.shape]
    return kernel_call(
        functools.partial(stage_kernel, roles),
        None,
        [in_hbm(x) for x in (directions, charges, present, left, wave, rotations)],
        [HBM] * 6,
        [pltpu.VMEM(shape, BF16) for shape in shapes],
        [VMEM] * len(shapes),
        scratch_shapes=[
            pltpu.SMEM((count,), jnp.int32),
            pltpu.SMEM((count,), jnp.int32),
            pltpu.SMEM((count, sectors), jnp.int32),
            pltpu.SemaphoreType.DMA,
            pltpu.SemaphoreType.DMA((3,)),
        ],
        mib=4,
        cost_estimate=estimate(0, 0),
        name="stage",
    )


def sigma_kernel(split, chunk, charges_ref, present_ref, left, right_ref, wave, rotations, *refs):
    outs, (acc, right, charges, present, few, sems) = refs[:-6], refs[-6:]
    count, sectors, width, _ = left.shape
    small = [
        pltpu.make_async_copy(charges_ref, charges, few),
        pltpu.make_async_copy(present_ref, present, few),
    ]
    loads = [pltpu.make_async_copy(right_ref.at[p], right.at[p], sems.at[p]) for p in range(count)]
    for copy in small + loads:
        copy.start()
    acc[...] = jnp.zeros_like(acc)
    for s in range(sectors):
        outs[-1][s] = rotations[s].T
    for copy in small:
        copy.wait()

    def step(pair, carry):
        pltpu.make_async_copy(right_ref.at[pair], right.at[pair], sems.at[pair]).wait()
        charge = charges[pair]
        for s in range(sectors):
            halfway = jnp.dot(left[pair, s], wave[s], preferred_element_type=F32)
            halfway = (halfway * present[pair, s].astype(F32)).astype(BF16)
            term = lax.dot_general(
                halfway, right[pair, s], (((1,), (1,)), ((), ())), preferred_element_type=F32
            )
            acc[jnp.clip(s + 1 + charge, 0, sectors + 1)] += term
        return carry

    lax.fori_loop(0, count, step, 0)
    if not split:
        outs[0][...] = acc[...]
        return
    bit = lax.rem(lax.axis_index("op"), 2)
    for q in range(width // chunk // 2):
        to = slice(q * chunk, (q + 1) * chunk)
        for t in range(sectors + 2):
            outs[0][t, to] = acc[t, pl.ds((2 * q + 1 - bit) * chunk, chunk)].astype(BF16)
            outs[1][t, to] = acc[t, pl.ds((2 * q + bit) * chunk, chunk)]


def sigma_terms(token, split, chunk, charges, present, left, right, wave, rotations):
    count, sectors, width, _ = left.shape
    if split:
        shapes = [((sectors + 2, width // 2, width), BF16), ((sectors + 2, width // 2, width), F32)]
    else:
        shapes = [((sectors + 2, width, width), F32)]
    shapes.append(((sectors, width, width), BF16))
    return kernel_call(
        functools.partial(sigma_kernel, split, chunk),
        token,
        (in_hbm(charges), in_hbm(present), left, in_hbm(right), wave, rotations),
        [HBM, HBM, VMEM, HBM, VMEM, VMEM],
        [pltpu.VMEM(*shape) for shape in shapes],
        [VMEM] * len(shapes),
        scratch_shapes=[
            pltpu.VMEM((sectors + 2, width, width), F32),
            pltpu.VMEM(right.shape, BF16),
            pltpu.SMEM((count,), jnp.int32),
            pltpu.SMEM((count, sectors), jnp.int32),
            pltpu.SemaphoreType.DMA,
            pltpu.SemaphoreType.DMA((count,)),
        ],
        mib=10,
        cost_estimate=estimate(0, 0),
        name="sigma_terms",
    )


def edges_kernel(keep, got, turned, first, second, mid):
    height = keep.shape[1]
    sectors = mid.shape[0]
    odd = lax.rem(lax.axis_index("sec"), 2)
    for out, upward in ((first, odd == 0), (second, odd == 1)):
        edge = jnp.where(upward, sectors + 1, 0)
        out[:height] = (keep[edge] + got[edge].astype(F32)).astype(BF16)
        out[height:] = turned[jnp.where(upward, sectors - 1, 0)]
    for s in range(sectors):
        mid[s] = keep[s + 1] + got[s + 1].astype(F32)


def edges(token, keep, got, turned):
    outer, height, width = keep.shape
    rows = height + turned.shape[1]
    return kernel_call(
        edges_kernel,
        token,
        (keep, got, turned),
        [VMEM] * 3,
        [
            jax.ShapeDtypeStruct((rows, width), BF16),
            jax.ShapeDtypeStruct((rows, width), BF16),
            jax.ShapeDtypeStruct((outer - 2, height, width), F32),
        ],
        [VMEM] * 3,
        mib=6,
        cost_estimate=estimate(keep.size, 12 * keep.size),
        name="edges",
    )


def split_kernel(bit, chunk, levels, first, *refs):
    if first:
        mid, one, two, send, keep = refs
    else:
        mid, got, send, keep = refs
    sectors, height, _ = mid.shape
    own = lax.rem(lax.axis_index("op") // bit, 2)
    level = lax.axis_index("sec")
    odd = lax.rem(level, 2) == 1

    def total(s, rows):
        value = mid[s, rows]
        if not first:
            return value + got[s, rows].astype(F32)
        if s == 0:
            below = jnp.where(odd, one[rows], two[rows]).astype(F32)
            value = value + jnp.where(level > 0, below, 0.0)
        if s == sectors - 1:
            above = jnp.where(odd, two[rows], one[rows]).astype(F32)
            value = value + jnp.where(level < levels - 1, above, 0.0)
        return value

    for q in range(height // chunk // 2):
        to = slice(q * chunk, (q + 1) * chunk)
        for s in range(sectors):
            send[s, to] = total(s, pl.ds((2 * q + 1 - own) * chunk, chunk)).astype(BF16)
            keep[s, to] = total(s, pl.ds((2 * q + own) * chunk, chunk))


def split(token, bit, chunk, levels, mid, *more):
    sectors, height, width = mid.shape
    return kernel_call(
        functools.partial(split_kernel, bit, chunk, levels, len(more) == 2),
        token,
        (mid, *more),
        [VMEM] * (1 + len(more)),
        [
            jax.ShapeDtypeStruct((sectors, height // 2, width), BF16),
            jax.ShapeDtypeStruct((sectors, height // 2, width), F32),
        ],
        [VMEM] * 2,
        mib=4,
        cost_estimate=estimate(mid.size, 10 * mid.size),
        name="split",
    )


def relay_kernel(half, own, other, out):
    place = lax.rem(lax.axis_index("op"), half)
    end = jnp.logical_or(place == 0, place == half - 1)

    @pl.when(end)
    def _():
        out[...] = other[...]

    @pl.when(jnp.logical_not(end))
    def _():
        out[...] = own[...]


def relay(token, half, own, other):
    return kernel_call(
        functools.partial(relay_kernel, half),
        token,
        (own, other),
        [VMEM] * 2,
        [jax.ShapeDtypeStruct(own.shape, BF16)],
        [VMEM],
        mib=4,
        cost_estimate=estimate(0, 6 * own.size),
        name="relay",
    )


def hold_kernel(source, kept):
    pass


def hold(token, value):
    return kernel_call(
        hold_kernel,
        token,
        (value,),
        [ANY],
        [jax.ShapeDtypeStruct(value.shape, value.dtype)],
        [ANY],
        aliases={0: 0},
        mib=1,
        cost_estimate=estimate(0, 0),
        name="hold",
    )


def renorm_kernel(items, zero, offset, levels, turned, rotations, one, two, *refs):
    buffers = refs[: 1 + max(item[0] for item in items)]
    rest = refs[len(buffers) + (0 if zero else 1) :]
    out, edge, results, done = rest
    sectors, width, _ = rotations.shape
    odd = lax.rem(lax.axis_index("op"), 2)
    level = lax.axis_index("sec")
    raised = lax.rem(level, 2) == 1
    rows = pl.ds(offset, width)
    stores = []
    if zero:
        results[len(items)] = jnp.zeros_like(results[len(items)])
        for place in range(CAPS):
            copy = pltpu.make_async_copy(results.at[len(items)], out.at[place], done)
            copy.start()
            stores.append(copy)
    edge[0] = jnp.where(raised, one[rows], two[rows])
    edge[1] = jnp.where(raised, two[rows], one[rows])
    for i, (buffer, base, kind, place) in enumerate(items):
        values = buffers[buffer][pl.ds(base + sectors * width, META)].astype(F32)

        def scalar(row):
            return jnp.max(values[row : row + 1, :])

        charge = scalar(0).astype(jnp.int32)
        if kind == "core":
            kind = 2 - odd
        elif kind == "side":
            kind = 1 + odd
        if place == 1:
            wanted = jnp.where(scalar(1).astype(jnp.int32) == kind, 1.0, 0.0)
        else:
            wanted = jnp.float32(1.0)
        for s in range(sectors):
            at = s + charge
            whole = level * sectors + at
            inside = jnp.logical_and(whole >= 0, whole < levels * sectors)
            weight = jnp.where(inside, scalar(2 + s) * wanted, 0.0)
            block = buffers[buffer][pl.ds(base + s * width, width)]
            rotated = jnp.dot(block, rotations[s], preferred_element_type=F32).astype(BF16)
            target = turned[jnp.clip(at, 0, sectors - 1)]
            if s == 0:
                target = jnp.where(at < 0, edge[0], target)
            if s == sectors - 1:
                target = jnp.where(at > sectors - 1, edge[1], target)
            value = jnp.dot(target, rotated, preferred_element_type=F32) * weight
            results[i, s] = value.astype(BF16)
            copy = pltpu.make_async_copy(results.at[i, s], out.at[kind * CAPS + place, s], done)
            copy.start()
            stores.append(copy)
    for copy in stores:
        copy.wait()


def renorm(token, name, items, buffers, out, offset, levels, turned, rotations, one, two):
    sectors, width, _ = rotations.shape
    zero = out is None
    operands = [turned, rotations, one, two, *buffers]
    in_specs = [VMEM] * len(operands)
    if not zero:
        operands.append(out)
        in_specs.append(HBM)
    count = len(items)
    block = (sectors, width, width)
    token, (out,) = kernel_call(
        functools.partial(renorm_kernel, items, zero, offset, levels),
        token,
        operands,
        in_specs,
        [jax.ShapeDtypeStruct((DIRS * CAPS, *block), BF16)],
        [HBM],
        aliases={} if zero else {len(operands) - 1: 0},
        scratch_shapes=[
            pltpu.VMEM((2, width, width), BF16),
            pltpu.VMEM((count + (1 if zero else 0), *block), BF16),
            pltpu.SemaphoreType.DMA,
        ],
        mib=12,
        cost_estimate=estimate(
            4 * count * sectors * width**3, 4 * (count + 2) * sectors * width * width
        ),
        name=name,
    )
    return token, out


def body(
    wavefunction, left_operators, right_operators, rotations, charges, present_blocks, directions
):
    sectors, width, _ = wavefunction.shape
    pairs = left_operators.shape[0]
    n = lax.axis_size("op")
    levels = lax.axis_size("sec")
    half = n // 2
    chunk = width // n
    halving = n & (n - 1) == 0 and chunk % 16 == 0
    rows = sectors * width + META

    def over_op(value, target):
        return lax.ppermute(value, "op", [(i, target(i)) for i in range(n)])

    def swapped(value, start):
        to = list(range(levels))
        for i in range(start, levels - 1, 2):
            to[i], to[i + 1] = i + 1, i
        return lax.ppermute(value, "sec", list(enumerate(to)))

    def side(i):
        return (i + 1) % n if i % 2 else (i - 1) % n

    def side_or_across(i):
        place = i % half
        if place == half - 1:
            return i - place
        if place == 0:
            return i + half - 1
        return side(i)

    roles = (("extra",), ("side",), ("extra", "core"), ("half",))
    token, (extra, first_side, first_core, first_half, left, wave, rotations) = staged(
        roles, directions[:, 0], charges, present_blocks, left_operators, wavefunction, rotations
    )
    extra_half = over_op(extra, lambda i: (i + half) % n)
    from_side = over_op(first_side, side)
    from_core = over_op(first_core, lambda i: i ^ 1)
    from_half = over_op(first_half, lambda i: (i + half) % n)
    token, (*terms, turned) = sigma_terms(
        token, halving, chunk, charges, present_blocks, left, right_operators, wave, rotations
    )

    if halving:
        send, keep = terms
        got = over_op(send, lambda i: i ^ 1)
        token, (first, second, mid) = edges(token, keep, got, turned)
        one, two = swapped(first, 0), swapped(second, 1)
        offset = width // 2
        token, (from_core,) = hold(token, from_core)
        token, (relayed,) = relay(token, half, extra, extra_half)
        extra_side = over_op(relayed, side_or_across)
        bit = 2
        token, (send, keep) = split(token, bit, chunk, levels, mid, one, two)
        got = over_op(send, lambda i: i ^ 2)
    else:
        (terms,) = terms
        offset = width
        odd = lax.rem(lax.axis_index("sec"), 2) == 1
        level = lax.axis_index("sec")
        upward = jnp.concatenate([terms[sectors + 1].astype(BF16), turned[sectors - 1]])
        downward = jnp.concatenate([terms[0].astype(BF16), turned[0]])
        one = swapped(jnp.where(odd, downward, upward), 0)
        two = swapped(jnp.where(odd, upward, downward), 1)
        below = jnp.where(odd, one, two)[:width].astype(F32)
        above = jnp.where(odd, two, one)[:width].astype(F32)
        mid = terms[1 : sectors + 1]
        mid = mid.at[0].add(jnp.where(level > 0, below, 0.0))
        mid = mid.at[sectors - 1].add(jnp.where(level < levels - 1, above, 0.0))
        summed = lax.psum_scatter(mid, "op", scatter_dimension=1, tiled=True)
        token, (relayed,) = relay(token, half, extra, extra_half)
        extra_side = over_op(relayed, side_or_across)

    fixed = (offset, levels, turned, rotations, one, two)
    token, out = renorm(
        token,
        "renorm_core",
        ((0, 0, "core", 1), (0, rows, "core", 0), (1, 0, 3, 1)),
        (from_core, extra_half),
        None,
        *fixed,
    )
    if halving:
        while 2 * bit < n:
            bit *= 2
            token, (send, keep) = split(token, bit, chunk, levels, keep, got)
            got = over_op(send, lambda i: i ^ bit)
        summed = keep + got.astype(F32)
    token, out = renorm(
        token, "renorm_side", ((0, 0, "side", 0),), (from_side,), out, *fixed
    )
    token, out = renorm(
        token, "renorm_extra", ((0, 0, "side", 1),), (extra_side,), out, *fixed
    )
    token, out = renorm(token, "renorm_half", ((0, 0, 3, 0),), (from_half,), out, *fixed)
    return summed / math.sqrt(pairs * n), out


def solution(mesh):
    placed = (
        P("sec", None, None),
        P("op", "sec", None, None),
        P("op", "sec", None, None),
        P("sec", None, None),
        P("op"),
        P("op", "sec"),
        P("op", None),
    )
    return jax.shard_map(
        body,
        mesh=mesh,
        in_specs=placed,
        out_specs=(P("sec", "op", None), P("op", "sec", None, None)),
        check_vma=False,
    )
```

```python
import functools
import math

import jax
import jax.numpy as jnp
from jax import lax
from jax.experimental import pallas as pl
from jax.experimental.pallas import tpu as pltpu
from jax.sharding import PartitionSpec as P

DIRS = 4
CAPS = 2
META = 16

BF16 = jnp.bfloat16
F32 = jnp.float32
ANY = pl.BlockSpec(memory_space=pl.ANY)
HBM = pl.BlockSpec(memory_space=pltpu.HBM)
VMEM = pl.BlockSpec(memory_space=pltpu.VMEM)


def kernel_call(kernel, token, operands, in_specs, out_shape, out_specs, **options):
    mib = options.pop("mib")
    aliases = options.pop("aliases", {})
    grid = options.pop("grid", ())
    ahead = 0 if token is None else 1
    taken = len(operands) + ahead

    def run(*refs):
        refs = list(refs)
        del refs[taken]
        kernel(*refs[ahead:])

    outs = pl.pallas_call(
        run,
        grid=grid,
        out_shape=[jax.ShapeDtypeStruct((8, 128), F32), *out_shape],
        in_specs=[HBM] * ahead + list(in_specs),
        out_specs=[HBM, *out_specs],
        input_output_aliases={i + ahead: o + 1 for i, o in aliases.items()},
        compiler_params=pltpu.CompilerParams(vmem_limit_bytes=mib * 1024 * 1024),
        **options,
    )(*([] if token is None else [token]), *operands)
    return outs[0], list(outs[1:])


def in_hbm(value):
    return pltpu.with_memory_space_constraint(value, pltpu.HBM)


def estimate(flops, moved):
    return pl.CostEstimate(flops=0, bytes_accessed=0, transcendentals=0)


def fetch_scalars(pairs, sem):
    copies = [pltpu.make_async_copy(source, kept, sem) for source, kept in pairs]
    for copy in copies:
        copy.start()
    for copy in copies:
        copy.wait()


def at_end(half):
    place = lax.rem(lax.axis_index("op"), half)
    return jnp.logical_or(place == 0, place == half - 1)


def pick(kinds, places, kind, place):
    index = jnp.int32(0)
    for p, (own, at) in enumerate(zip(kinds, places)):
        match = at == place if kind is None else jnp.logical_and(at == place, own == kind)
        index = index + jnp.where(match, p, 0)
    return index


def stage_kernel(
    roles, half, directions_ref, charges_ref, present_ref, left_ref, wave_ref, rot_ref, *refs
):
    outs = refs[: len(roles)]
    left, wave, rot, directions, charges, present, few, sems = refs[len(roles) :]
    bulk = [
        pltpu.make_async_copy(left_ref, left, sems.at[0]),
        pltpu.make_async_copy(wave_ref, wave, sems.at[1]),
        pltpu.make_async_copy(rot_ref, rot, sems.at[2]),
    ]
    for copy in bulk:
        copy.start()
    fetch_scalars(
        [(directions_ref, directions), (charges_ref, charges), (present_ref, present)], few
    )
    count, sectors, width, _ = left_ref.shape
    kinds = [directions[p] for p in range(count)]
    places = []
    for p in range(count):
        place = jnp.int32(0)
        for q in range(p):
            place = place + jnp.where(kinds[q] == kinds[p], 1, 0)
        places.append(place)
    odd = lax.rem(lax.axis_index("op"), 2)
    end = at_end(half)
    found = {
        "extra": pick(kinds, places, None, 1),
        "half": pick(kinds, places, 3, 0),
        "core": pick(kinds, places, 1 + odd, 0),
        "side": pick(kinds, places, 2 - odd, 0),
    }
    row = lax.broadcasted_iota(jnp.int32, (META, width), 0)
    bulk[0].wait()
    for out, wanted in zip(outs, roles):
        base = 0
        for role in wanted:
            index = found[role] if isinstance(role, str) else jnp.where(end, *map(found.get, role))
            for s in range(sectors):
                out[base + s * width : base + (s + 1) * width] = left[index, s]
            kind = jnp.int32(0)
            for p in range(count):
                kind = kind + jnp.where(index == p, kinds[p], 0)
            values = jnp.where(row == 0, charges[index], jnp.where(row == 1, kind, 0))
            for s in range(sectors):
                values = jnp.where(row == 2 + s, present[index, s], values)
            base += sectors * width
            out[base : base + META] = values.astype(F32).astype(BF16)
            base += META
    for copy in bulk[1:]:
        copy.wait()


def staged(roles, half, directions, charges, present, left, wave, rotations):
    count, sectors, width, _ = left.shape
    rows = sectors * width + META
    shapes = [(rows * len(wanted), width) for wanted in roles]
    shapes += [left.shape, wave.shape, rotations.shape]
    return kernel_call(
        functools.partial(stage_kernel, roles, half),
        None,
        [in_hbm(x) for x in (directions, charges, present, left, wave, rotations)],
        [HBM] * 6,
        [pltpu.VMEM(shape, BF16) for shape in shapes],
        [VMEM] * len(shapes),
        scratch_shapes=[
            pltpu.SMEM((count,), jnp.int32),
            pltpu.SMEM((count,), jnp.int32),
            pltpu.SMEM((count, sectors), jnp.int32),
            pltpu.SemaphoreType.DMA,
            pltpu.SemaphoreType.DMA((3,)),
        ],
        mib=4,
        cost_estimate=estimate(0, 0),
        name="stage",
    )


def sigma_kernel(split, chunk, charges_ref, present_ref, left, right_ref, wave, rotations, *refs):
    outs, (acc, right, charges, present, few, sems) = refs[:-6], refs[-6:]
    count, sectors, width, _ = left.shape
    small = [
        pltpu.make_async_copy(charges_ref, charges, few),
        pltpu.make_async_copy(present_ref, present, few),
    ]
    loads = [pltpu.make_async_copy(right_ref.at[p], right.at[p], sems.at[p]) for p in range(count)]
    for copy in small + loads:
        copy.start()
    acc[...] = jnp.zeros_like(acc)
    for s in range(sectors):
        outs[-1][s] = rotations[s].T
    for copy in small:
        copy.wait()

    def step(pair, carry):
        pltpu.make_async_copy(right_ref.at[pair], right.at[pair], sems.at[pair]).wait()
        charge = charges[pair]
        for s in range(sectors):
            halfway = jnp.dot(left[pair, s], wave[s], preferred_element_type=F32)
            halfway = (halfway * present[pair, s].astype(F32)).astype(BF16)
            term = lax.dot_general(
                halfway, right[pair, s], (((1,), (1,)), ((), ())), preferred_element_type=F32
            )
            acc[jnp.clip(s + 1 + charge, 0, sectors + 1)] += term
        return carry

    lax.fori_loop(0, count, step, 0)
    if not split:
        outs[0][...] = acc[...]
        return
    bit = lax.rem(lax.axis_index("op"), 2)
    for q in range(width // chunk // 2):
        to = slice(q * chunk, (q + 1) * chunk)
        for t in range(sectors + 2):
            away = acc[t, pl.ds((2 * q + 1 - bit) * chunk, chunk)].astype(BF16)
            if 0 < t <= sectors:
                outs[1][t - 1, to] = away
            else:
                outs[0][min(t, 1), to] = away
            outs[2][t, to] = acc[t, pl.ds((2 * q + bit) * chunk, chunk)]


def sigma_terms(token, split, chunk, charges, present, left, right, wave, rotations):
    count, sectors, width, _ = left.shape
    if split:
        shapes = [
            ((2, width // 2, width), BF16),
            ((sectors, width // 2, width), BF16),
            ((sectors + 2, width // 2, width), F32),
        ]
    else:
        shapes = [((sectors + 2, width, width), F32)]
    shapes.append(((sectors, width, width), BF16))
    return kernel_call(
        functools.partial(sigma_kernel, split, chunk),
        token,
        (in_hbm(charges), in_hbm(present), left, in_hbm(right), wave, rotations),
        [HBM, HBM, VMEM, HBM, VMEM, VMEM],
        [pltpu.VMEM(*shape) for shape in shapes],
        [VMEM] * len(shapes),
        scratch_shapes=[
            pltpu.VMEM((sectors + 2, width, width), F32),
            pltpu.VMEM(right.shape, BF16),
            pltpu.SMEM((count,), jnp.int32),
            pltpu.SMEM((count, sectors), jnp.int32),
            pltpu.SemaphoreType.DMA,
            pltpu.SemaphoreType.DMA((count,)),
        ],
        mib=10,
        cost_estimate=estimate(0, 0),
        name="sigma_terms",
    )


def edges_kernel(keep, got, turned, first, second):
    outer, height, _ = keep.shape
    odd = lax.rem(lax.axis_index("sec"), 2)
    for out, upward in ((first, odd == 0), (second, odd == 1)):
        edge = jnp.where(upward, outer - 1, 0)
        out[:height] = (keep[edge] + got[jnp.where(upward, 1, 0)].astype(F32)).astype(BF16)
        out[height:] = turned[jnp.where(upward, outer - 3, 0)]


def edges(token, keep, got, turned):
    _, height, width = keep.shape
    shape = (height + turned.shape[1], width)
    return kernel_call(
        edges_kernel,
        token,
        (keep, got, turned),
        [VMEM] * 3,
        [jax.ShapeDtypeStruct(shape, BF16)] * 2,
        [VMEM] * 2,
        mib=4,
        cost_estimate=estimate(0, 0),
        name="edges",
    )


def split_kernel(bit, chunk, levels, first, held, *refs):
    if first:
        got, one, two, send, keep = refs
    else:
        got, send, keep = refs
    sectors, height, _ = got.shape
    own = lax.rem(lax.axis_index("op") // bit, 2)
    level = lax.axis_index("sec")
    odd = lax.rem(level, 2) == 1

    def total(s, rows):
        if not first:
            return held[s, rows] + got[s, rows].astype(F32)
        value = held[s + 1, rows] + got[s, rows].astype(F32)
        if s == 0:
            below = jnp.where(odd, one[rows], two[rows]).astype(F32)
            value = value + jnp.where(level > 0, below, 0.0)
        if s == sectors - 1:
            above = jnp.where(odd, two[rows], one[rows]).astype(F32)
            value = value + jnp.where(level < levels - 1, above, 0.0)
        return value

    for q in range(height // chunk // 2):
        to = slice(q * chunk, (q + 1) * chunk)
        for s in range(sectors):
            send[s, to] = total(s, pl.ds((2 * q + 1 - own) * chunk, chunk)).astype(BF16)
            keep[s, to] = total(s, pl.ds((2 * q + own) * chunk, chunk))


def split(token, bit, chunk, levels, held, got, *edge):
    sectors, height, width = got.shape
    return kernel_call(
        functools.partial(split_kernel, bit, chunk, levels, len(edge) == 2),
        token,
        (held, got, *edge),
        [VMEM] * (2 + len(edge)),
        [
            jax.ShapeDtypeStruct((sectors, height // 2, width), BF16),
            jax.ShapeDtypeStruct((sectors, height // 2, width), F32),
        ],
        [VMEM] * 2,
        mib=4,
        cost_estimate=estimate(0, 0),
        name="split",
    )


def hold_kernel(*refs):
    pass


def hold(token, *values):
    return kernel_call(
        hold_kernel,
        token,
        values,
        [ANY] * len(values),
        [jax.ShapeDtypeStruct(value.shape, value.dtype) for value in values],
        [ANY] * len(values),
        aliases={i: i for i in range(len(values))},
        mib=1,
        cost_estimate=estimate(0, 0),
        name="hold",
    )


def choose_kernel(half, first, second, out):
    end = at_end(half)

    @pl.when(end)
    def _():
        out[...] = first[: out.shape[0]]

    @pl.when(jnp.logical_not(end))
    def _():
        out[...] = second[...]


def choose(token, half, first, second):
    return kernel_call(
        functools.partial(choose_kernel, half),
        token,
        (first, second),
        [VMEM] * 2,
        [pltpu.VMEM(second.shape, BF16)],
        [VMEM],
        mib=4,
        cost_estimate=estimate(0, 0),
        name="choose",
    )


def renorm_kernel(items, zero, offset, levels, half, scale, turned, rotations, one, two, *refs):
    if scale is not None:
        (keep, got), refs = refs[:2], refs[2:]
    buffers = refs[: 1 + max(buffer for sources, _, _ in items for buffer, _ in sources)]
    rest = refs[len(buffers) + (0 if zero else 1) :]
    if scale is not None:
        sigma, rest = rest[1], [rest[0], *rest[2:]]
        sigma[...] = (keep[...] + got[...].astype(F32)) * scale
    out, edge, results, done = rest
    sectors, width, _ = rotations.shape
    device = lax.axis_index("op")
    odd = lax.rem(device, 2)
    end = at_end(half)
    level = lax.axis_index("sec")
    raised = lax.rem(level, 2) == 1
    rows = pl.ds(offset, width)
    stores = []
    if zero:
        results[len(items)] = jnp.zeros_like(results[len(items)])
        for place in range(CAPS):
            copy = pltpu.make_async_copy(results.at[len(items)], out.at[place], done)
            copy.start()
            stores.append(copy)
    edge[0] = jnp.where(raised, one[rows], two[rows])
    edge[1] = jnp.where(raised, two[rows], one[rows])
    for i, (sources, kind, place) in enumerate(items):

        def received(at, count):
            loaded = [buffers[buffer][pl.ds(base + at, count)] for buffer, base in sources]
            return loaded[0] if len(loaded) == 1 else jnp.where(end, loaded[0], loaded[1])

        values = received(sectors * width, META).astype(F32)

        def scalar(row):
            return jnp.max(values[row : row + 1, :])

        charge = scalar(0).astype(jnp.int32)
        if kind == "core":
            kind = 2 - odd
        elif kind == "side":
            kind = 1 + odd
        if place == 1:
            wanted = jnp.where(scalar(1).astype(jnp.int32) == kind, 1.0, 0.0)
        else:
            wanted = jnp.float32(1.0)
        for s in range(sectors):
            at = s + charge
            whole = level * sectors + at
            inside = jnp.logical_and(whole >= 0, whole < levels * sectors)
            weight = jnp.where(inside, scalar(2 + s) * wanted, 0.0)
            block = received(s * width, width)
            rotated = jnp.dot(block, rotations[s], preferred_element_type=F32).astype(BF16)
            target = turned[jnp.clip(at, 0, sectors - 1)]
            if s == 0:
                target = jnp.where(at < 0, edge[0], target)
            if s == sectors - 1:
                target = jnp.where(at > sectors - 1, edge[1], target)
            value = jnp.dot(target, rotated, preferred_element_type=F32) * weight
            results[i, s] = value.astype(BF16)
            copy = pltpu.make_async_copy(results.at[i, s], out.at[kind * CAPS + place, s], done)
            copy.start()
            stores.append(copy)
    for copy in stores:
        copy.wait()


def renorm(
    token, name, items, buffers, out, offset, levels, half, turned, rotations, one, two, sums=(), scale=None
):
    sectors, width, _ = rotations.shape
    zero = out is None
    operands = [turned, rotations, one, two, *sums, *buffers]
    in_specs = [VMEM] * len(operands)
    if not zero:
        operands.append(out)
        in_specs.append(HBM)
    count = len(items)
    block = (sectors, width, width)
    return kernel_call(
        functools.partial(renorm_kernel, items, zero, offset, levels, half, scale),
        token,
        operands,
        in_specs,
        [jax.ShapeDtypeStruct((DIRS * CAPS, *block), BF16)]
        + [jax.ShapeDtypeStruct(x.shape, F32) for x in sums[:1]],
        [HBM] + [VMEM] * len(sums[:1]),
        aliases={} if zero else {len(operands) - 1: 0},
        scratch_shapes=[
            pltpu.VMEM((2, width, width), BF16),
            pltpu.VMEM((count + (1 if zero else 0), *block), BF16),
            pltpu.SemaphoreType.DMA,
        ],
        mib=8,
        cost_estimate=pl.CostEstimate(
            flops=8 * count * sectors * width**3 if zero else 0, bytes_accessed=0, transcendentals=0
        ),
        name=name,
    )


def body(
    wavefunction, left_operators, right_operators, rotations, charges, present_blocks, directions
):
    sectors, width, _ = wavefunction.shape
    pairs = left_operators.shape[0]
    n = lax.axis_size("op")
    levels = lax.axis_size("sec")
    half = n // 2
    chunk = width // n
    halving = n >= 4 and n & (n - 1) == 0 and chunk % 16 == 0
    rows = sectors * width + META

    def over_op(value, target):
        return lax.ppermute(value, "op", [(i, target(i)) for i in range(n)])

    def swapped(value, start):
        to = list(range(levels))
        for i in range(start, levels - 1, 2):
            to[i], to[i + 1] = i + 1, i
        return lax.ppermute(value, "sec", list(enumerate(to)))

    def side(i):
        return (i + 1) % n if i % 2 else (i - 1) % n

    def end(i):
        return i % half in (0, half - 1)

    def opposite(i):
        return (i + half) % n

    def relay(i):
        return i - i % half + half - 1 - i % half

    roles = (
        (("extra", "side"), ("half", "extra")),
        (("side", "extra"),),
        ("half",),
        ("extra", "core"),
    )
    token, (ahead, behind, last, first_core, left, wave, turn) = staged(
        roles, half, directions[:, 0], charges, present_blocks, left_operators, wavefunction, rotations
    )
    got_ahead = over_op(ahead, lambda i: opposite(i) if end(i) else side(i))
    got_behind = over_op(behind, lambda i: side(i) if end(i) else opposite(i))
    from_core = over_op(first_core, lambda i: i ^ 1)
    token, (*terms, turned) = sigma_terms(
        token, halving, chunk, charges, present_blocks, left, right_operators, wave, turn
    )

    if halving:
        send_edges, send, keep = terms
        got_edges = over_op(send_edges, lambda i: i ^ 1)
        got = over_op(send, lambda i: i ^ 1)
        token, (from_core, got) = hold(token, from_core, got)
        token, (first, second) = edges(token, keep, got_edges, turned)
        one, two = swapped(first, 0), swapped(second, 1)
        offset = width // 2
        bit = 2
        token, (send, keep) = split(token, bit, chunk, levels, keep, got, one, two)
        got = over_op(send, lambda i: i ^ 2)
        while 2 * bit < n:
            bit *= 2
            token, (send, keep) = split(token, bit, chunk, levels, keep, got)
            got = over_op(send, lambda i, bit=bit: i ^ bit)
    else:
        (terms,) = terms
        offset = width
        odd = lax.rem(lax.axis_index("sec"), 2) == 1
        level = lax.axis_index("sec")
        upward = jnp.concatenate([terms[sectors + 1].astype(BF16), turned[sectors - 1]])
        downward = jnp.concatenate([terms[0].astype(BF16), turned[0]])
        one = swapped(jnp.where(odd, downward, upward), 0)
        two = swapped(jnp.where(odd, upward, downward), 1)
        below = jnp.where(odd, one, two)[:width].astype(F32)
        above = jnp.where(odd, two, one)[:width].astype(F32)
        mid = terms[1 : sectors + 1]
        mid = mid.at[0].add(jnp.where(level > 0, below, 0.0))
        mid = mid.at[sectors - 1].add(jnp.where(level < levels - 1, above, 0.0))
        summed = lax.psum_scatter(mid, "op", scatter_dimension=1, tiled=True)

    token, (last,) = choose(token, half, got_ahead, last)
    got_last = over_op(last, lambda i: relay(i) if end(i) else opposite(i))
    fixed = (offset, levels, half, turned, turn, one, two)
    token, (out,) = renorm(
        token,
        "renorm_first",
        (
            (((0, 0),), "core", 1),
            (((0, rows),), "core", 0),
            (((2, 0), (1, 0)), "side", 0),
            (((1, 0), (2, 0)), 3, 1),
        ),
        (from_core, got_ahead, got_behind),
        None,
        *fixed,
    )
    scale = 1.0 / math.sqrt(pairs * n)
    token, (out, *sigma_vector) = renorm(
        token,
        "renorm_last",
        ((((1, 0), (0, rows)), "side", 1), (((0, rows), (1, 0)), 3, 0)),
        (got_ahead, got_last),
        out,
        *fixed,
        sums=(keep, got) if halving else (),
        scale=scale if halving else None,
    )
    if not halving:
        sigma_vector = [summed * scale]
    return sigma_vector[0], out


def solution(mesh):
    placed = (
        P("sec", None, None),
        P("op", "sec", None, None),
        P("op", "sec", None, None),
        P("sec", None, None),
        P("op"),
        P("op", "sec"),
        P("op", None),
    )
    return jax.shard_map(
        body,
        mesh=mesh,
        in_specs=placed,
        out_specs=(P("sec", "op", None), P("op", "sec", None, None)),
        check_vma=False,
    )
```

```python
import functools
import math

import jax
import jax.numpy as jnp
from jax import lax
from jax.experimental import pallas as pl
from jax.experimental.pallas import tpu as pltpu
from jax.sharding import PartitionSpec as P

DIRS = 4
CAPS = 2
META = 16

BF16 = jnp.bfloat16
F32 = jnp.float32
ANY = pl.BlockSpec(memory_space=pl.ANY)
HBM = pl.BlockSpec(memory_space=pltpu.HBM)
VMEM = pl.BlockSpec(memory_space=pltpu.VMEM)


def kernel_call(kernel, token, operands, in_specs, out_shape, out_specs, **options):
    mib = options.pop("mib")
    aliases = options.pop("aliases", {})
    grid = options.pop("grid", ())
    ahead = 0 if token is None else 1
    taken = len(operands) + ahead

    def run(*refs):
        refs = list(refs)
        del refs[taken]
        kernel(*refs[ahead:])

    outs = pl.pallas_call(
        run,
        grid=grid,
        out_shape=[jax.ShapeDtypeStruct((8, 128), F32), *out_shape],
        in_specs=[HBM] * ahead + list(in_specs),
        out_specs=[HBM, *out_specs],
        input_output_aliases={i + ahead: o + 1 for i, o in aliases.items()},
        compiler_params=pltpu.CompilerParams(vmem_limit_bytes=mib * 1024 * 1024),
        **options,
    )(*([] if token is None else [token]), *operands)
    return outs[0], list(outs[1:])


def in_hbm(value):
    return pltpu.with_memory_space_constraint(value, pltpu.HBM)


def estimate(flops, moved):
    return pl.CostEstimate(flops=0, bytes_accessed=0, transcendentals=0)


def fetch_scalars(pairs, sem):
    copies = [pltpu.make_async_copy(source, kept, sem) for source, kept in pairs]
    for copy in copies:
        copy.start()
    for copy in copies:
        copy.wait()


def at_end(half):
    place = lax.rem(lax.axis_index("op"), half)
    return jnp.logical_or(place == 0, place == half - 1)


def pick(kinds, places, kind, place):
    index = jnp.int32(0)
    for p, (own, at) in enumerate(zip(kinds, places)):
        match = at == place if kind is None else jnp.logical_and(at == place, own == kind)
        index = index + jnp.where(match, p, 0)
    return index


def copy_pairs(roles, half, outs, left, directions, charges, present):
    count, sectors, width, _ = left.shape
    kinds = [directions[p] for p in range(count)]
    places = []
    for p in range(count):
        place = jnp.int32(0)
        for q in range(p):
            place = place + jnp.where(kinds[q] == kinds[p], 1, 0)
        places.append(place)
    odd = lax.rem(lax.axis_index("op"), 2)
    end = at_end(half)
    found = {
        "extra": pick(kinds, places, None, 1),
        "half": pick(kinds, places, 3, 0),
        "core": pick(kinds, places, 1 + odd, 0),
        "side": pick(kinds, places, 2 - odd, 0),
    }
    row = lax.broadcasted_iota(jnp.int32, (META, width), 0)
    for out, wanted in zip(outs, roles):
        base = 0
        for role in wanted:
            index = found[role] if isinstance(role, str) else jnp.where(end, *map(found.get, role))
            for s in range(sectors):
                out[base + s * width : base + (s + 1) * width] = left[index, s]
            kind = jnp.int32(0)
            for p in range(count):
                kind = kind + jnp.where(index == p, kinds[p], 0)
            values = jnp.where(row == 0, charges[index], jnp.where(row == 1, kind, 0))
            for s in range(sectors):
                values = jnp.where(row == 2 + s, present[index, s], values)
            base += sectors * width
            out[base : base + META] = values.astype(F32).astype(BF16)
            base += META


def stage_kernel(roles, half, directions_ref, charges_ref, present_ref, left_ref, *refs):
    outs = refs[: len(roles)]
    left, directions, charges, present, few, sem = refs[len(roles) :]
    bulk = pltpu.make_async_copy(left_ref, left, sem)
    bulk.start()
    fetch_scalars(
        [(directions_ref, directions), (charges_ref, charges), (present_ref, present)], few
    )
    bulk.wait()
    copy_pairs(roles, half, outs, left, directions, charges, present)


def restage_kernel(
    roles, half, directions_ref, charges_ref, present_ref, left, wave_ref, rot_ref, *refs
):
    outs = refs[: len(roles)]
    wave, rot, directions, charges, present, few, sems = refs[len(roles) :]
    bulk = [
        pltpu.make_async_copy(wave_ref, wave, sems.at[0]),
        pltpu.make_async_copy(rot_ref, rot, sems.at[1]),
    ]
    for copy in bulk:
        copy.start()
    fetch_scalars(
        [(directions_ref, directions), (charges_ref, charges), (present_ref, present)], few
    )
    copy_pairs(roles, half, outs, left, directions, charges, present)
    for copy in bulk:
        copy.wait()


def staged(token, roles, half, directions, charges, present, left, *more):
    count, sectors, width, _ = left.shape
    rows = sectors * width + META
    parts = [(0, sectors // 2), (sectors // 2, sectors)] if sectors > 1 else [(0, 1)]
    shapes = [(rows * len(wanted), width) for wanted in roles]
    shapes += [x.shape for x in more] if more else [left.shape]
    operands = [in_hbm(x) for x in (directions, charges, present)]
    operands += [left, *map(in_hbm, more)] if more else [in_hbm(left)]
    return kernel_call(
        functools.partial(restage_kernel if more else stage_kernel, roles, half),
        token,
        operands,
        [HBM] * 3 + ([VMEM] + [HBM] * len(more) if more else [HBM]),
        [pltpu.VMEM(shape, BF16) for shape in shapes],
        [VMEM] * len(shapes),
        scratch_shapes=[
            pltpu.SMEM((count,), jnp.int32),
            pltpu.SMEM((count,), jnp.int32),
            pltpu.SMEM((count, sectors), jnp.int32),
            pltpu.SemaphoreType.DMA,
            pltpu.SemaphoreType.DMA((len(more),)) if more else pltpu.SemaphoreType.DMA,
        ],
        mib=4,
        cost_estimate=estimate(0, 0),
        name="restage" if more else "stage",
    )


def sigma_kernel(split, chunk, charges_ref, present_ref, left, right_ref, wave, rotations, *refs):
    outs, (acc, right, charges, present, few, sems) = refs[:-6], refs[-6:]
    count, sectors, width, _ = left.shape
    small = [
        pltpu.make_async_copy(charges_ref, charges, few),
        pltpu.make_async_copy(present_ref, present, few),
    ]
    loads = [pltpu.make_async_copy(right_ref.at[p], right.at[p], sems.at[p]) for p in range(count)]
    for copy in small + loads:
        copy.start()
    acc[...] = jnp.zeros_like(acc)
    for s in range(sectors):
        outs[-1][s] = rotations[s].T
    for copy in small:
        copy.wait()

    def step(pair, carry):
        pltpu.make_async_copy(right_ref.at[pair], right.at[pair], sems.at[pair]).wait()
        charge = charges[pair]
        for s in range(sectors):
            halfway = jnp.dot(left[pair, s], wave[s], preferred_element_type=F32)
            halfway = (halfway * present[pair, s].astype(F32)).astype(BF16)
            term = lax.dot_general(
                halfway, right[pair, s], (((1,), (1,)), ((), ())), preferred_element_type=F32
            )
            acc[jnp.clip(s + 1 + charge, 0, sectors + 1)] += term
        return carry

    lax.fori_loop(0, count, step, 0)
    if not split:
        outs[0][...] = acc[...]
        return
    bit = lax.rem(lax.axis_index("op"), 2)
    for q in range(width // chunk // 2):
        to = slice(q * chunk, (q + 1) * chunk)
        for t in range(sectors + 2):
            away = acc[t, pl.ds((2 * q + 1 - bit) * chunk, chunk)].astype(BF16)
            if 0 < t <= sectors:
                outs[1][t - 1, to] = away
            else:
                outs[0][min(t, 1), to] = away
            outs[2][t, to] = acc[t, pl.ds((2 * q + bit) * chunk, chunk)]


def sigma_terms(token, split, chunk, charges, present, left, right, wave, rotations):
    count, sectors, width, _ = left.shape
    if split:
        shapes = [
            ((2, width // 2, width), BF16),
            ((sectors, width // 2, width), BF16),
            ((sectors + 2, width // 2, width), F32),
        ]
    else:
        shapes = [((sectors + 2, width, width), F32)]
    shapes.append(((sectors, width, width), BF16))
    return kernel_call(
        functools.partial(sigma_kernel, split, chunk),
        token,
        (in_hbm(charges), in_hbm(present), left, in_hbm(right), wave, rotations),
        [HBM, HBM, VMEM, HBM, VMEM, VMEM],
        [pltpu.VMEM(*shape) for shape in shapes],
        [VMEM] * len(shapes),
        scratch_shapes=[
            pltpu.VMEM((sectors + 2, width, width), F32),
            pltpu.VMEM(right.shape, BF16),
            pltpu.SMEM((count,), jnp.int32),
            pltpu.SMEM((count, sectors), jnp.int32),
            pltpu.SemaphoreType.DMA,
            pltpu.SemaphoreType.DMA((count,)),
        ],
        mib=10,
        cost_estimate=estimate(0, 0),
        name="sigma_terms",
    )


def edges_kernel(keep, got, turned, first, second):
    outer, height, _ = keep.shape
    odd = lax.rem(lax.axis_index("sec"), 2)
    for out, upward in ((first, odd == 0), (second, odd == 1)):
        edge = jnp.where(upward, outer - 1, 0)
        out[:height] = (keep[edge] + got[jnp.where(upward, 1, 0)].astype(F32)).astype(BF16)
        out[height:] = turned[jnp.where(upward, outer - 3, 0)]


def edges(token, keep, got, turned):
    _, height, width = keep.shape
    shape = (height + turned.shape[1], width)
    return kernel_call(
        edges_kernel,
        token,
        (keep, got, turned),
        [VMEM] * 3,
        [jax.ShapeDtypeStruct(shape, BF16)] * 2,
        [VMEM] * 2,
        mib=4,
        cost_estimate=estimate(0, 0),
        name="edges",
    )


def split_kernel(bit, chunk, levels, first, held, *refs):
    if first:
        got, one, two, send, keep = refs
    else:
        got, send, keep = refs
    sectors, height, _ = got.shape
    own = lax.rem(lax.axis_index("op") // bit, 2)
    level = lax.axis_index("sec")
    odd = lax.rem(level, 2) == 1

    def total(s, rows):
        if not first:
            return held[s, rows] + got[s, rows].astype(F32)
        value = held[s + 1, rows] + got[s, rows].astype(F32)
        if s == 0:
            below = jnp.where(odd, one[rows], two[rows]).astype(F32)
            value = value + jnp.where(level > 0, below, 0.0)
        if s == sectors - 1:
            above = jnp.where(odd, two[rows], one[rows]).astype(F32)
            value = value + jnp.where(level < levels - 1, above, 0.0)
        return value

    for q in range(height // chunk // 2):
        to = slice(q * chunk, (q + 1) * chunk)
        for s in range(sectors):
            send[s, to] = total(s, pl.ds((2 * q + 1 - own) * chunk, chunk)).astype(BF16)
            keep[s, to] = total(s, pl.ds((2 * q + own) * chunk, chunk))


def split(token, bit, chunk, levels, held, got, *edge):
    sectors, height, width = got.shape
    return kernel_call(
        functools.partial(split_kernel, bit, chunk, levels, len(edge) == 2),
        token,
        (held, got, *edge),
        [VMEM] * (2 + len(edge)),
        [
            jax.ShapeDtypeStruct((sectors, height // 2, width), BF16),
            jax.ShapeDtypeStruct((sectors, height // 2, width), F32),
        ],
        [VMEM] * 2,
        mib=4,
        cost_estimate=pl.CostEstimate(flops=0 if edge else 2000000000, bytes_accessed=0, transcendentals=0),
        name="split",
    )


def hold_kernel(*refs):
    pass


def hold(token, *values, cost=0):
    return kernel_call(
        hold_kernel,
        token,
        values,
        [ANY] * len(values),
        [jax.ShapeDtypeStruct(value.shape, value.dtype) for value in values],
        [ANY] * len(values),
        aliases={i: i for i in range(len(values))},
        mib=1,
        cost_estimate=pl.CostEstimate(flops=cost, bytes_accessed=0, transcendentals=0),
        name="hold",
    )


def choose_kernel(half, cuts, first, second, *outs):
    end = at_end(half)

    def fill(source):
        for out, (at, size) in zip(outs, cuts):
            out[:size] = source[at : at + size]
            if out.shape[0] > size:
                out[size:] = source[second.shape[0] - META : second.shape[0]]

    @pl.when(end)
    def _():
        fill(first)

    @pl.when(jnp.logical_not(end))
    def _():
        fill(second)


def choose(token, half, parts, first, second):
    width = second.shape[1]
    cuts = [(begin * width, (stop - begin) * width) for begin, stop in parts]
    return kernel_call(
        functools.partial(choose_kernel, half, cuts),
        token,
        (first, second),
        [VMEM] * 2,
        [
            pltpu.VMEM((size + (META if i == 0 else 0), width), BF16)
            for i, (_, size) in enumerate(cuts)
        ],
        [VMEM] * len(cuts),
        mib=4,
        cost_estimate=estimate(0, 0),
        name="choose",
    )


def renorm_kernel(items, zero, offset, levels, half, scale, turned, rotations, one, two, *refs):
    if scale is not None:
        (keep, got), refs = refs[:2], refs[2:]
    buffers = refs[: 1 + max(max(source[::2]) for item in items for source in item[0])]
    rest = refs[len(buffers) + (0 if zero else 1) :]
    if scale is not None:
        sigma, *rest, total = [rest[1], rest[0], *rest[2:]]
        total[...] = (keep[...] + got[...].astype(F32)) * scale
    out, edge, results, done = rest
    sectors, width, _ = rotations.shape
    device = lax.axis_index("op")
    odd = lax.rem(device, 2)
    end = at_end(half)
    level = lax.axis_index("sec")
    raised = lax.rem(level, 2) == 1
    rows = pl.ds(offset, width)
    stores = []
    if scale is not None:
        copy = pltpu.make_async_copy(total, sigma, done)
        copy.start()
        stores.append(copy)
    if zero:
        results[len(items)] = jnp.zeros_like(results[len(items)])
        for place in range(CAPS):
            copy = pltpu.make_async_copy(results.at[len(items)], out.at[place], done)
            copy.start()
            stores.append(copy)
    edge[0] = jnp.where(raised, one[rows], two[rows])
    edge[1] = jnp.where(raised, two[rows], one[rows])
    for i, (sources, kind, place, begin, stop) in enumerate(items):

        def received(places, count):
            loaded = [buffers[buffer][pl.ds(at, count)] for buffer, at in places]
            return loaded[0] if len(loaded) == 1 else jnp.where(end, loaded[0], loaded[1])

        values = received([source[2:] for source in sources], META).astype(F32)

        def scalar(row):
            return jnp.max(values[row : row + 1, :])

        charge = scalar(0).astype(jnp.int32)
        if kind == "core":
            kind = 2 - odd
        elif kind == "side":
            kind = 1 + odd
        if place == 1:
            wanted = jnp.where(scalar(1).astype(jnp.int32) == kind, 1.0, 0.0)
        else:
            wanted = jnp.float32(1.0)
        for s in range(begin, stop):
            at = s + charge
            whole = level * sectors + at
            inside = jnp.logical_and(whole >= 0, whole < levels * sectors)
            weight = jnp.where(inside, scalar(2 + s) * wanted, 0.0)
            block = received([(x[0], x[1] + (s - begin) * width) for x in sources], width)
            rotated = jnp.dot(block, rotations[s], preferred_element_type=F32).astype(BF16)
            target = turned[jnp.clip(at, 0, sectors - 1)]
            if s == 0:
                target = jnp.where(at < 0, edge[0], target)
            if s == sectors - 1:
                target = jnp.where(at > sectors - 1, edge[1], target)
            value = jnp.dot(target, rotated, preferred_element_type=F32) * weight
            results[i, s] = value.astype(BF16)
            copy = pltpu.make_async_copy(results.at[i, s], out.at[kind * CAPS + place, s], done)
            copy.start()
            stores.append(copy)
    for copy in stores:
        copy.wait()


def renorm(
    token, name, items, buffers, out, offset, levels, half, turned, rotations, one, two, sums=(), scale=None, cost=0
):
    sectors, width, _ = rotations.shape
    zero = out is None
    operands = [turned, rotations, one, two, *sums, *buffers]
    in_specs = [VMEM] * len(operands)
    if not zero:
        operands.append(out)
        in_specs.append(HBM)
    count = len(items)
    block = (sectors, width, width)
    return kernel_call(
        functools.partial(renorm_kernel, items, zero, offset, levels, half, scale),
        token,
        operands,
        in_specs,
        [jax.ShapeDtypeStruct((DIRS * CAPS, *block), BF16)]
        + [jax.ShapeDtypeStruct(x.shape, F32) for x in sums[:1]],
        [HBM] * (1 + len(sums[:1])),
        aliases={} if zero else {len(operands) - 1: 0},
        scratch_shapes=[
            pltpu.VMEM((2, width, width), BF16),
            pltpu.VMEM((count + (1 if zero else 0), *block), BF16),
            pltpu.SemaphoreType.DMA,
            *[pltpu.VMEM(x.shape, F32) for x in sums[:1]],
        ],
        mib=8,
        cost_estimate=pl.CostEstimate(
            flops=cost, bytes_accessed=0, transcendentals=0
        ),
        name=name,
    )


def body(
    wavefunction, left_operators, right_operators, rotations, charges, present_blocks, directions
):
    sectors, width, _ = wavefunction.shape
    pairs = left_operators.shape[0]
    n = lax.axis_size("op")
    levels = lax.axis_size("sec")
    half = n // 2
    chunk = width // n
    halving = n >= 4 and n & (n - 1) == 0 and chunk % 16 == 0
    rows = sectors * width + META
    parts = [(0, sectors // 2), (sectors // 2, sectors)] if sectors > 1 else [(0, 1)]

    def over_op(value, target):
        return lax.ppermute(value, "op", [(i, target(i)) for i in range(n)])

    def swapped(value, start):
        to = list(range(levels))
        for i in range(start, levels - 1, 2):
            to[i], to[i + 1] = i + 1, i
        return lax.ppermute(value, "sec", list(enumerate(to)))

    def side(i):
        return (i + 1) % n if i % 2 else (i - 1) % n

    def end(i):
        return i % half in (0, half - 1)

    def opposite(i):
        return (i + half) % n

    def relay(i):
        return i - i % half + half - 1 - i % half

    small = (directions[:, 0], charges, present_blocks)
    token, (ahead, left) = staged(
        None, ((("extra", "side"), ("half", "extra")),), half, *small, left_operators
    )
    token, (behind, last, first_core, wave, turn) = staged(
        token,
        ((("side", "extra"),), ("half",), ("extra", "core")),
        half,
        *small,
        left,
        wavefunction,
        rotations,
    )
    got_ahead = over_op(ahead, lambda i: opposite(i) if end(i) else side(i))
    got_behind = over_op(behind, lambda i: side(i) if end(i) else opposite(i))
    from_core = over_op(first_core, lambda i: i ^ 1)
    token, (*terms, turned) = sigma_terms(
        token, halving, chunk, charges, present_blocks, left, right_operators, wave, turn
    )

    if halving:
        send_edges, send, keep = terms
        got_edges = over_op(send_edges, lambda i: i ^ 1)
        got = over_op(send, lambda i: i ^ 1)
        token, (got,) = hold(token, got)
        token, (first, second) = edges(token, keep, got_edges, turned)
        one, two = swapped(first, 0), swapped(second, 1)
        offset = width // 2
        token, (one,) = hold(token, one, cost=1200000000)
        bit = 2
        token, (send, keep) = split(token, bit, chunk, levels, keep, got, one, two)
        got = over_op(send, lambda i: i ^ 2)
        token, last = choose(token, half, parts, got_ahead, last)
        while 2 * bit < n:
            bit *= 2
            token, (send, keep) = split(token, bit, chunk, levels, keep, got)
            got = over_op(send, lambda i, bit=bit: i ^ bit)
    else:
        (terms,) = terms
        offset = width
        odd = lax.rem(lax.axis_index("sec"), 2) == 1
        level = lax.axis_index("sec")
        upward = jnp.concatenate([terms[sectors + 1].astype(BF16), turned[sectors - 1]])
        downward = jnp.concatenate([terms[0].astype(BF16), turned[0]])
        one = swapped(jnp.where(odd, downward, upward), 0)
        two = swapped(jnp.where(odd, upward, downward), 1)
        below = jnp.where(odd, one, two)[:width].astype(F32)
        above = jnp.where(odd, two, one)[:width].astype(F32)
        mid = terms[1 : sectors + 1]
        mid = mid.at[0].add(jnp.where(level > 0, below, 0.0))
        mid = mid.at[sectors - 1].add(jnp.where(level < levels - 1, above, 0.0))
        summed = lax.psum_scatter(mid, "op", scatter_dimension=1, tiled=True)
        token, last = choose(token, half, parts, got_ahead, last)

    if len(last) > 1:
        token, last[1:] = hold(token, *last[1:])
    got_last = [over_op(x, lambda i: relay(i) if end(i) else opposite(i)) for x in last]
    fixed = (offset, levels, half, turned, turn, one, two)
    meta = sectors * width
    whole = (0, sectors)
    token, (out,) = renorm(
        token,
        "renorm_first",
        (
            (((0, 0, 0, meta),), "core", 1, *whole),
            (((0, rows, 0, rows + meta),), "core", 0, *whole),
            (((2, 0, 2, meta), (1, 0, 1, meta)), "side", 0, *whole),
            (((1, 0, 1, meta), (2, 0, 2, meta)), 3, 1, *whole),
        ),
        (from_core, got_ahead, got_behind),
        None,
        *fixed,
        cost=2100000000,
    )
    scale = 1.0 / math.sqrt(pairs * n)
    for i, (begin, stop) in enumerate(parts):
        final = i == len(parts) - 1
        piece = begin * width
        behind_first = (parts[0][1] - parts[0][0]) * width
        token, (out, *sums) = renorm(
            token,
            "renorm_last",
            (
                (
                    ((1, 0, 2, behind_first), (0, rows + piece, 0, rows + meta)),
                    "side",
                    1,
                    begin,
                    stop,
                ),
                (((0, rows + piece, 0, rows + meta), (1, 0, 2, behind_first)), 3, 0, begin, stop),
            ),
            (got_ahead, got_last[i], got_last[0]),
            out,
            *fixed,
            sums=(keep, got) if halving and i == 0 else (),
            scale=scale if halving and i == 0 else None,
            cost=0 if final else 2000000000,
        )
        if sums:
            (sigma_vector,) = sums
    if not halving:
        sigma_vector = summed * scale
    return sigma_vector, out


def solution(mesh):
    placed = (
        P("sec", None, None),
        P("op", "sec", None, None),
        P("op", "sec", None, None),
        P("sec", None, None),
        P("op"),
        P("op", "sec"),
        P("op", None),
    )
    return jax.shard_map(
        body,
        mesh=mesh,
        in_specs=placed,
        out_specs=(P("sec", "op", None), P("op", "sec", None, None)),
        check_vma=False,
    )
```

```python
import functools
import math

import jax
import jax.numpy as jnp
from jax import lax
from jax.experimental import pallas as pl
from jax.experimental.pallas import tpu as pltpu
from jax.sharding import PartitionSpec as P

DIRS = 4
CAPS = 2

STEP = 2_000_000_000

BF16 = jnp.bfloat16
F32 = jnp.float32
ANY = pl.BlockSpec(memory_space=pl.ANY)
HBM = pl.BlockSpec(memory_space=pltpu.HBM)
VMEM = pl.BlockSpec(memory_space=pltpu.VMEM)


def kernel_call(kernel, token, operands, in_specs, out_shape, out_specs, **options):
    mib = options.pop("mib")
    aliases = options.pop("aliases", {})
    grid = options.pop("grid", ())
    ahead = 0 if token is None else 1
    taken = len(operands) + ahead

    def run(*refs):
        refs = list(refs)
        del refs[taken]
        kernel(*refs[ahead:])

    outs = pl.pallas_call(
        run,
        grid=grid,
        out_shape=[jax.ShapeDtypeStruct((8, 128), F32), *out_shape],
        in_specs=[HBM] * ahead + list(in_specs),
        out_specs=[HBM, *out_specs],
        input_output_aliases={i + ahead: o + 1 for i, o in aliases.items()},
        compiler_params=pltpu.CompilerParams(vmem_limit_bytes=mib * 1024 * 1024),
        **options,
    )(*([] if token is None else [token]), *operands)
    return outs[0], list(outs[1:])


def in_hbm(value):
    return pltpu.with_memory_space_constraint(value, pltpu.HBM)


def estimate(flops):
    return pl.CostEstimate(flops=flops, bytes_accessed=0, transcendentals=0)


def fetch_scalars(pairs, sem):
    copies = [pltpu.make_async_copy(source, kept, sem) for source, kept in pairs]
    for copy in copies:
        copy.start()
    for copy in copies:
        copy.wait()


def meta_rows(sectors):
    return -(-2 * (2 + sectors) // 16) * 16


def at_end(half):
    place = lax.rem(lax.axis_index("op"), half)
    return jnp.logical_or(place == 0, place == half - 1)


def pick(kinds, places, kind, place):
    index = jnp.int32(0)
    for p, (own, at) in enumerate(zip(kinds, places)):
        match = at == place if kind is None else jnp.logical_and(at == place, own == kind)
        index = index + jnp.where(match, p, 0)
    return index


def copy_pairs(roles, half, outs, left, directions, charges, present):
    count, sectors, width, _ = left.shape
    kinds = [directions[p] for p in range(count)]
    places = []
    for p in range(count):
        place = jnp.int32(0)
        for q in range(p):
            place = place + jnp.where(kinds[q] == kinds[p], 1, 0)
        places.append(place)
    odd = lax.rem(lax.axis_index("op"), 2)
    end = at_end(half)
    found = {
        "extra": pick(kinds, places, None, 1),
        "half": pick(kinds, places, 3, 0),
        "core": pick(kinds, places, 1 + odd, 0),
        "side": pick(kinds, places, 2 - odd, 0),
    }

    def index_of(role):
        return found[role] if isinstance(role, str) else jnp.where(end, *map(found.get, role))

    height = meta_rows(sectors)
    row = lax.broadcasted_iota(jnp.int32, (height, width), 0)
    for out, (sent, told) in zip(outs, roles):
        for i, role in enumerate(sent):
            index = index_of(role)
            for s in range(sectors):
                at = (i * sectors + s) * width
                out[at : at + width] = left[index, s]
        if not told:
            continue
        values = jnp.zeros((height, width), jnp.int32)
        for i, role in enumerate(told):
            index = index_of(role)
            at = i * (height // 2)
            kind = jnp.int32(0)
            for p in range(count):
                kind = kind + jnp.where(index == p, kinds[p], 0)
            values = jnp.where(row == at, charges[index], jnp.where(row == at + 1, kind, values))
            for s in range(sectors):
                values = jnp.where(row == at + 2 + s, present[index, s], values)
        at = len(sent) * sectors * width
        out[at : at + height] = values.astype(F32).astype(BF16)


def stage_kernel(roles, half, directions_ref, charges_ref, present_ref, left_ref, *refs):
    outs = refs[: len(roles)]
    left, directions, charges, present, few, sem = refs[len(roles) :]
    bulk = [
        pltpu.make_async_copy(left_ref.at[p], left.at[p], sem) for p in range(left.shape[0])
    ]
    for copy in bulk:
        copy.start()
    fetch_scalars(
        [(directions_ref, directions), (charges_ref, charges), (present_ref, present)], few
    )
    for copy in bulk:
        copy.wait()
    copy_pairs(roles, half, outs, left, directions, charges, present)


def restage_kernel(
    roles, half, directions_ref, charges_ref, present_ref, left, wave_ref, rot_ref, *refs
):
    outs = refs[: len(roles)]
    wave, rot, directions, charges, present, few, sems = refs[len(roles) :]
    bulk = [
        pltpu.make_async_copy(wave_ref, wave, sems.at[0]),
        pltpu.make_async_copy(rot_ref, rot, sems.at[1]),
    ]
    for copy in bulk:
        copy.start()
    fetch_scalars(
        [(directions_ref, directions), (charges_ref, charges), (present_ref, present)], few
    )
    copy_pairs(roles, half, outs, left, directions, charges, present)
    for copy in bulk:
        copy.wait()


def staged(token, roles, half, directions, charges, present, left, *more):
    count, sectors, width, _ = left.shape
    shapes = [
        (len(sent) * sectors * width + (meta_rows(sectors) if told else 0), width)
        for sent, told in roles
    ]
    shapes += [x.shape for x in more] if more else [left.shape]
    operands = [in_hbm(x) for x in (directions, charges, present)]
    operands += [left, *map(in_hbm, more)] if more else [in_hbm(left)]
    return kernel_call(
        functools.partial(restage_kernel if more else stage_kernel, roles, half),
        token,
        operands,
        [HBM] * 3 + ([VMEM] + [HBM] * len(more) if more else [HBM]),
        [pltpu.VMEM(shape, BF16) for shape in shapes],
        [VMEM] * len(shapes),
        scratch_shapes=[
            pltpu.SMEM((count,), jnp.int32),
            pltpu.SMEM((count,), jnp.int32),
            pltpu.SMEM((count, sectors), jnp.int32),
            pltpu.SemaphoreType.DMA,
            pltpu.SemaphoreType.DMA((len(more),)) if more else pltpu.SemaphoreType.DMA,
        ],
        mib=4,
        cost_estimate=estimate(0),
        name="restage" if more else "stage",
    )


def sigma_kernel(split, chunk, charges_ref, present_ref, left, right_ref, wave, rotations, *refs):
    outs, (acc, right, charges, present, few, sems) = refs[:-6], refs[-6:]
    count, sectors, width, _ = left.shape
    small = [
        pltpu.make_async_copy(charges_ref, charges, few),
        pltpu.make_async_copy(present_ref, present, few),
    ]
    loads = [pltpu.make_async_copy(right_ref.at[p], right.at[p], sems.at[p]) for p in range(count)]
    for copy in small + loads:
        copy.start()
    acc[...] = jnp.zeros_like(acc)
    for s in range(sectors):
        outs[-1][s] = rotations[s].T
    for copy in small:
        copy.wait()

    def step(pair, carry):
        pltpu.make_async_copy(right_ref.at[pair], right.at[pair], sems.at[pair]).wait()
        charge = charges[pair]
        for s in range(sectors):
            halfway = jnp.dot(left[pair, s], wave[s], preferred_element_type=F32)
            halfway = (halfway * present[pair, s].astype(F32)).astype(BF16)
            term = lax.dot_general(
                halfway, right[pair, s], (((1,), (1,)), ((), ())), preferred_element_type=F32
            )
            acc[jnp.clip(s + 1 + charge, 0, sectors + 1)] += term
        return carry

    lax.fori_loop(0, count, step, 0)
    if not split:
        outs[0][...] = acc[...]
        return
    bit = lax.rem(lax.axis_index("op"), 2)
    for q in range(width // chunk // 2):
        to = slice(q * chunk, (q + 1) * chunk)
        for t in range(sectors + 2):
            away = acc[t, pl.ds((2 * q + 1 - bit) * chunk, chunk)].astype(BF16)
            if 0 < t <= sectors:
                outs[1][t - 1, to] = away
            else:
                outs[0][min(t, 1), to] = away
            outs[2][t, to] = acc[t, pl.ds((2 * q + bit) * chunk, chunk)]


def sigma_terms(token, split, chunk, charges, present, left, right, wave, rotations):
    count, sectors, width, _ = left.shape
    if split:
        shapes = [
            ((2, width // 2, width), BF16),
            ((sectors, width // 2, width), BF16),
            ((sectors + 2, width // 2, width), F32),
        ]
    else:
        shapes = [((sectors + 2, width, width), F32)]
    shapes.append(((sectors, width, width), BF16))
    return kernel_call(
        functools.partial(sigma_kernel, split, chunk),
        token,
        (in_hbm(charges), in_hbm(present), left, in_hbm(right), wave, rotations),
        [HBM, HBM, VMEM, HBM, VMEM, VMEM],
        [pltpu.VMEM(*shape) for shape in shapes],
        [VMEM] * len(shapes),
        scratch_shapes=[
            pltpu.VMEM((sectors + 2, width, width), F32),
            pltpu.VMEM(right.shape, BF16),
            pltpu.SMEM((count,), jnp.int32),
            pltpu.SMEM((count, sectors), jnp.int32),
            pltpu.SemaphoreType.DMA,
            pltpu.SemaphoreType.DMA((count,)),
        ],
        mib=10,
        cost_estimate=estimate(0),
        name="sigma_terms",
    )


def edges_kernel(keep, got, turned, first, second):
    outer, height, _ = keep.shape
    odd = lax.rem(lax.axis_index("sec"), 2)
    for out, upward in ((first, odd == 0), (second, odd == 1)):
        edge = jnp.where(upward, outer - 1, 0)
        out[:height] = (keep[edge] + got[jnp.where(upward, 1, 0)].astype(F32)).astype(BF16)
        out[height:] = turned[jnp.where(upward, outer - 3, 0)]


def edges(token, keep, got, turned):
    _, height, width = keep.shape
    shape = (height + turned.shape[1], width)
    return kernel_call(
        edges_kernel,
        token,
        (keep, got, turned),
        [VMEM] * 3,
        [jax.ShapeDtypeStruct(shape, BF16)] * 2,
        [VMEM] * 2,
        mib=4,
        cost_estimate=estimate(0),
        name="edges",
    )


def split_kernel(bit, chunk, levels, first, held, *refs):
    if first:
        got, one, two, send, keep = refs
    else:
        got, send, keep = refs
    sectors, height, _ = got.shape
    own = lax.rem(lax.axis_index("op") // bit, 2)
    level = lax.axis_index("sec")
    odd = lax.rem(level, 2) == 1

    def total(s, rows):
        if not first:
            return held[s, rows] + got[s, rows].astype(F32)
        value = held[s + 1, rows] + got[s, rows].astype(F32)
        if s == 0:
            below = jnp.where(odd, one[rows], two[rows]).astype(F32)
            value = value + jnp.where(level > 0, below, 0.0)
        if s == sectors - 1:
            above = jnp.where(odd, two[rows], one[rows]).astype(F32)
            value = value + jnp.where(level < levels - 1, above, 0.0)
        return value

    for q in range(height // chunk // 2):
        to = slice(q * chunk, (q + 1) * chunk)
        for s in range(sectors):
            send[s, to] = total(s, pl.ds((2 * q + 1 - own) * chunk, chunk)).astype(BF16)
            keep[s, to] = total(s, pl.ds((2 * q + own) * chunk, chunk))


def split(token, bit, chunk, levels, held, got, *edge):
    sectors, height, width = got.shape
    return kernel_call(
        functools.partial(split_kernel, bit, chunk, levels, len(edge) == 2),
        token,
        (held, got, *edge),
        [VMEM] * (2 + len(edge)),
        [
            jax.ShapeDtypeStruct((sectors, height // 2, width), BF16),
            jax.ShapeDtypeStruct((sectors, height // 2, width), F32),
        ],
        [VMEM] * 2,
        mib=4,
        cost_estimate=estimate(0 if edge else STEP),
        name="split",
    )


def hold_kernel(*refs):
    pass


def hold(token, *values, cost=0):
    return kernel_call(
        hold_kernel,
        token,
        values,
        [ANY] * len(values),
        [jax.ShapeDtypeStruct(value.shape, value.dtype) for value in values],
        [ANY] * len(values),
        aliases={i: i for i in range(len(values))},
        mib=1,
        cost_estimate=estimate(cost),
        name="hold",
    )


def choose_kernel(half, cuts, first, second, *outs):
    end = at_end(half)

    def fill(source):
        for out, (at, size) in zip(outs, cuts):
            out[...] = source[at : at + size]

    @pl.when(end)
    def _():
        fill(first)

    @pl.when(jnp.logical_not(end))
    def _():
        fill(second)


def choose(token, half, parts, first, second):
    width = second.shape[1]
    cuts = [(begin * width, (stop - begin) * width) for begin, stop in parts]
    return kernel_call(
        functools.partial(choose_kernel, half, cuts),
        token,
        (first, second),
        [VMEM] * 2,
        [pltpu.VMEM((size, width), BF16) for _, size in cuts],
        [VMEM] * len(cuts),
        mib=4,
        cost_estimate=estimate(0),
        name="choose",
    )


def renorm_kernel(items, zero, offset, levels, half, turned, rotations, one, two, *refs):
    buffers = refs[: 1 + max(buffer for came, told, *_ in items for buffer in (came[0], told[0]))]
    rest = refs[len(buffers) + (0 if zero else 1) :]
    out, edge, results, done = rest
    sectors, width, _ = rotations.shape
    odd = lax.rem(lax.axis_index("op"), 2)
    end = at_end(half)
    level = lax.axis_index("sec")
    raised = lax.rem(level, 2) == 1
    rows = pl.ds(offset, width)
    height = meta_rows(sectors)
    stores = []
    if zero:
        results[len(items)] = jnp.zeros_like(results[len(items)])
        for place in range(CAPS):
            copy = pltpu.make_async_copy(results.at[len(items)], out.at[place], done)
            copy.start()
            stores.append(copy)
    if any(begin == 0 for *_, begin, _ in items):
        edge[0] = jnp.where(raised, one[rows], two[rows])
    if any(stop == sectors for *_, stop in items):
        edge[1] = jnp.where(raised, two[rows], one[rows])
    kinds = {"core": 2 - odd, "side": 1 + odd, "half": 3}
    for i, ((buffer, base), (about, top, slot), targets, begin, stop) in enumerate(items):
        values = buffers[about][pl.ds(top, height)].astype(F32)
        values = values[slot * (height // 2) : (slot + 1) * (height // 2)]
        charge = jnp.max(values[:1]).astype(jnp.int32)
        kind, place = (kinds[targets[0][0]], targets[0][1])
        if len(targets) > 1:
            kind = jnp.where(end, kind, kinds[targets[1][0]])
            place = jnp.where(end, place, targets[1][1])
        weights = values[2 : 2 + sectors]
        named = jnp.where(values[1:2] == jnp.asarray(kind).astype(F32), weights, 0.0)
        weights = jnp.where(place == 1, named, weights)
        for s in range(begin, stop):
            at = s + charge
            whole = level * sectors + at
            inside = jnp.logical_and(whole >= 0, whole < levels * sectors)
            weight = jnp.where(inside, weights[s : s + 1], 0.0)
            block = buffers[buffer][pl.ds(base + (s - begin) * width, width)]
            rotated = jnp.dot(block, rotations[s], preferred_element_type=F32).astype(BF16)
            target = turned[jnp.clip(at, 0, sectors - 1)]
            if s == 0:
                target = jnp.where(at < 0, edge[0], target)
            if s == sectors - 1:
                target = jnp.where(at > sectors - 1, edge[1], target)
            value = jnp.dot(target, rotated, preferred_element_type=F32) * weight
            results[i, s] = value.astype(BF16)
            copy = pltpu.make_async_copy(results.at[i, s], out.at[kind * CAPS + place, s], done)
            copy.start()
            stores.append(copy)
    for copy in stores:
        copy.wait()


def renorm(
    token, name, items, buffers, out, offset, levels, half, turned, rotations, one, two, cost=0
):
    sectors, width, _ = rotations.shape
    zero = out is None
    operands = [turned, rotations, one, two, *buffers]
    in_specs = [VMEM] * len(operands)
    if not zero:
        operands.append(out)
        in_specs.append(HBM)
    count = len(items)
    block = (sectors, width, width)
    token, (out,) = kernel_call(
        functools.partial(renorm_kernel, items, zero, offset, levels, half),
        token,
        operands,
        in_specs,
        [jax.ShapeDtypeStruct((DIRS * CAPS, *block), BF16)],
        [HBM],
        aliases={} if zero else {len(operands) - 1: 0},
        scratch_shapes=[
            pltpu.VMEM((2, width, width), BF16),
            pltpu.VMEM((count + (1 if zero else 0), *block), BF16),
            pltpu.SemaphoreType.DMA,
        ],
        mib=8,
        cost_estimate=estimate(cost),
        name=name,
    )
    return token, out


def finish_kernel(scale, keep, got, out):
    out[...] = (keep[...] + got[...].astype(F32)) * scale


def finish(token, scale, keep, got):
    return kernel_call(
        functools.partial(finish_kernel, scale),
        token,
        (keep, got),
        [VMEM] * 2,
        [jax.ShapeDtypeStruct(keep.shape, F32)],
        [VMEM],
        mib=4,
        cost_estimate=estimate(STEP),
        name="finish",
    )


def body(
    wavefunction, left_operators, right_operators, rotations, charges, present_blocks, directions
):
    sectors, width, _ = wavefunction.shape
    pairs = left_operators.shape[0]
    n = lax.axis_size("op")
    levels = lax.axis_size("sec")
    half = n // 2
    chunk = width // n
    halving = n >= 4 and n & (n - 1) == 0 and chunk % 16 == 0
    rows = sectors * width
    parts = [(0, sectors // 2), (sectors // 2, sectors)] if sectors > 1 else [(0, 1)]

    def over_op(value, target):
        return lax.ppermute(value, "op", [(i, target(i)) for i in range(n)])

    def swapped(value, start):
        to = list(range(levels))
        for i in range(start, levels - 1, 2):
            to[i], to[i + 1] = i + 1, i
        return lax.ppermute(value, "sec", list(enumerate(to)))

    def side(i):
        return (i + 1) % n if i % 2 else (i - 1) % n

    def end(i):
        return i % half in (0, half - 1)

    def opposite(i):
        return (i + half) % n

    def relay(i):
        return i - i % half + half - 1 - i % half

    small = (directions[:, 0], charges, present_blocks)
    ahead_roles = (("extra", "side"), ("half", "extra"))
    behind_roles = (("side", "extra"), ("extra", "half"))
    core_roles = ("extra", "core")
    token, (ahead, left) = staged(
        None, ((ahead_roles, ahead_roles),), half, *small, left_operators
    )
    token, (behind, last, first_core, wave, turn) = staged(
        token,
        ((behind_roles[:1], behind_roles), (("half",), ()), (core_roles, core_roles)),
        half,
        *small,
        left,
        wavefunction,
        rotations,
    )
    got_ahead = over_op(ahead, lambda i: opposite(i) if end(i) else side(i))
    got_behind = over_op(behind, lambda i: side(i) if end(i) else opposite(i))
    from_core = over_op(first_core, lambda i: i ^ 1)
    token, (*terms, turned) = sigma_terms(
        token, halving, chunk, charges, present_blocks, left, right_operators, wave, turn
    )

    if halving:
        send_edges, send, keep = terms
        got_edges = over_op(send_edges, lambda i: i ^ 1)
        got = over_op(send, lambda i: i ^ 1)
        token, (got,) = hold(token, got)
        token, (first, second) = edges(token, keep, got_edges, turned)
        one, two = swapped(first, 0), swapped(second, 1)
        offset = width // 2
        token, (one,) = hold(token, one, cost=STEP // 2)
        bit = 2
        token, (send, keep) = split(token, bit, chunk, levels, keep, got, one, two)
        got = over_op(send, lambda i: i ^ 2)
        token, last = choose(token, half, parts, got_ahead, last)
        while 2 * bit < n:
            bit *= 2
            token, (send, keep) = split(token, bit, chunk, levels, keep, got)
            got = over_op(send, lambda i, bit=bit: i ^ bit)
    else:
        (terms,) = terms
        offset = width
        odd = lax.rem(lax.axis_index("sec"), 2) == 1
        level = lax.axis_index("sec")
        upward = jnp.concatenate([terms[sectors + 1].astype(BF16), turned[sectors - 1]])
        downward = jnp.concatenate([terms[0].astype(BF16), turned[0]])
        one = swapped(jnp.where(odd, downward, upward), 0)
        two = swapped(jnp.where(odd, upward, downward), 1)
        below = jnp.where(odd, one, two)[:width].astype(F32)
        above = jnp.where(odd, two, one)[:width].astype(F32)
        mid = terms[1 : sectors + 1]
        mid = mid.at[0].add(jnp.where(level > 0, below, 0.0))
        mid = mid.at[sectors - 1].add(jnp.where(level < levels - 1, above, 0.0))
        summed = lax.psum_scatter(mid, "op", scatter_dimension=1, tiled=True)
        token, last = choose(token, half, parts, got_ahead, last)

    if len(last) > 1:
        token, last[1:] = hold(token, *last[1:])
    got_last = [over_op(x, lambda i: relay(i) if end(i) else opposite(i)) for x in last]
    fixed = (offset, levels, half, turned, turn, one, two)
    whole = (0, sectors)
    token, out = renorm(
        token,
        "renorm_first",
        (
            ((0, 0), (0, 2 * rows, 0), (("core", 1),), *whole),
            ((0, rows), (0, 2 * rows, 1), (("core", 0),), *whole),
            ((1, 0), (1, 2 * rows, 0), (("half", 1), ("side", 0)), *whole),
            ((1, rows), (1, 2 * rows, 1), (("half", 0), ("side", 1)), *whole),
            ((2, 0), (2, rows, 0), (("side", 0), ("half", 1)), *whole),
        ),
        (from_core, got_ahead, got_behind),
        None,
        *fixed,
        cost=STEP,
    )
    scale = 1.0 / math.sqrt(pairs * n)
    for i, (begin, stop) in enumerate(parts):
        if halving and i == len(parts) - 1:
            token, (sigma_vector,) = finish(token, scale, keep, got)
        token, out = renorm(
            token,
            "renorm_last",
            (((0, 0), (1, rows, 1), (("side", 1), ("half", 0)), begin, stop),),
            (got_last[i], got_behind),
            out,
            *fixed,
        )
    if not halving:
        sigma_vector = summed * scale
    return sigma_vector, out


def solution(mesh):
    placed = (
        P("sec", None, None),
        P("op", "sec", None, None),
        P("op", "sec", None, None),
        P("sec", None, None),
        P("op"),
        P("op", "sec"),
        P("op", None),
    )
    return jax.shard_map(
        body,
        mesh=mesh,
        in_specs=placed,
        out_specs=(P("sec", "op", None), P("op", "sec", None, None)),
        check_vma=False,
    )
```

```python
import functools
import math

import jax
import jax.numpy as jnp
from jax import lax
from jax.experimental import pallas as pl
from jax.experimental.pallas import tpu as pltpu
from jax.sharding import PartitionSpec as P

DIRS = 4
CAPS = 2

PEAK = 1_153_500_000

BF16 = jnp.bfloat16
F32 = jnp.float32
ANY = pl.BlockSpec(memory_space=pl.ANY)
HBM = pl.BlockSpec(memory_space=pltpu.HBM)
VMEM = pl.BlockSpec(memory_space=pltpu.VMEM)


def kernel_call(kernel, token, operands, in_specs, out_shape, out_specs, **options):
    mib = options.pop("mib")
    aliases = options.pop("aliases", {})
    grid = options.pop("grid", ())
    ahead = 0 if token is None else 1
    taken = len(operands) + ahead

    def run(*refs):
        refs = list(refs)
        del refs[taken]
        kernel(*refs[ahead:])

    outs = pl.pallas_call(
        run,
        grid=grid,
        out_shape=[jax.ShapeDtypeStruct((8, 128), F32), *out_shape],
        in_specs=[HBM] * ahead + list(in_specs),
        out_specs=[HBM, *out_specs],
        input_output_aliases={i + ahead: o + 1 for i, o in aliases.items()},
        compiler_params=pltpu.CompilerParams(vmem_limit_bytes=mib * 1024 * 1024),
        **options,
    )(*([] if token is None else [token]), *operands)
    return outs[0], list(outs[1:])


def in_hbm(value):
    return pltpu.with_memory_space_constraint(value, pltpu.HBM)


def estimate(microseconds):
    return pl.CostEstimate(flops=int(microseconds * PEAK), bytes_accessed=0, transcendentals=0)


def fetch_scalars(pairs, sem):
    copies = [pltpu.make_async_copy(source, kept, sem) for source, kept in pairs]
    for copy in copies:
        copy.start()
    for copy in copies:
        copy.wait()


def meta_rows(sectors):
    return -(-2 * (2 + sectors) // 16) * 16


def at_end(half):
    place = lax.rem(lax.axis_index("op"), half)
    return jnp.logical_or(place == 0, place == half - 1)


def pick(kinds, places, kind, place):
    index = jnp.int32(0)
    for p, (own, at) in enumerate(zip(kinds, places)):
        match = at == place if kind is None else jnp.logical_and(at == place, own == kind)
        index = index + jnp.where(match, p, 0)
    return index


def copy_pairs(roles, half, outs, left, directions, charges, present):
    count, _, width, _ = left.shape
    sectors = present.shape[1]
    kinds = [directions[p] for p in range(count)]
    places = []
    for p in range(count):
        place = jnp.int32(0)
        for q in range(p):
            place = place + jnp.where(kinds[q] == kinds[p], 1, 0)
        places.append(place)
    odd = lax.rem(lax.axis_index("op"), 2)
    end = at_end(half)
    found = {
        "extra": pick(kinds, places, None, 1),
        "half": pick(kinds, places, 3, 0),
        "core": pick(kinds, places, 1 + odd, 0),
        "side": pick(kinds, places, 2 - odd, 0),
    }

    def index_of(role):
        return found[role] if isinstance(role, str) else jnp.where(end, *map(found.get, role))

    height = meta_rows(sectors)
    row = lax.broadcasted_iota(jnp.int32, (height, width), 0)
    for out, (sent, told, begin, stop) in zip(outs, roles):
        for i, role in enumerate(sent):
            index = index_of(role)
            for s in range(begin, stop):
                at = (i * (stop - begin) + s - begin) * width
                out[at : at + width] = left[index, s]
        if not told:
            continue
        values = jnp.zeros((height, width), jnp.int32)
        for i, role in enumerate(told):
            index = index_of(role)
            at = i * (height // 2)
            kind = jnp.int32(0)
            for p in range(count):
                kind = kind + jnp.where(index == p, kinds[p], 0)
            values = jnp.where(row == at, charges[index], jnp.where(row == at + 1, kind, values))
            for s in range(sectors):
                values = jnp.where(row == at + 2 + s, present[index, s], values)
        at = len(sent) * (stop - begin) * width
        out[at : at + height] = values.astype(F32).astype(BF16)


def stage_kernel(roles, half, directions_ref, charges_ref, present_ref, left_ref, *refs):
    *outs, left, directions, charges, present, few, sem = refs
    first = left.shape[1]
    bulk = [
        pltpu.make_async_copy(left_ref.at[p, pl.ds(0, first)], left.at[p], sem)
        for p in range(left.shape[0])
    ]
    for copy in bulk:
        copy.start()
    fetch_scalars(
        [(directions_ref, directions), (charges_ref, charges), (present_ref, present)], few
    )
    for copy in bulk:
        copy.wait()
    copy_pairs(roles, half, outs, left, directions, charges, present)


def restage_kernel(
    roles, half, directions_ref, charges_ref, present_ref, left_ref, wave_ref, rot_ref, *refs
):
    outs = refs[: len(roles)]
    left, wave, rot, directions, charges, present, few, sems = refs[len(roles) :]
    bulk = [
        pltpu.make_async_copy(left_ref, left, sems.at[0]),
        pltpu.make_async_copy(wave_ref, wave, sems.at[1]),
        pltpu.make_async_copy(rot_ref, rot, sems.at[2]),
    ]
    for copy in bulk:
        copy.start()
    fetch_scalars(
        [(directions_ref, directions), (charges_ref, charges), (present_ref, present)], few
    )
    bulk[0].wait()
    copy_pairs(roles, half, outs, left, directions, charges, present)
    for copy in bulk[1:]:
        copy.wait()


def staged(token, roles, half, directions, charges, present, *bulk):
    count, sectors, width, _ = bulk[0].shape
    shapes = [
        (len(sent) * (stop - begin) * width + (meta_rows(sectors) if told else 0), width)
        for sent, told, begin, stop in roles
    ]
    scratch = [
        pltpu.SMEM((count,), jnp.int32),
        pltpu.SMEM((count,), jnp.int32),
        pltpu.SMEM((count, sectors), jnp.int32),
        pltpu.SemaphoreType.DMA,
    ]
    if token is None:
        scratch.insert(0, pltpu.VMEM((count, roles[0][3], width, width), BF16))
        scratch.append(pltpu.SemaphoreType.DMA)
    else:
        shapes += [x.shape for x in bulk]
        scratch.append(pltpu.SemaphoreType.DMA((3,)))
    return kernel_call(
        functools.partial(stage_kernel if token is None else restage_kernel, roles, half),
        token,
        [in_hbm(x) for x in (directions, charges, present, *bulk)],
        [HBM] * (3 + len(bulk)),
        [pltpu.VMEM(shape, BF16) for shape in shapes],
        [VMEM] * len(shapes),
        scratch_shapes=scratch,
        mib=6,
        cost_estimate=estimate(0),
        name="stage" if token is None else "restage",
    )


def grouped_few(sectors):
    return max(0, sectors // 2 - 1)


def grouped(target, sectors):
    few = grouped_few(sectors)
    if target in (0, sectors + 1):
        return 0, min(target, 1)
    return (0, 1 + target) if target <= few else (1, target - 1 - few)


def sigma_kernel(split, chunk, charges_ref, present_ref, left, right_ref, wave, rotations, *refs):
    outs, (acc, right, charges, present, few, sems) = refs[:-6], refs[-6:]
    count, sectors, width, _ = left.shape
    small = [
        pltpu.make_async_copy(charges_ref, charges, few),
        pltpu.make_async_copy(present_ref, present, few),
    ]
    loads = [pltpu.make_async_copy(right_ref.at[p], right.at[p], sems.at[p]) for p in range(count)]
    for copy in small + loads:
        copy.start()
    acc[...] = jnp.zeros_like(acc)
    for s in range(sectors):
        outs[-1][s] = rotations[s].T
    for copy in small:
        copy.wait()

    def step(pair, carry):
        pltpu.make_async_copy(right_ref.at[pair], right.at[pair], sems.at[pair]).wait()
        charge = charges[pair]
        for s in range(sectors):
            halfway = jnp.dot(left[pair, s], wave[s], preferred_element_type=F32)
            halfway = (halfway * present[pair, s].astype(F32)).astype(BF16)
            term = lax.dot_general(
                halfway, right[pair, s], (((1,), (1,)), ((), ())), preferred_element_type=F32
            )
            acc[jnp.clip(s + 1 + charge, 0, sectors + 1)] += term
        return carry

    lax.fori_loop(0, count, step, 0)
    if not split:
        outs[0][...] = acc[...]
        return
    bit = lax.rem(lax.axis_index("op"), 2)
    for q in range(width // chunk // 2):
        to = slice(q * chunk, (q + 1) * chunk)
        for t in range(sectors + 2):
            away = acc[t, pl.ds((2 * q + 1 - bit) * chunk, chunk)].astype(BF16)
            group, place = grouped(t, sectors)
            outs[group][place, to] = away
            outs[2][t, to] = acc[t, pl.ds((2 * q + bit) * chunk, chunk)]


def sigma_terms(token, split, chunk, charges, present, left, right, wave, rotations):
    count, sectors, width, _ = left.shape
    if split:
        few = grouped_few(sectors)
        shapes = [
            ((2 + few, width // 2, width), BF16),
            ((sectors - few, width // 2, width), BF16),
            ((sectors + 2, width // 2, width), F32),
        ]
    else:
        shapes = [((sectors + 2, width, width), F32)]
    shapes.append(((sectors, width, width), BF16))
    return kernel_call(
        functools.partial(sigma_kernel, split, chunk),
        token,
        (in_hbm(charges), in_hbm(present), left, in_hbm(right), wave, rotations),
        [HBM, HBM, VMEM, HBM, VMEM, VMEM],
        [pltpu.VMEM(*shape) for shape in shapes],
        [VMEM] * len(shapes),
        scratch_shapes=[
            pltpu.VMEM((sectors + 2, width, width), F32),
            pltpu.VMEM(right.shape, BF16),
            pltpu.SMEM((count,), jnp.int32),
            pltpu.SMEM((count, sectors), jnp.int32),
            pltpu.SemaphoreType.DMA,
            pltpu.SemaphoreType.DMA((count,)),
        ],
        mib=10,
        cost_estimate=estimate(0),
        name="sigma_terms",
    )


def edges_kernel(keep, got, turned, first, second):
    outer, height, _ = keep.shape
    odd = lax.rem(lax.axis_index("sec"), 2)
    for out, upward in ((first, odd == 0), (second, odd == 1)):
        edge = jnp.where(upward, outer - 1, 0)
        out[:height] = (keep[edge] + got[jnp.where(upward, 1, 0)].astype(F32)).astype(BF16)
        out[height:] = turned[jnp.where(upward, outer - 3, 0)]


def edges(token, keep, got, turned):
    _, height, width = keep.shape
    shape = (height + turned.shape[1], width)
    return kernel_call(
        edges_kernel,
        token,
        (keep, got, turned),
        [VMEM] * 3,
        [jax.ShapeDtypeStruct(shape, BF16)] * 2,
        [VMEM] * 2,
        mib=4,
        cost_estimate=estimate(0),
        name="edges",
    )


def split_kernel(bit, chunk, levels, first, held, *refs):
    if first:
        *core, one, two, send, keep = refs
    else:
        got, send, keep = refs
    sectors, height = send.shape[0], held.shape[1]
    own = lax.rem(lax.axis_index("op") // bit, 2)
    level = lax.axis_index("sec")
    odd = lax.rem(level, 2) == 1

    def total(s, rows):
        if not first:
            return held[s, rows] + got[s, rows].astype(F32)
        group, place = grouped(s + 1, sectors)
        value = held[s + 1, rows] + core[group][place, rows].astype(F32)
        if s == 0:
            below = jnp.where(odd, one[rows], two[rows]).astype(F32)
            value = value + jnp.where(level > 0, below, 0.0)
        if s == sectors - 1:
            above = jnp.where(odd, two[rows], one[rows]).astype(F32)
            value = value + jnp.where(level < levels - 1, above, 0.0)
        return value

    for q in range(height // chunk // 2):
        to = slice(q * chunk, (q + 1) * chunk)
        for s in range(sectors):
            send[s, to] = total(s, pl.ds((2 * q + 1 - own) * chunk, chunk)).astype(BF16)
            keep[s, to] = total(s, pl.ds((2 * q + own) * chunk, chunk))


def split(token, bit, chunk, levels, held, *got):
    first = len(got) > 1
    outer, height, width = held.shape
    sectors = outer - 2 if first else outer
    return kernel_call(
        functools.partial(split_kernel, bit, chunk, levels, first),
        token,
        (held, *got),
        [VMEM] * (1 + len(got)),
        [
            jax.ShapeDtypeStruct((sectors, height // 2, width), BF16),
            jax.ShapeDtypeStruct((sectors, height // 2, width), F32),
        ],
        [VMEM] * 2,
        mib=4,
        cost_estimate=estimate(0 if first else 1.3),
        name="split",
    )


def hold_kernel(*refs):
    pass


def hold(token, *values, cost=0):
    return kernel_call(
        hold_kernel,
        token,
        values,
        [ANY] * len(values),
        [jax.ShapeDtypeStruct(value.shape, value.dtype) for value in values],
        [ANY] * len(values),
        aliases={i: i for i in range(len(values))},
        mib=1,
        cost_estimate=estimate(cost),
        name="hold",
    )


def choose_kernel(half, parts, lead, front, rear, second, *outs):
    end = at_end(half)
    width = second.shape[1]

    @pl.when(end)
    def _():
        for out, (begin, stop) in zip(outs, parts):
            for s in range(begin, stop):
                source, at = (front, s) if s < lead else (rear, s - lead)
                out[(s - begin) * width : (s - begin + 1) * width] = source[
                    at * width : (at + 1) * width
                ]

    @pl.when(jnp.logical_not(end))
    def _():
        for out, (begin, stop) in zip(outs, parts):
            out[...] = second[begin * width : stop * width]


def choose(token, half, parts, lead, front, rear, second):
    width = second.shape[1]
    return kernel_call(
        functools.partial(choose_kernel, half, parts, lead),
        token,
        (front, rear, second),
        [VMEM] * 3,
        [pltpu.VMEM(((stop - begin) * width, width), BF16) for begin, stop in parts],
        [VMEM] * len(parts),
        mib=4,
        cost_estimate=estimate(0.9),
        name="choose",
    )


def renorm_kernel(items, zero, offset, levels, half, turned, rotations, one, two, *refs):
    buffers = refs[: 1 + max(buffer for came, told, *_ in items for buffer in (came[0], told[0]))]
    rest = refs[len(buffers) + (0 if zero else 1) :]
    out, edge, results, done = rest
    sectors, width, _ = rotations.shape
    odd = lax.rem(lax.axis_index("op"), 2)
    end = at_end(half)
    level = lax.axis_index("sec")
    raised = lax.rem(level, 2) == 1
    rows = pl.ds(offset, width)
    height = meta_rows(sectors)
    stores = []
    if zero:
        results[len(items)] = jnp.zeros_like(results[len(items)])
        for place in range(CAPS):
            copy = pltpu.make_async_copy(results.at[len(items)], out.at[place], done)
            copy.start()
            stores.append(copy)
    if any(begin == 0 for *_, begin, _ in items):
        edge[0] = jnp.where(raised, one[rows], two[rows])
    if any(stop == sectors for *_, stop in items):
        edge[1] = jnp.where(raised, two[rows], one[rows])
    kinds = {"core": 2 - odd, "side": 1 + odd, "half": 3}
    for i, ((buffer, base), (about, top, slot), targets, begin, stop) in enumerate(items):
        values = buffers[about][pl.ds(top, height)].astype(F32)
        values = values[slot * (height // 2) : (slot + 1) * (height // 2)]
        charge = jnp.max(values[:1]).astype(jnp.int32)
        kind, place = (kinds[targets[0][0]], targets[0][1])
        if len(targets) > 1:
            kind = jnp.where(end, kind, kinds[targets[1][0]])
            place = jnp.where(end, place, targets[1][1])
        weights = values[2 : 2 + sectors]
        named = jnp.where(values[1:2] == jnp.asarray(kind).astype(F32), weights, 0.0)
        weights = jnp.where(place == 1, named, weights)
        for s in range(begin, stop):
            at = s + charge
            whole = level * sectors + at
            inside = jnp.logical_and(whole >= 0, whole < levels * sectors)
            weight = jnp.where(inside, weights[s : s + 1], 0.0)
            block = buffers[buffer][pl.ds(base + (s - begin) * width, width)]
            rotated = jnp.dot(block, rotations[s], preferred_element_type=F32).astype(BF16)
            target = turned[jnp.clip(at, 0, sectors - 1)]
            if s == 0:
                target = jnp.where(at < 0, edge[0], target)
            if s == sectors - 1:
                target = jnp.where(at > sectors - 1, edge[1], target)
            value = jnp.dot(target, rotated, preferred_element_type=F32) * weight
            results[i, s] = value.astype(BF16)
            copy = pltpu.make_async_copy(results.at[i, s], out.at[kind * CAPS + place, s], done)
            copy.start()
            stores.append(copy)
    for copy in stores:
        copy.wait()


def renorm(
    token, name, items, buffers, out, offset, levels, half, turned, rotations, one, two, cost=0
):
    sectors, width, _ = rotations.shape
    zero = out is None
    operands = [turned, rotations, one, two, *buffers]
    in_specs = [VMEM] * len(operands)
    if not zero:
        operands.append(out)
        in_specs.append(HBM)
    count = len(items)
    block = (sectors, width, width)
    token, (out,) = kernel_call(
        functools.partial(renorm_kernel, items, zero, offset, levels, half),
        token,
        operands,
        in_specs,
        [jax.ShapeDtypeStruct((DIRS * CAPS, *block), BF16)],
        [HBM],
        aliases={} if zero else {len(operands) - 1: 0},
        scratch_shapes=[
            pltpu.VMEM((2, width, width), BF16),
            pltpu.VMEM((count + (1 if zero else 0), *block), BF16),
            pltpu.SemaphoreType.DMA,
        ],
        mib=10,
        cost_estimate=estimate(cost),
        name=name,
    )
    return token, out


def finish_kernel(scale, keep, got, out):
    out[...] = (keep[...] + got[...].astype(F32)) * scale


def finish(token, scale, keep, got):
    return kernel_call(
        functools.partial(finish_kernel, scale),
        token,
        (keep, got),
        [VMEM] * 2,
        [jax.ShapeDtypeStruct(keep.shape, F32)],
        [VMEM],
        mib=4,
        cost_estimate=estimate(0),
        name="finish",
    )


def body(
    wavefunction, left_operators, right_operators, rotations, charges, present_blocks, directions
):
    sectors, width, _ = wavefunction.shape
    pairs = left_operators.shape[0]
    n = lax.axis_size("op")
    levels = lax.axis_size("sec")
    half = n // 2
    chunk = width // n
    halving = n >= 4 and n & (n - 1) == 0 and chunk % 16 == 0
    rows = sectors * width
    parts = [(0, 3 * sectors // 4), (3 * sectors // 4, sectors)] if sectors > 1 else [(0, 1)]

    def over_op(value, target):
        return lax.ppermute(value, "op", [(i, target(i)) for i in range(n)])

    def swapped(value, start):
        to = list(range(levels))
        for i in range(start, levels - 1, 2):
            to[i], to[i + 1] = i + 1, i
        return lax.ppermute(value, "sec", list(enumerate(to)))

    def side(i):
        return (i + 1) % n if i % 2 else (i - 1) % n

    def end(i):
        return i % half in (0, half - 1)

    def opposite(i):
        return (i + half) % n

    def relay(i):
        return i - i % half + half - 1 - i % half

    small = (directions[:, 0], charges, present_blocks)
    ahead_roles = (("extra", "side"), ("half", "extra"))
    behind_roles = (("side", "extra"), ("extra", "half"))
    core_roles = ("extra", "core")
    lead = min(2, sectors)
    whole = (0, sectors)
    token, (front,) = staged(
        None, ((ahead_roles, (), 0, lead),), half, *small, left_operators
    )
    token, (rear, behind, last, first_core, left, wave, turn) = staged(
        token,
        (
            (ahead_roles, ahead_roles, lead, sectors),
            (behind_roles[:1], behind_roles, *whole),
            (("half",), (), *whole),
            (core_roles, core_roles, *whole),
        ),
        half,
        *small,
        left_operators,
        wavefunction,
        rotations,
    )
    got_front, got_rear = [
        over_op(x, lambda i: opposite(i) if end(i) else side(i)) for x in (front, rear)
    ]
    got_behind = over_op(behind, lambda i: side(i) if end(i) else opposite(i))
    from_core = over_op(first_core, lambda i: i ^ 1)
    token, (*terms, turned) = sigma_terms(
        token, halving, chunk, charges, present_blocks, left, right_operators, wave, turn
    )

    if halving:
        send_edges, send, keep = terms
        got_edges = over_op(send_edges, lambda i: i ^ 1)
        got = over_op(send, lambda i: i ^ 1)
        token, (got_front,) = hold(token, got_front, cost=1.75)
        token, (got,) = hold(token, got)
        token, (first, second) = edges(token, keep, got_edges, turned)
        one, two = swapped(first, 0), swapped(second, 1)
        offset = width // 2
        token, (one,) = hold(token, one, cost=0.6)
        bit = 2
        token, (send, keep) = split(token, bit, chunk, levels, keep, got_edges, got, one, two)
        got = over_op(send, lambda i: i ^ 2)
        token, last = choose(token, half, parts, lead, got_front, got_rear, last)
        while 2 * bit < n:
            bit *= 2
            token, (send, keep) = split(token, bit, chunk, levels, keep, got)
            got = over_op(send, lambda i, bit=bit: i ^ bit)
    else:
        (terms,) = terms
        offset = width
        odd = lax.rem(lax.axis_index("sec"), 2) == 1
        level = lax.axis_index("sec")
        upward = jnp.concatenate([terms[sectors + 1].astype(BF16), turned[sectors - 1]])
        downward = jnp.concatenate([terms[0].astype(BF16), turned[0]])
        one = swapped(jnp.where(odd, downward, upward), 0)
        two = swapped(jnp.where(odd, upward, downward), 1)
        below = jnp.where(odd, one, two)[:width].astype(F32)
        above = jnp.where(odd, two, one)[:width].astype(F32)
        mid = terms[1 : sectors + 1]
        mid = mid.at[0].add(jnp.where(level > 0, below, 0.0))
        mid = mid.at[sectors - 1].add(jnp.where(level < levels - 1, above, 0.0))
        summed = lax.psum_scatter(mid, "op", scatter_dimension=1, tiled=True)
        token, last = choose(token, half, parts, lead, got_front, got_rear, last)

    got_last = [over_op(x, lambda i: relay(i) if end(i) else opposite(i)) for x in last]
    fixed = (offset, levels, half, turned, turn, one, two)
    tail = (sectors - lead) * width
    told = 2 * tail
    token, out = renorm(
        token,
        "renorm_first",
        (
            ((0, 0), (0, 2 * rows, 0), (("core", 1),), *whole),
            ((0, rows), (0, 2 * rows, 1), (("core", 0),), *whole),
            ((1, 0), (2, told, 0), (("half", 1), ("side", 0)), 0, lead),
            ((2, 0), (2, told, 0), (("half", 1), ("side", 0)), lead, sectors),
            ((1, lead * width), (2, told, 1), (("half", 0), ("side", 1)), 0, lead),
            ((2, tail), (2, told, 1), (("half", 0), ("side", 1)), lead, sectors),
            ((3, 0), (3, rows, 0), (("side", 0), ("half", 1)), *whole),
        ),
        (from_core, got_front, got_rear, got_behind),
        None,
        *fixed,
        cost=1.75,
    )
    scale = 1.0 / math.sqrt(pairs * n)
    for i, (begin, stop) in enumerate(parts):
        token, out = renorm(
            token,
            "renorm_last",
            (((0, 0), (1, rows, 1), (("side", 1), ("half", 0)), begin, stop),),
            (got_last[i], got_behind),
            out,
            *fixed,
        )
    if halving:
        token, (sigma_vector,) = finish(token, scale, keep, got)
    else:
        sigma_vector = summed * scale
    return sigma_vector, out


def solution(mesh):
    placed = (
        P("sec", None, None),
        P("op", "sec", None, None),
        P("op", "sec", None, None),
        P("sec", None, None),
        P("op"),
        P("op", "sec"),
        P("op", None),
    )
    return jax.shard_map(
        body,
        mesh=mesh,
        in_specs=placed,
        out_specs=(P("sec", "op", None), P("op", "sec", None, None)),
        check_vma=False,
    )
```

```python
import functools
import math

import jax
import jax.numpy as jnp
from jax import lax
from jax.experimental import pallas as pl
from jax.experimental.pallas import tpu as pltpu
from jax.sharding import PartitionSpec as P

DIRS = 4
CAPS = 2

PEAK = 1_153_500_000

BF16 = jnp.bfloat16
F32 = jnp.float32
ANY = pl.BlockSpec(memory_space=pl.ANY)
HBM = pl.BlockSpec(memory_space=pltpu.HBM)
VMEM = pl.BlockSpec(memory_space=pltpu.VMEM)


def kernel_call(kernel, token, operands, in_specs, out_shape, out_specs, **options):
    mib = options.pop("mib")
    aliases = options.pop("aliases", {})
    grid = options.pop("grid", ())
    ahead = 0 if token is None else 1
    taken = len(operands) + ahead

    def run(*refs):
        refs = list(refs)
        del refs[taken]
        kernel(*refs[ahead:])

    outs = pl.pallas_call(
        run,
        grid=grid,
        out_shape=[jax.ShapeDtypeStruct((8, 128), F32), *out_shape],
        in_specs=[HBM] * ahead + list(in_specs),
        out_specs=[HBM, *out_specs],
        input_output_aliases={i + ahead: o + 1 for i, o in aliases.items()},
        compiler_params=pltpu.CompilerParams(vmem_limit_bytes=mib * 1024 * 1024),
        **options,
    )(*([] if token is None else [token]), *operands)
    return outs[0], list(outs[1:])


def in_hbm(value):
    return pltpu.with_memory_space_constraint(value, pltpu.HBM)


def estimate(microseconds):
    return pl.CostEstimate(flops=int(microseconds * PEAK), bytes_accessed=0, transcendentals=0)


def fetch_scalars(pairs, sem):
    copies = [pltpu.make_async_copy(source, kept, sem) for source, kept in pairs]
    for copy in copies:
        copy.start()
    for copy in copies:
        copy.wait()


def meta_rows(sectors):
    return -(-2 * (2 + sectors) // 16) * 16


def at_end(half):
    place = lax.rem(lax.axis_index("op"), half)
    return jnp.logical_or(place == 0, place == half - 1)


def pick(kinds, places, kind, place):
    index = jnp.int32(0)
    for p, (own, at) in enumerate(zip(kinds, places)):
        match = at == place if kind is None else jnp.logical_and(at == place, own == kind)
        index = index + jnp.where(match, p, 0)
    return index


def copy_pairs(roles, half, outs, left, directions, charges, present, arrived=None):
    count, _, width, _ = left.shape
    sectors = present.shape[1]
    kinds = [directions[p] for p in range(count)]
    places = []
    for p in range(count):
        place = jnp.int32(0)
        for q in range(p):
            place = place + jnp.where(kinds[q] == kinds[p], 1, 0)
        places.append(place)
    odd = lax.rem(lax.axis_index("op"), 2)
    end = at_end(half)
    found = {
        "extra": pick(kinds, places, None, 1),
        "half": pick(kinds, places, 3, 0),
        "core": pick(kinds, places, 1 + odd, 0),
        "side": pick(kinds, places, 2 - odd, 0),
    }

    def index_of(role):
        return found[role] if isinstance(role, str) else jnp.where(end, *map(found.get, role))

    height = meta_rows(sectors)
    row = lax.broadcasted_iota(jnp.int32, (height, width), 0)
    for out, (sent, told, begin, stop) in zip(outs, roles):
        indices = [index_of(role) for role in sent]
        for s in range(begin, stop):
            if arrived is not None:
                arrived(s)
            for i, index in enumerate(indices):
                at = (i * (stop - begin) + s - begin) * width
                out[at : at + width] = left[index, s]
        if not told:
            continue
        values = jnp.zeros((height, width), jnp.int32)
        for i, role in enumerate(told):
            index = index_of(role)
            at = i * (height // 2)
            kind = jnp.int32(0)
            for p in range(count):
                kind = kind + jnp.where(index == p, kinds[p], 0)
            values = jnp.where(row == at, charges[index], jnp.where(row == at + 1, kind, values))
            for s in range(sectors):
                values = jnp.where(row == at + 2 + s, present[index, s], values)
        at = len(sent) * (stop - begin) * width
        out[at : at + height] = values.astype(F32).astype(BF16)


def stage_kernel(roles, half, directions_ref, charges_ref, present_ref, left_ref, *refs):
    *outs, left, directions, charges, present, few, sems = refs
    bulk = [
        pltpu.make_async_copy(left_ref.at[:, s], left.at[:, s], sems.at[s])
        for s in range(left.shape[1])
    ]
    for copy in bulk:
        copy.start()
    fetch_scalars([(directions_ref, directions)], few)
    copy_pairs(
        roles, half, outs, left, directions, charges, present, lambda s: bulk[s].wait()
    )


def restage_kernel(
    roles, half, directions_ref, charges_ref, present_ref, left_ref, wave_ref, rot_ref, *refs
):
    outs = refs[: len(roles)]
    left, wave, rot, directions, charges, present, few, sems = refs[len(roles) :]
    bulk = [
        pltpu.make_async_copy(left_ref, left, sems.at[0]),
        pltpu.make_async_copy(wave_ref, wave, sems.at[1]),
        pltpu.make_async_copy(rot_ref, rot, sems.at[2]),
    ]
    for copy in bulk:
        copy.start()
    fetch_scalars(
        [(directions_ref, directions), (charges_ref, charges), (present_ref, present)], few
    )
    bulk[0].wait()
    copy_pairs(roles, half, outs, left, directions, charges, present)
    for copy in bulk[1:]:
        copy.wait()


def staged(token, roles, half, directions, charges, present, *bulk):
    count, sectors, width, _ = bulk[0].shape
    shapes = [
        (len(sent) * (stop - begin) * width + (meta_rows(sectors) if told else 0), width)
        for sent, told, begin, stop in roles
    ]
    scratch = [
        pltpu.SMEM((count,), jnp.int32),
        pltpu.SMEM((count,), jnp.int32),
        pltpu.SMEM((count, sectors), jnp.int32),
        pltpu.SemaphoreType.DMA,
    ]
    if token is None:
        scratch.insert(0, pltpu.VMEM((count, roles[0][3], width, width), BF16))
        scratch.append(pltpu.SemaphoreType.DMA((roles[0][3],)))
    else:
        shapes += [x.shape for x in bulk]
        scratch.append(pltpu.SemaphoreType.DMA((3,)))
    return kernel_call(
        functools.partial(stage_kernel if token is None else restage_kernel, roles, half),
        token,
        [in_hbm(x) for x in (directions, charges, present, *bulk)],
        [HBM] * (3 + len(bulk)),
        [pltpu.VMEM(shape, BF16) for shape in shapes],
        [VMEM] * len(shapes),
        scratch_shapes=scratch,
        mib=6,
        cost_estimate=estimate(0),
        name="stage" if token is None else "restage",
    )


def grouped_few(sectors):
    return max(0, sectors // 2 - 1)


def grouped(target, sectors):
    few = grouped_few(sectors)
    if target in (0, sectors + 1):
        return 0, min(target, 1)
    return (0, 1 + target) if target <= few else (1, target - 1 - few)


def sigma_kernel(split, chunk, charges_ref, present_ref, left, right_ref, wave, rotations, *refs):
    outs, (acc, right, charges, present, few, sems) = refs[:-6], refs[-6:]
    count, sectors, width, _ = left.shape
    small = [
        pltpu.make_async_copy(charges_ref, charges, few),
        pltpu.make_async_copy(present_ref, present, few),
    ]
    loads = [pltpu.make_async_copy(right_ref.at[p], right.at[p], sems.at[p]) for p in range(count)]
    for copy in small + loads:
        copy.start()
    acc[...] = jnp.zeros_like(acc)
    for s in range(sectors):
        outs[-1][s] = rotations[s].T
    for copy in small:
        copy.wait()

    def step(pair, carry):
        pltpu.make_async_copy(right_ref.at[pair], right.at[pair], sems.at[pair]).wait()
        charge = charges[pair]
        for s in range(sectors):
            halfway = jnp.dot(left[pair, s], wave[s], preferred_element_type=F32)
            halfway = (halfway * present[pair, s].astype(F32)).astype(BF16)
            term = lax.dot_general(
                halfway, right[pair, s], (((1,), (1,)), ((), ())), preferred_element_type=F32
            )
            acc[jnp.clip(s + 1 + charge, 0, sectors + 1)] += term
        return carry

    lax.fori_loop(0, count, step, 0)
    if not split:
        outs[0][...] = acc[...]
        return
    bit = lax.rem(lax.axis_index("op"), 2)
    for q in range(width // chunk // 2):
        to = slice(q * chunk, (q + 1) * chunk)
        for t in range(sectors + 2):
            away = acc[t, pl.ds((2 * q + 1 - bit) * chunk, chunk)].astype(BF16)
            group, place = grouped(t, sectors)
            outs[group][place, to] = away
            outs[2][t, to] = acc[t, pl.ds((2 * q + bit) * chunk, chunk)]


def sigma_terms(token, split, chunk, charges, present, left, right, wave, rotations):
    count, sectors, width, _ = left.shape
    if split:
        few = grouped_few(sectors)
        shapes = [
            ((2 + few, width // 2, width), BF16),
            ((sectors - few, width // 2, width), BF16),
            ((sectors + 2, width // 2, width), F32),
        ]
    else:
        shapes = [((sectors + 2, width, width), F32)]
    shapes.append(((sectors, width, width), BF16))
    return kernel_call(
        functools.partial(sigma_kernel, split, chunk),
        token,
        (in_hbm(charges), in_hbm(present), left, in_hbm(right), wave, rotations),
        [HBM, HBM, VMEM, HBM, VMEM, VMEM],
        [pltpu.VMEM(*shape) for shape in shapes],
        [VMEM] * len(shapes),
        scratch_shapes=[
            pltpu.VMEM((sectors + 2, width, width), F32),
            pltpu.VMEM(right.shape, BF16),
            pltpu.SMEM((count,), jnp.int32),
            pltpu.SMEM((count, sectors), jnp.int32),
            pltpu.SemaphoreType.DMA,
            pltpu.SemaphoreType.DMA((count,)),
        ],
        mib=10,
        cost_estimate=estimate(0),
        name="sigma_terms",
    )


def edges_kernel(keep, got, turned, first, second):
    outer, height, _ = keep.shape
    odd = lax.rem(lax.axis_index("sec"), 2)
    for out, upward in ((first, odd == 0), (second, odd == 1)):
        edge = jnp.where(upward, outer - 1, 0)
        out[:height] = (keep[edge] + got[jnp.where(upward, 1, 0)].astype(F32)).astype(BF16)
        out[height:] = turned[jnp.where(upward, outer - 3, 0)]


def edges(token, keep, got, turned):
    _, height, width = keep.shape
    shape = (height + turned.shape[1], width)
    return kernel_call(
        edges_kernel,
        token,
        (keep, got, turned),
        [VMEM] * 3,
        [jax.ShapeDtypeStruct(shape, BF16)] * 2,
        [VMEM] * 2,
        mib=4,
        cost_estimate=estimate(0),
        name="edges",
    )


def split_kernel(bit, chunk, levels, first, held, *refs):
    if first:
        *core, one, two, send, keep = refs
    else:
        got, send, keep = refs
    sectors, height = send.shape[0], held.shape[1]
    own = lax.rem(lax.axis_index("op") // bit, 2)
    level = lax.axis_index("sec")
    odd = lax.rem(level, 2) == 1

    def total(s, rows):
        if not first:
            return held[s, rows] + got[s, rows].astype(F32)
        group, place = grouped(s + 1, sectors)
        value = held[s + 1, rows] + core[group][place, rows].astype(F32)
        if s == 0:
            below = jnp.where(odd, one[rows], two[rows]).astype(F32)
            value = value + jnp.where(level > 0, below, 0.0)
        if s == sectors - 1:
            above = jnp.where(odd, two[rows], one[rows]).astype(F32)
            value = value + jnp.where(level < levels - 1, above, 0.0)
        return value

    for q in range(height // chunk // 2):
        to = slice(q * chunk, (q + 1) * chunk)
        for s in range(sectors):
            send[s, to] = total(s, pl.ds((2 * q + 1 - own) * chunk, chunk)).astype(BF16)
            keep[s, to] = total(s, pl.ds((2 * q + own) * chunk, chunk))


def split(token, bit, chunk, levels, held, *got):
    first = len(got) > 1
    outer, height, width = held.shape
    sectors = outer - 2 if first else outer
    return kernel_call(
        functools.partial(split_kernel, bit, chunk, levels, first),
        token,
        (held, *got),
        [VMEM] * (1 + len(got)),
        [
            jax.ShapeDtypeStruct((sectors, height // 2, width), BF16),
            jax.ShapeDtypeStruct((sectors, height // 2, width), F32),
        ],
        [VMEM] * 2,
        mib=4,
        cost_estimate=estimate(0 if first else 1.3),
        name="split",
    )


def hold_kernel(*refs):
    pass


def hold(token, *values, cost=0):
    return kernel_call(
        hold_kernel,
        token,
        values,
        [ANY] * len(values),
        [jax.ShapeDtypeStruct(value.shape, value.dtype) for value in values],
        [ANY] * len(values),
        aliases={i: i for i in range(len(values))},
        mib=1,
        cost_estimate=estimate(cost),
        name="hold",
    )


def choose_kernel(half, parts, lead, front, rear, second, *outs):
    end = at_end(half)
    width = second.shape[1]

    @pl.when(end)
    def _():
        for out, (begin, stop) in zip(outs, parts):
            for s in range(begin, stop):
                source, at = (front, s) if s < lead else (rear, s - lead)
                out[(s - begin) * width : (s - begin + 1) * width] = source[
                    at * width : (at + 1) * width
                ]

    @pl.when(jnp.logical_not(end))
    def _():
        for out, (begin, stop) in zip(outs, parts):
            out[...] = second[begin * width : stop * width]


def choose(token, half, parts, lead, front, rear, second):
    width = second.shape[1]
    return kernel_call(
        functools.partial(choose_kernel, half, parts, lead),
        token,
        (front, rear, second),
        [VMEM] * 3,
        [pltpu.VMEM(((stop - begin) * width, width), BF16) for begin, stop in parts],
        [VMEM] * len(parts),
        mib=4,
        cost_estimate=estimate(0.9),
        name="choose",
    )


def frame_kernel(offset, turned, one, two, framed):
    sectors, width, _ = turned.shape
    raised = lax.rem(lax.axis_index("sec"), 2) == 1
    rows = pl.ds(offset, width)

    @pl.when(raised)
    def _():
        framed[0] = one[rows]
        framed[sectors + 1] = two[rows]

    @pl.when(jnp.logical_not(raised))
    def _():
        framed[0] = two[rows]
        framed[sectors + 1] = one[rows]

    for s in range(sectors):
        framed[s + 1] = turned[s]


def frame(token, offset, turned, one, two):
    sectors, width, _ = turned.shape
    return kernel_call(
        functools.partial(frame_kernel, offset),
        token,
        (turned, one, two),
        [VMEM] * 3,
        [pltpu.VMEM((sectors + 2, width, width), BF16)],
        [VMEM],
        mib=4,
        cost_estimate=estimate(0),
        name="frame",
    )


def renorm_kernel(items, zero, levels, half, framed, rotations, *refs):
    buffers = refs[: 1 + max(buffer for came, told, *_ in items for buffer in (came[0], told[0]))]
    rest = refs[len(buffers) + (0 if zero else 1) :]
    out, results, done = rest
    sectors, width, _ = rotations.shape
    odd = lax.rem(lax.axis_index("op"), 2)
    end = at_end(half)
    level = lax.axis_index("sec")
    height = meta_rows(sectors)
    stores = []
    if zero:
        results[len(items)] = jnp.zeros_like(results[len(items)])
        for place in range(CAPS):
            copy = pltpu.make_async_copy(results.at[len(items)], out.at[place], done)
            copy.start()
            stores.append(copy)
    kinds = {"core": 2 - odd, "side": 1 + odd, "half": 3}
    for i, ((buffer, base), (about, top, slot), targets, begin, stop) in enumerate(items):
        values = buffers[about][pl.ds(top, height)].astype(F32)
        values = values[slot * (height // 2) : (slot + 1) * (height // 2)]
        charge = jnp.max(values[:1]).astype(jnp.int32)
        kind, place = (kinds[targets[0][0]], targets[0][1])
        if len(targets) > 1:
            kind = jnp.where(end, kind, kinds[targets[1][0]])
            place = jnp.where(end, place, targets[1][1])
        weights = values[2 : 2 + sectors]
        named = jnp.where(values[1:2] == jnp.asarray(kind).astype(F32), weights, 0.0)
        weights = jnp.where(place == 1, named, weights)
        for s in range(begin, stop):
            at = s + charge
            whole = level * sectors + at
            inside = jnp.logical_and(whole >= 0, whole < levels * sectors)
            weight = jnp.where(inside, weights[s : s + 1], 0.0)
            block = buffers[buffer][pl.ds(base + (s - begin) * width, width)]
            rotated = jnp.dot(block, rotations[s], preferred_element_type=F32).astype(BF16)
            target = framed[jnp.clip(at + 1, 0, sectors + 1)]
            value = jnp.dot(target, rotated, preferred_element_type=F32) * weight
            results[i, s] = value.astype(BF16)
            copy = pltpu.make_async_copy(results.at[i, s], out.at[kind * CAPS + place, s], done)
            copy.start()
            stores.append(copy)
    for copy in stores:
        copy.wait()


def renorm(
    token, name, items, buffers, out, levels, half, framed, rotations, cost=0
):
    sectors, width, _ = rotations.shape
    zero = out is None
    operands = [framed, rotations, *buffers]
    in_specs = [VMEM] * len(operands)
    if not zero:
        operands.append(out)
        in_specs.append(HBM)
    count = len(items)
    block = (sectors, width, width)
    token, (out,) = kernel_call(
        functools.partial(renorm_kernel, items, zero, levels, half),
        token,
        operands,
        in_specs,
        [jax.ShapeDtypeStruct((DIRS * CAPS, *block), BF16)],
        [HBM],
        aliases={} if zero else {len(operands) - 1: 0},
        scratch_shapes=[
            pltpu.VMEM((count + (1 if zero else 0), *block), BF16),
            pltpu.SemaphoreType.DMA,
        ],
        mib=10,
        cost_estimate=estimate(cost),
        name=name,
    )
    return token, out


def finish_kernel(scale, keep, got, out):
    out[...] = (keep[...] + got[...].astype(F32)) * scale


def finish(token, scale, keep, got):
    return kernel_call(
        functools.partial(finish_kernel, scale),
        token,
        (keep, got),
        [VMEM] * 2,
        [jax.ShapeDtypeStruct(keep.shape, F32)],
        [VMEM],
        mib=4,
        cost_estimate=estimate(0),
        name="finish",
    )


def body(
    wavefunction, left_operators, right_operators, rotations, charges, present_blocks, directions
):
    sectors, width, _ = wavefunction.shape
    pairs = left_operators.shape[0]
    n = lax.axis_size("op")
    levels = lax.axis_size("sec")
    half = n // 2
    chunk = width // n
    halving = n >= 4 and n & (n - 1) == 0 and chunk % 16 == 0
    rows = sectors * width
    parts = [(0, 3 * sectors // 4), (3 * sectors // 4, sectors)] if sectors > 1 else [(0, 1)]

    def over_op(value, target):
        return lax.ppermute(value, "op", [(i, target(i)) for i in range(n)])

    def swapped(value, start):
        to = list(range(levels))
        for i in range(start, levels - 1, 2):
            to[i], to[i + 1] = i + 1, i
        return lax.ppermute(value, "sec", list(enumerate(to)))

    def side(i):
        return (i + 1) % n if i % 2 else (i - 1) % n

    def end(i):
        return i % half in (0, half - 1)

    def opposite(i):
        return (i + half) % n

    def relay(i):
        return i - i % half + half - 1 - i % half

    small = (directions[:, 0], charges, present_blocks)
    ahead_roles = (("extra", "side"), ("half", "extra"))
    behind_roles = (("side", "extra"), ("extra", "half"))
    core_roles = ("extra", "core")
    lead = min(2, sectors)
    whole = (0, sectors)
    token, (front,) = staged(
        None, ((ahead_roles, (), 0, lead),), half, *small, left_operators
    )
    token, (rear, behind, last, first_core, left, wave, turn) = staged(
        token,
        (
            (ahead_roles, ahead_roles, lead, sectors),
            (behind_roles[:1], behind_roles, *whole),
            (("half",), (), *whole),
            (core_roles, core_roles, *whole),
        ),
        half,
        *small,
        left_operators,
        wavefunction,
        rotations,
    )
    got_front, got_rear = [
        over_op(x, lambda i: opposite(i) if end(i) else side(i)) for x in (front, rear)
    ]
    got_behind = over_op(behind, lambda i: side(i) if end(i) else opposite(i))
    from_core = over_op(first_core, lambda i: i ^ 1)
    token, (*terms, turned) = sigma_terms(
        token, halving, chunk, charges, present_blocks, left, right_operators, wave, turn
    )

    if halving:
        send_edges, send, keep = terms
        got_edges = over_op(send_edges, lambda i: i ^ 1)
        got = over_op(send, lambda i: i ^ 1)
        token, (got_front,) = hold(token, got_front, cost=1.75)
        token, (got,) = hold(token, got)
        token, (first, second) = edges(token, keep, got_edges, turned)
        one, two = swapped(first, 0), swapped(second, 1)
        offset = width // 2
        token, (one,) = hold(token, one, cost=0.6)
        bit = 2
        token, (send, keep) = split(token, bit, chunk, levels, keep, got_edges, got, one, two)
        got = over_op(send, lambda i: i ^ 2)
        token, (framed,) = frame(token, offset, turned, one, two)
        token, last = choose(token, half, parts, lead, got_front, got_rear, last)
        while 2 * bit < n:
            bit *= 2
            token, (send, keep) = split(token, bit, chunk, levels, keep, got)
            got = over_op(send, lambda i, bit=bit: i ^ bit)
    else:
        (terms,) = terms
        offset = width
        odd = lax.rem(lax.axis_index("sec"), 2) == 1
        level = lax.axis_index("sec")
        upward = jnp.concatenate([terms[sectors + 1].astype(BF16), turned[sectors - 1]])
        downward = jnp.concatenate([terms[0].astype(BF16), turned[0]])
        one = swapped(jnp.where(odd, downward, upward), 0)
        two = swapped(jnp.where(odd, upward, downward), 1)
        below = jnp.where(odd, one, two)[:width].astype(F32)
        above = jnp.where(odd, two, one)[:width].astype(F32)
        mid = terms[1 : sectors + 1]
        mid = mid.at[0].add(jnp.where(level > 0, below, 0.0))
        mid = mid.at[sectors - 1].add(jnp.where(level < levels - 1, above, 0.0))
        summed = lax.psum_scatter(mid, "op", scatter_dimension=1, tiled=True)
        token, (framed,) = frame(token, offset, turned, one, two)
        token, last = choose(token, half, parts, lead, got_front, got_rear, last)

    got_last = [over_op(x, lambda i: relay(i) if end(i) else opposite(i)) for x in last]
    fixed = (levels, half, framed, turn)
    tail = (sectors - lead) * width
    told = 2 * tail
    token, out = renorm(
        token,
        "renorm_first",
        (
            ((0, 0), (0, 2 * rows, 0), (("core", 1),), *whole),
            ((0, rows), (0, 2 * rows, 1), (("core", 0),), *whole),
            ((1, 0), (2, told, 0), (("half", 1), ("side", 0)), 0, lead),
            ((2, 0), (2, told, 0), (("half", 1), ("side", 0)), lead, sectors),
            ((1, lead * width), (2, told, 1), (("half", 0), ("side", 1)), 0, lead),
            ((2, tail), (2, told, 1), (("half", 0), ("side", 1)), lead, sectors),
            ((3, 0), (3, rows, 0), (("side", 0), ("half", 1)), *whole),
        ),
        (from_core, got_front, got_rear, got_behind),
        None,
        *fixed,
        cost=1.75,
    )
    scale = 1.0 / math.sqrt(pairs * n)
    for i, (begin, stop) in enumerate(parts):
        token, out = renorm(
            token,
            "renorm_last",
            (((0, 0), (1, rows, 1), (("side", 1), ("half", 0)), begin, stop),),
            (got_last[i], got_behind),
            out,
            *fixed,
        )
    if halving:
        token, (sigma_vector,) = finish(token, scale, keep, got)
    else:
        sigma_vector = summed * scale
    return sigma_vector, out


def solution(mesh):
    placed = (
        P("sec", None, None),
        P("op", "sec", None, None),
        P("op", "sec", None, None),
        P("sec", None, None),
        P("op"),
        P("op", "sec"),
        P("op", None),
    )
    return jax.shard_map(
        body,
        mesh=mesh,
        in_specs=placed,
        out_specs=(P("sec", "op", None), P("op", "sec", None, None)),
        check_vma=False,
    )
```

```python
import functools
import math

import jax
import jax.numpy as jnp
from jax import lax
from jax.experimental import pallas as pl
from jax.experimental.pallas import tpu as pltpu
from jax.sharding import PartitionSpec as P

DIRS = 4
CAPS = 2

PEAK = 1_153_500_000

BF16 = jnp.bfloat16
F32 = jnp.float32
ANY = pl.BlockSpec(memory_space=pl.ANY)
HBM = pl.BlockSpec(memory_space=pltpu.HBM)
VMEM = pl.BlockSpec(memory_space=pltpu.VMEM)


def kernel_call(kernel, token, operands, in_specs, out_shape, out_specs, **options):
    mib = options.pop("mib")
    aliases = options.pop("aliases", {})
    grid = options.pop("grid", ())
    ahead = 0 if token is None else 1
    taken = len(operands) + ahead

    def run(*refs):
        refs = list(refs)
        del refs[taken]
        kernel(*refs[ahead:])

    outs = pl.pallas_call(
        run,
        grid=grid,
        out_shape=[jax.ShapeDtypeStruct((8, 128), F32), *out_shape],
        in_specs=[HBM] * ahead + list(in_specs),
        out_specs=[HBM, *out_specs],
        input_output_aliases={i + ahead: o + 1 for i, o in aliases.items()},
        compiler_params=pltpu.CompilerParams(vmem_limit_bytes=mib * 1024 * 1024),
        **options,
    )(*([] if token is None else [token]), *operands)
    return outs[0], list(outs[1:])


def in_hbm(value):
    return pltpu.with_memory_space_constraint(value, pltpu.HBM)


def estimate(microseconds):
    return pl.CostEstimate(flops=int(microseconds * PEAK), bytes_accessed=0, transcendentals=0)


def fetch_scalars(pairs, sem):
    copies = [pltpu.make_async_copy(source, kept, sem) for source, kept in pairs]
    for copy in copies:
        copy.start()
    for copy in copies:
        copy.wait()


def meta_rows(sectors):
    return -(-2 * (2 + sectors) // 16) * 16


def at_end(half):
    place = lax.rem(lax.axis_index("op"), half)
    return jnp.logical_or(place == 0, place == half - 1)


def pick(kinds, places, kind, place):
    index = jnp.int32(0)
    for p, (own, at) in enumerate(zip(kinds, places)):
        match = at == place if kind is None else jnp.logical_and(at == place, own == kind)
        index = index + jnp.where(match, p, 0)
    return index


def copy_pairs(roles, half, outs, left, directions, charges, present, arrived=None):
    count, _, width, _ = left.shape
    sectors = present.shape[1]
    kinds = [directions[p] for p in range(count)]
    places = []
    for p in range(count):
        place = jnp.int32(0)
        for q in range(p):
            place = place + jnp.where(kinds[q] == kinds[p], 1, 0)
        places.append(place)
    odd = lax.rem(lax.axis_index("op"), 2)
    end = at_end(half)
    found = {
        "extra": pick(kinds, places, None, 1),
        "half": pick(kinds, places, 3, 0),
        "core": pick(kinds, places, 1 + odd, 0),
        "side": pick(kinds, places, 2 - odd, 0),
    }

    def index_of(role):
        return found[role] if isinstance(role, str) else jnp.where(end, *map(found.get, role))

    height = meta_rows(sectors)
    row = lax.broadcasted_iota(jnp.int32, (height, width), 0)
    for out, (sent, told, begin, stop) in zip(outs, roles):
        indices = [index_of(role) for role in sent]
        for s in range(begin, stop):
            if arrived is not None:
                arrived(s)
            for i, index in enumerate(indices):
                at = (i * (stop - begin) + s - begin) * width
                out[at : at + width] = left[index, s]
        if not told:
            continue
        values = jnp.zeros((height, width), jnp.int32)
        for i, role in enumerate(told):
            index = index_of(role)
            at = i * (height // 2)
            kind = jnp.int32(0)
            for p in range(count):
                kind = kind + jnp.where(index == p, kinds[p], 0)
            values = jnp.where(row == at, charges[index], jnp.where(row == at + 1, kind, values))
            for s in range(sectors):
                values = jnp.where(row == at + 2 + s, present[index, s], values)
        at = len(sent) * (stop - begin) * width
        out[at : at + height] = values.astype(F32).astype(BF16)


def stage_kernel(roles, half, directions_ref, charges_ref, present_ref, left_ref, *refs):
    *outs, left, directions, charges, present, few, sems = refs
    bulk = [
        pltpu.make_async_copy(left_ref.at[:, s], left.at[:, s], sems.at[s])
        for s in range(left.shape[1])
    ]
    for copy in bulk:
        copy.start()
    fetch_scalars([(directions_ref, directions)], few)
    copy_pairs(
        roles, half, outs, left, directions, charges, present, lambda s: bulk[s].wait()
    )


def restage_kernel(
    roles, half, directions_ref, charges_ref, present_ref, left_ref, wave_ref, rot_ref, had, *refs
):
    outs = refs[: len(roles)]
    left, wave, rot, directions, charges, present, few, sems = refs[len(roles) :]
    count, lead = had.shape[:2]
    rest = pl.ds(lead, left.shape[1] - lead)
    bulk = [
        pltpu.make_async_copy(left_ref.at[:, rest], left.at[:, rest], sems.at[0]),
        pltpu.make_async_copy(wave_ref, wave, sems.at[1]),
        pltpu.make_async_copy(rot_ref, rot, sems.at[2]),
    ]
    for copy in bulk:
        copy.start()
    fetch_scalars(
        [(directions_ref, directions), (charges_ref, charges), (present_ref, present)], few
    )
    for p in range(count):
        for s in range(lead):
            left[p, s] = had[p, s]
    bulk[0].wait()
    copy_pairs(roles, half, outs, left, directions, charges, present)
    for copy in bulk[1:]:
        copy.wait()


def staged(token, roles, half, directions, charges, present, *bulk, had=()):
    count, sectors, width, _ = bulk[0].shape
    shapes = [
        (len(sent) * (stop - begin) * width + (meta_rows(sectors) if told else 0), width)
        for sent, told, begin, stop in roles
    ]
    scratch = [
        pltpu.SMEM((count,), jnp.int32),
        pltpu.SMEM((count,), jnp.int32),
        pltpu.SMEM((count, sectors), jnp.int32),
        pltpu.SemaphoreType.DMA,
    ]
    if token is None:
        shapes.append((count, roles[0][3], width, width))
        scratch.append(pltpu.SemaphoreType.DMA((roles[0][3],)))
    else:
        shapes += [x.shape for x in bulk]
        scratch.append(pltpu.SemaphoreType.DMA((3,)))
    return kernel_call(
        functools.partial(stage_kernel if token is None else restage_kernel, roles, half),
        token,
        [in_hbm(x) for x in (directions, charges, present, *bulk)] + list(had),
        [HBM] * (3 + len(bulk)) + [VMEM] * len(had),
        [pltpu.VMEM(shape, BF16) for shape in shapes],
        [VMEM] * len(shapes),
        scratch_shapes=scratch,
        mib=6,
        cost_estimate=estimate(0),
        name="stage" if token is None else "restage",
    )


def grouped_few(sectors):
    return max(0, sectors // 2 - 1)


def grouped(target, sectors):
    few = grouped_few(sectors)
    if target in (0, sectors + 1):
        return 0, min(target, 1)
    return (0, 1 + target) if target <= few else (1, target - 1 - few)


def sigma_kernel(split, chunk, charges_ref, present_ref, left, right_ref, wave, rotations, *refs):
    outs, (acc, right, charges, present, few, sems) = refs[:-6], refs[-6:]
    count, sectors, width, _ = left.shape
    small = [
        pltpu.make_async_copy(charges_ref, charges, few),
        pltpu.make_async_copy(present_ref, present, few),
    ]
    loads = [pltpu.make_async_copy(right_ref.at[p], right.at[p], sems.at[p]) for p in range(count)]
    for copy in small + loads:
        copy.start()
    acc[...] = jnp.zeros_like(acc)
    for s in range(sectors):
        outs[-1][s] = rotations[s].T
    for copy in small:
        copy.wait()

    def step(pair, carry):
        pltpu.make_async_copy(right_ref.at[pair], right.at[pair], sems.at[pair]).wait()
        charge = charges[pair]
        for s in range(sectors):
            halfway = jnp.dot(left[pair, s], wave[s], preferred_element_type=F32)
            halfway = (halfway * present[pair, s].astype(F32)).astype(BF16)
            term = lax.dot_general(
                halfway, right[pair, s], (((1,), (1,)), ((), ())), preferred_element_type=F32
            )
            acc[jnp.clip(s + 1 + charge, 0, sectors + 1)] += term
        return carry

    lax.fori_loop(0, count, step, 0)
    if not split:
        outs[0][...] = acc[...]
        return
    bit = lax.rem(lax.axis_index("op"), 2)
    for q in range(width // chunk // 2):
        to = slice(q * chunk, (q + 1) * chunk)
        for t in range(sectors + 2):
            away = acc[t, pl.ds((2 * q + 1 - bit) * chunk, chunk)].astype(BF16)
            group, place = grouped(t, sectors)
            outs[group][place, to] = away
            outs[2][t, to] = acc[t, pl.ds((2 * q + bit) * chunk, chunk)]


def sigma_terms(token, split, chunk, charges, present, left, right, wave, rotations):
    count, sectors, width, _ = left.shape
    if split:
        few = grouped_few(sectors)
        shapes = [
            ((2 + few, width // 2, width), BF16),
            ((sectors - few, width // 2, width), BF16),
            ((sectors + 2, width // 2, width), F32),
        ]
    else:
        shapes = [((sectors + 2, width, width), F32)]
    shapes.append(((sectors, width, width), BF16))
    return kernel_call(
        functools.partial(sigma_kernel, split, chunk),
        token,
        (in_hbm(charges), in_hbm(present), left, in_hbm(right), wave, rotations),
        [HBM, HBM, VMEM, HBM, VMEM, VMEM],
        [pltpu.VMEM(*shape) for shape in shapes],
        [VMEM] * len(shapes),
        scratch_shapes=[
            pltpu.VMEM((sectors + 2, width, width), F32),
            pltpu.VMEM(right.shape, BF16),
            pltpu.SMEM((count,), jnp.int32),
            pltpu.SMEM((count, sectors), jnp.int32),
            pltpu.SemaphoreType.DMA,
            pltpu.SemaphoreType.DMA((count,)),
        ],
        mib=10,
        cost_estimate=estimate(0),
        name="sigma_terms",
    )


def edges_kernel(keep, got, turned, first, second):
    outer, height, _ = keep.shape
    odd = lax.rem(lax.axis_index("sec"), 2)
    for out, upward in ((first, odd == 0), (second, odd == 1)):
        edge = jnp.where(upward, outer - 1, 0)
        out[:height] = (keep[edge] + got[jnp.where(upward, 1, 0)].astype(F32)).astype(BF16)
        out[height:] = turned[jnp.where(upward, outer - 3, 0)]


def edges(token, keep, got, turned):
    _, height, width = keep.shape
    shape = (height + turned.shape[1], width)
    return kernel_call(
        edges_kernel,
        token,
        (keep, got, turned),
        [VMEM] * 3,
        [jax.ShapeDtypeStruct(shape, BF16)] * 2,
        [VMEM] * 2,
        mib=4,
        cost_estimate=estimate(0),
        name="edges",
    )


def split_kernel(bit, chunk, levels, first, held, *refs):
    if first:
        *core, one, two, send, keep = refs
    else:
        got, send, keep = refs
    sectors, height = send.shape[0], held.shape[1]
    own = lax.rem(lax.axis_index("op") // bit, 2)
    level = lax.axis_index("sec")
    odd = lax.rem(level, 2) == 1

    def total(s, rows):
        if not first:
            return held[s, rows] + got[s, rows].astype(F32)
        group, place = grouped(s + 1, sectors)
        value = held[s + 1, rows] + core[group][place, rows].astype(F32)
        if s == 0:
            below = jnp.where(odd, one[rows], two[rows]).astype(F32)
            value = value + jnp.where(level > 0, below, 0.0)
        if s == sectors - 1:
            above = jnp.where(odd, two[rows], one[rows]).astype(F32)
            value = value + jnp.where(level < levels - 1, above, 0.0)
        return value

    for q in range(height // chunk // 2):
        to = slice(q * chunk, (q + 1) * chunk)
        for s in range(sectors):
            send[s, to] = total(s, pl.ds((2 * q + 1 - own) * chunk, chunk)).astype(BF16)
            keep[s, to] = total(s, pl.ds((2 * q + own) * chunk, chunk))


def split(token, bit, chunk, levels, held, *got):
    first = len(got) > 1
    outer, height, width = held.shape
    sectors = outer - 2 if first else outer
    return kernel_call(
        functools.partial(split_kernel, bit, chunk, levels, first),
        token,
        (held, *got),
        [VMEM] * (1 + len(got)),
        [
            jax.ShapeDtypeStruct((sectors, height // 2, width), BF16),
            jax.ShapeDtypeStruct((sectors, height // 2, width), F32),
        ],
        [VMEM] * 2,
        mib=4,
        cost_estimate=estimate(0 if first else 1.3),
        name="split",
    )


def hold_kernel(*refs):
    pass


def hold(token, *values, cost=0):
    return kernel_call(
        hold_kernel,
        token,
        values,
        [ANY] * len(values),
        [jax.ShapeDtypeStruct(value.shape, value.dtype) for value in values],
        [ANY] * len(values),
        aliases={i: i for i in range(len(values))},
        mib=1,
        cost_estimate=estimate(cost),
        name="hold",
    )


def choose_kernel(half, parts, lead, front, rear, second, *outs):
    end = at_end(half)
    width = second.shape[1]

    @pl.when(end)
    def _():
        for out, (begin, stop) in zip(outs, parts):
            for s in range(begin, stop):
                source, at = (front, s) if s < lead else (rear, s - lead)
                out[(s - begin) * width : (s - begin + 1) * width] = source[
                    at * width : (at + 1) * width
                ]

    @pl.when(jnp.logical_not(end))
    def _():
        for out, (begin, stop) in zip(outs, parts):
            out[...] = second[begin * width : stop * width]


def choose(token, half, parts, lead, front, rear, second):
    width = second.shape[1]
    return kernel_call(
        functools.partial(choose_kernel, half, parts, lead),
        token,
        (front, rear, second),
        [VMEM] * 3,
        [pltpu.VMEM(((stop - begin) * width, width), BF16) for begin, stop in parts],
        [VMEM] * len(parts),
        mib=4,
        cost_estimate=estimate(0.9),
        name="choose",
    )


def frame_kernel(offset, turned, one, two, framed):
    sectors, width, _ = turned.shape
    raised = lax.rem(lax.axis_index("sec"), 2) == 1
    rows = pl.ds(offset, width)

    @pl.when(raised)
    def _():
        framed[0] = one[rows]
        framed[sectors + 1] = two[rows]

    @pl.when(jnp.logical_not(raised))
    def _():
        framed[0] = two[rows]
        framed[sectors + 1] = one[rows]

    for s in range(sectors):
        framed[s + 1] = turned[s]


def frame(token, offset, turned, one, two):
    sectors, width, _ = turned.shape
    return kernel_call(
        functools.partial(frame_kernel, offset),
        token,
        (turned, one, two),
        [VMEM] * 3,
        [pltpu.VMEM((sectors + 2, width, width), BF16)],
        [VMEM],
        mib=4,
        cost_estimate=estimate(0),
        name="frame",
    )


def renorm_kernel(items, zero, levels, half, framed, rotations, *refs):
    buffers = refs[: 1 + max(buffer for came, told, *_ in items for buffer in (came[0], told[0]))]
    rest = refs[len(buffers) + (0 if zero else 1) :]
    out, results, done = rest
    sectors, width, _ = rotations.shape
    odd = lax.rem(lax.axis_index("op"), 2)
    end = at_end(half)
    level = lax.axis_index("sec")
    height = meta_rows(sectors)
    stores = []
    if zero:
        results[len(items)] = jnp.zeros_like(results[len(items)])
        for place in range(CAPS):
            copy = pltpu.make_async_copy(results.at[len(items)], out.at[place], done)
            copy.start()
            stores.append(copy)
    kinds = {"core": 2 - odd, "side": 1 + odd, "half": 3}
    for i, ((buffer, base), (about, top, slot), targets, begin, stop) in enumerate(items):
        values = buffers[about][pl.ds(top, height)].astype(F32)
        values = values[slot * (height // 2) : (slot + 1) * (height // 2)]
        charge = jnp.max(values[:1]).astype(jnp.int32)
        kind, place = (kinds[targets[0][0]], targets[0][1])
        if len(targets) > 1:
            kind = jnp.where(end, kind, kinds[targets[1][0]])
            place = jnp.where(end, place, targets[1][1])
        weights = values[2 : 2 + sectors]
        named = jnp.where(values[1:2] == jnp.asarray(kind).astype(F32), weights, 0.0)
        weights = jnp.where(place == 1, named, weights)
        for s in range(begin, stop):
            at = s + charge
            whole = level * sectors + at
            inside = jnp.logical_and(whole >= 0, whole < levels * sectors)
            weight = jnp.where(inside, weights[s : s + 1], 0.0)
            block = buffers[buffer][pl.ds(base + (s - begin) * width, width)]
            rotated = jnp.dot(block, rotations[s], preferred_element_type=F32).astype(BF16)
            target = framed[jnp.clip(at + 1, 0, sectors + 1)]
            value = jnp.dot(target, rotated, preferred_element_type=F32) * weight
            results[i, s] = value.astype(BF16)
            copy = pltpu.make_async_copy(results.at[i, s], out.at[kind * CAPS + place, s], done)
            copy.start()
            stores.append(copy)
    for copy in stores:
        copy.wait()


def renorm(
    token, name, items, buffers, out, levels, half, framed, rotations, cost=0
):
    sectors, width, _ = rotations.shape
    zero = out is None
    operands = [framed, rotations, *buffers]
    in_specs = [VMEM] * len(operands)
    if not zero:
        operands.append(out)
        in_specs.append(HBM)
    count = len(items)
    block = (sectors, width, width)
    token, (out,) = kernel_call(
        functools.partial(renorm_kernel, items, zero, levels, half),
        token,
        operands,
        in_specs,
        [jax.ShapeDtypeStruct((DIRS * CAPS, *block), BF16)],
        [HBM],
        aliases={} if zero else {len(operands) - 1: 0},
        scratch_shapes=[
            pltpu.VMEM((count + (1 if zero else 0), *block), BF16),
            pltpu.SemaphoreType.DMA,
        ],
        mib=10,
        cost_estimate=estimate(cost),
        name=name,
    )
    return token, out


def finish_kernel(scale, keep, got, out):
    out[...] = (keep[...] + got[...].astype(F32)) * scale


def finish(token, scale, keep, got):
    return kernel_call(
        functools.partial(finish_kernel, scale),
        token,
        (keep, got),
        [VMEM] * 2,
        [jax.ShapeDtypeStruct(keep.shape, F32)],
        [VMEM],
        mib=4,
        cost_estimate=estimate(0),
        name="finish",
    )


def body(
    wavefunction, left_operators, right_operators, rotations, charges, present_blocks, directions
):
    sectors, width, _ = wavefunction.shape
    pairs = left_operators.shape[0]
    n = lax.axis_size("op")
    levels = lax.axis_size("sec")
    half = n // 2
    chunk = width // n
    halving = n >= 4 and n & (n - 1) == 0 and chunk % 16 == 0
    rows = sectors * width
    parts = [(0, 3 * sectors // 4), (3 * sectors // 4, sectors)] if sectors > 1 else [(0, 1)]

    def over_op(value, target):
        return lax.ppermute(value, "op", [(i, target(i)) for i in range(n)])

    def swapped(value, start):
        to = list(range(levels))
        for i in range(start, levels - 1, 2):
            to[i], to[i + 1] = i + 1, i
        return lax.ppermute(value, "sec", list(enumerate(to)))

    def side(i):
        return (i + 1) % n if i % 2 else (i - 1) % n

    def end(i):
        return i % half in (0, half - 1)

    def opposite(i):
        return (i + half) % n

    def relay(i):
        return i - i % half + half - 1 - i % half

    small = (directions[:, 0], charges, present_blocks)
    ahead_roles = (("extra", "side"), ("half", "extra"))
    behind_roles = (("side", "extra"), ("extra", "half"))
    core_roles = ("extra", "core")
    lead = min(2, sectors)
    whole = (0, sectors)
    token, (front, had) = staged(
        None, ((ahead_roles, (), 0, lead),), half, *small, left_operators
    )
    token, (rear, behind, last, first_core, left, wave, turn) = staged(
        token,
        (
            (ahead_roles, ahead_roles, lead, sectors),
            (behind_roles[:1], behind_roles, *whole),
            (("half",), (), *whole),
            (core_roles, core_roles, *whole),
        ),
        half,
        *small,
        left_operators,
        wavefunction,
        rotations,
        had=(had,),
    )
    got_front, got_rear = [
        over_op(x, lambda i: opposite(i) if end(i) else side(i)) for x in (front, rear)
    ]
    got_behind = over_op(behind, lambda i: side(i) if end(i) else opposite(i))
    from_core = over_op(first_core, lambda i: i ^ 1)
    token, (*terms, turned) = sigma_terms(
        token, halving, chunk, charges, present_blocks, left, right_operators, wave, turn
    )

    if halving:
        send_edges, send, keep = terms
        got_edges = over_op(send_edges, lambda i: i ^ 1)
        got = over_op(send, lambda i: i ^ 1)
        token, (got_front,) = hold(token, got_front, cost=1.75)
        token, (got,) = hold(token, got)
        token, (first, second) = edges(token, keep, got_edges, turned)
        one, two = swapped(first, 0), swapped(second, 1)
        offset = width // 2
        token, (one,) = hold(token, one, cost=0.6)
        bit = 2
        token, (send, keep) = split(token, bit, chunk, levels, keep, got_edges, got, one, two)
        got = over_op(send, lambda i: i ^ 2)
        token, (framed,) = frame(token, offset, turned, one, two)
        token, last = choose(token, half, parts, lead, got_front, got_rear, last)
        while 2 * bit < n:
            bit *= 2
            token, (send, keep) = split(token, bit, chunk, levels, keep, got)
            got = over_op(send, lambda i, bit=bit: i ^ bit)
    else:
        (terms,) = terms
        offset = width
        odd = lax.rem(lax.axis_index("sec"), 2) == 1
        level = lax.axis_index("sec")
        upward = jnp.concatenate([terms[sectors + 1].astype(BF16), turned[sectors - 1]])
        downward = jnp.concatenate([terms[0].astype(BF16), turned[0]])
        one = swapped(jnp.where(odd, downward, upward), 0)
        two = swapped(jnp.where(odd, upward, downward), 1)
        below = jnp.where(odd, one, two)[:width].astype(F32)
        above = jnp.where(odd, two, one)[:width].astype(F32)
        mid = terms[1 : sectors + 1]
        mid = mid.at[0].add(jnp.where(level > 0, below, 0.0))
        mid = mid.at[sectors - 1].add(jnp.where(level < levels - 1, above, 0.0))
        summed = lax.psum_scatter(mid, "op", scatter_dimension=1, tiled=True)
        token, (framed,) = frame(token, offset, turned, one, two)
        token, last = choose(token, half, parts, lead, got_front, got_rear, last)

    got_last = [over_op(x, lambda i: relay(i) if end(i) else opposite(i)) for x in last]
    fixed = (levels, half, framed, turn)
    tail = (sectors - lead) * width
    told = 2 * tail
    token, out = renorm(
        token,
        "renorm_first",
        (
            ((0, 0), (0, 2 * rows, 0), (("core", 1),), *whole),
            ((0, rows), (0, 2 * rows, 1), (("core", 0),), *whole),
            ((1, 0), (2, told, 0), (("half", 1), ("side", 0)), 0, lead),
            ((2, 0), (2, told, 0), (("half", 1), ("side", 0)), lead, sectors),
            ((1, lead * width), (2, told, 1), (("half", 0), ("side", 1)), 0, lead),
            ((2, tail), (2, told, 1), (("half", 0), ("side", 1)), lead, sectors),
            ((3, 0), (3, rows, 0), (("side", 0), ("half", 1)), *whole),
        ),
        (from_core, got_front, got_rear, got_behind),
        None,
        *fixed,
        cost=1.75,
    )
    scale = 1.0 / math.sqrt(pairs * n)
    for i, (begin, stop) in enumerate(parts):
        token, out = renorm(
            token,
            "renorm_last",
            (((0, 0), (1, rows, 1), (("side", 1), ("half", 0)), begin, stop),),
            (got_last[i], got_behind),
            out,
            *fixed,
        )
    if halving:
        token, (sigma_vector,) = finish(token, scale, keep, got)
    else:
        sigma_vector = summed * scale
    return sigma_vector, out


def solution(mesh):
    placed = (
        P("sec", None, None),
        P("op", "sec", None, None),
        P("op", "sec", None, None),
        P("sec", None, None),
        P("op"),
        P("op", "sec"),
        P("op", None),
    )
    return jax.shard_map(
        body,
        mesh=mesh,
        in_specs=placed,
        out_specs=(P("sec", "op", None), P("op", "sec", None, None)),
        check_vma=False,
    )
```

```python
import functools
import math

import jax
import jax.numpy as jnp
from jax import lax
from jax.experimental import pallas as pl
from jax.experimental.pallas import tpu as pltpu
from jax.sharding import PartitionSpec as P

DIRS = 4
CAPS = 2

PEAK = 1_153_500_000

BF16 = jnp.bfloat16
F32 = jnp.float32
ANY = pl.BlockSpec(memory_space=pl.ANY)
HBM = pl.BlockSpec(memory_space=pltpu.HBM)
VMEM = pl.BlockSpec(memory_space=pltpu.VMEM)


def kernel_call(kernel, token, operands, in_specs, out_shape, out_specs, **options):
    mib = options.pop("mib")
    aliases = options.pop("aliases", {})
    grid = options.pop("grid", ())
    ahead = 0 if token is None else 1
    taken = len(operands) + ahead

    def run(*refs):
        refs = list(refs)
        del refs[taken]
        kernel(*refs[ahead:])

    outs = pl.pallas_call(
        run,
        grid=grid,
        out_shape=[jax.ShapeDtypeStruct((8, 128), F32), *out_shape],
        in_specs=[HBM] * ahead + list(in_specs),
        out_specs=[HBM, *out_specs],
        input_output_aliases={i + ahead: o + 1 for i, o in aliases.items()},
        compiler_params=pltpu.CompilerParams(vmem_limit_bytes=mib * 1024 * 1024),
        **options,
    )(*([] if token is None else [token]), *operands)
    return outs[0], list(outs[1:])


def in_hbm(value):
    return pltpu.with_memory_space_constraint(value, pltpu.HBM)


def estimate(microseconds):
    return pl.CostEstimate(flops=int(microseconds * PEAK), bytes_accessed=0, transcendentals=0)


def fetch_scalars(pairs, sem):
    copies = [pltpu.make_async_copy(source, kept, sem) for source, kept in pairs]
    for copy in copies:
        copy.start()
    for copy in copies:
        copy.wait()


def meta_rows(sectors):
    return -(-2 * (2 + sectors) // 16) * 16


def at_end(half):
    place = lax.rem(lax.axis_index("op"), half)
    return jnp.logical_or(place == 0, place == half - 1)


def pick(kinds, places, kind, place):
    index = jnp.int32(0)
    for p, (own, at) in enumerate(zip(kinds, places)):
        match = at == place if kind is None else jnp.logical_and(at == place, own == kind)
        index = index + jnp.where(match, p, 0)
    return index


def copy_pairs(roles, half, outs, left, directions, charges, present, arrived=None):
    count, _, width, _ = left.shape
    sectors = present.shape[1]
    kinds = [directions[p] for p in range(count)]
    places = []
    for p in range(count):
        place = jnp.int32(0)
        for q in range(p):
            place = place + jnp.where(kinds[q] == kinds[p], 1, 0)
        places.append(place)
    odd = lax.rem(lax.axis_index("op"), 2)
    end = at_end(half)
    found = {
        "extra": pick(kinds, places, None, 1),
        "half": pick(kinds, places, 3, 0),
        "core": pick(kinds, places, 1 + odd, 0),
        "side": pick(kinds, places, 2 - odd, 0),
    }

    def index_of(role):
        return found[role] if isinstance(role, str) else jnp.where(end, *map(found.get, role))

    height = meta_rows(sectors)
    row = lax.broadcasted_iota(jnp.int32, (height, width), 0)
    for out, (sent, told, begin, stop) in zip(outs, roles):
        indices = [index_of(role) for role in sent]
        for s in range(begin, stop):
            if arrived is not None:
                arrived(s)
            for i, index in enumerate(indices):
                at = (i * (stop - begin) + s - begin) * width
                out[at : at + width] = left[index, s]
        if not told:
            continue
        values = jnp.zeros((height, width), jnp.int32)
        for i, role in enumerate(told):
            index = index_of(role)
            at = i * (height // 2)
            kind = jnp.int32(0)
            for p in range(count):
                kind = kind + jnp.where(index == p, kinds[p], 0)
            values = jnp.where(row == at, charges[index], jnp.where(row == at + 1, kind, values))
            for s in range(sectors):
                values = jnp.where(row == at + 2 + s, present[index, s], values)
        at = len(sent) * (stop - begin) * width
        out[at : at + height] = values.astype(F32).astype(BF16)


def stage_kernel(roles, half, directions_ref, charges_ref, present_ref, left_ref, *refs):
    *outs, left, directions, charges, present, few, sems = refs
    bulk = [
        pltpu.make_async_copy(left_ref.at[:, s], left.at[:, s], sems.at[s])
        for s in range(left.shape[1])
    ]
    for copy in bulk:
        copy.start()
    fetch_scalars([(directions_ref, directions)], few)
    copy_pairs(
        roles, half, outs, left, directions, charges, present, lambda s: bulk[s].wait()
    )


def restage_kernel(
    roles, half, directions_ref, charges_ref, present_ref, left_ref, wave_ref, rot_ref, had, *refs
):
    outs = refs[: len(roles)]
    left, wave, rot, directions, charges, present, few, sems = refs[len(roles) :]
    count, lead = had.shape[:2]
    rest = pl.ds(lead, left.shape[1] - lead)
    bulk = [
        pltpu.make_async_copy(left_ref.at[:, rest], left.at[:, rest], sems.at[0]),
        pltpu.make_async_copy(wave_ref, wave, sems.at[1]),
        pltpu.make_async_copy(rot_ref, rot, sems.at[2]),
    ]
    for copy in bulk:
        copy.start()
    fetch_scalars(
        [(directions_ref, directions), (charges_ref, charges), (present_ref, present)], few
    )
    for p in range(count):
        for s in range(lead):
            left[p, s] = had[p, s]
    bulk[0].wait()
    copy_pairs(roles, half, outs, left, directions, charges, present)
    for copy in bulk[1:]:
        copy.wait()


def staged(token, roles, half, directions, charges, present, *bulk, had=()):
    count, sectors, width, _ = bulk[0].shape
    shapes = [
        (len(sent) * (stop - begin) * width + (meta_rows(sectors) if told else 0), width)
        for sent, told, begin, stop in roles
    ]
    scratch = [
        pltpu.SMEM((count,), jnp.int32),
        pltpu.SMEM((count,), jnp.int32),
        pltpu.SMEM((count, sectors), jnp.int32),
        pltpu.SemaphoreType.DMA,
    ]
    if token is None:
        shapes.append((count, roles[0][3], width, width))
        scratch.append(pltpu.SemaphoreType.DMA((roles[0][3],)))
    else:
        shapes += [x.shape for x in bulk]
        scratch.append(pltpu.SemaphoreType.DMA((3,)))
    return kernel_call(
        functools.partial(stage_kernel if token is None else restage_kernel, roles, half),
        token,
        [in_hbm(x) for x in (directions, charges, present, *bulk)] + list(had),
        [HBM] * (3 + len(bulk)) + [VMEM] * len(had),
        [pltpu.VMEM(shape, BF16) for shape in shapes],
        [VMEM] * len(shapes),
        scratch_shapes=scratch,
        mib=6,
        cost_estimate=estimate(0),
        name="stage" if token is None else "restage",
    )


def grouped_few(sectors):
    return max(0, sectors // 2 - 1)


def grouped(target, sectors):
    few = grouped_few(sectors)
    if target in (0, sectors + 1):
        return 0, min(target, 1)
    return (0, 1 + target) if target <= few else (1, target - 1 - few)


def sigma_kernel(split, chunk, charges_ref, present_ref, left, right_ref, wave, rotations, *refs):
    outs, (acc, right, charges, present, few, sems) = refs[:-6], refs[-6:]
    count, sectors, width, _ = left.shape
    small = [
        pltpu.make_async_copy(charges_ref, charges, few),
        pltpu.make_async_copy(present_ref, present, few),
    ]
    loads = [pltpu.make_async_copy(right_ref.at[p], right.at[p], sems.at[p]) for p in range(count)]
    for copy in small + loads:
        copy.start()
    acc[...] = jnp.zeros_like(acc)
    for s in range(sectors):
        outs[-1][s] = rotations[s].T
    for copy in small:
        copy.wait()

    def step(pair, carry):
        pltpu.make_async_copy(right_ref.at[pair], right.at[pair], sems.at[pair]).wait()
        charge = charges[pair]
        for s in range(sectors):
            halfway = jnp.dot(left[pair, s], wave[s], preferred_element_type=F32)
            halfway = (halfway * present[pair, s].astype(F32)).astype(BF16)
            term = lax.dot_general(
                halfway, right[pair, s], (((1,), (1,)), ((), ())), preferred_element_type=F32
            )
            acc[jnp.clip(s + 1 + charge, 0, sectors + 1)] += term
        return carry

    lax.fori_loop(0, count, step, 0)
    if not split:
        outs[0][...] = acc[...]
        return
    bit = lax.rem(lax.axis_index("op"), 2)
    for q in range(width // chunk // 2):
        to = slice(q * chunk, (q + 1) * chunk)
        for t in range(sectors + 2):
            away = acc[t, pl.ds((2 * q + 1 - bit) * chunk, chunk)].astype(BF16)
            group, place = grouped(t, sectors)
            outs[group][place, to] = away
            outs[2][t, to] = acc[t, pl.ds((2 * q + bit) * chunk, chunk)]


def sigma_terms(token, split, chunk, charges, present, left, right, wave, rotations):
    count, sectors, width, _ = left.shape
    if split:
        few = grouped_few(sectors)
        shapes = [
            ((2 + few, width // 2, width), BF16),
            ((sectors - few, width // 2, width), BF16),
            ((sectors + 2, width // 2, width), F32),
        ]
    else:
        shapes = [((sectors + 2, width, width), F32)]
    shapes.append(((sectors, width, width), BF16))
    return kernel_call(
        functools.partial(sigma_kernel, split, chunk),
        token,
        (in_hbm(charges), in_hbm(present), left, in_hbm(right), wave, rotations),
        [HBM, HBM, VMEM, HBM, VMEM, VMEM],
        [pltpu.VMEM(*shape) for shape in shapes],
        [VMEM] * len(shapes),
        scratch_shapes=[
            pltpu.VMEM((sectors + 2, width, width), F32),
            pltpu.VMEM(right.shape, BF16),
            pltpu.SMEM((count,), jnp.int32),
            pltpu.SMEM((count, sectors), jnp.int32),
            pltpu.SemaphoreType.DMA,
            pltpu.SemaphoreType.DMA((count,)),
        ],
        mib=10,
        cost_estimate=estimate(0),
        name="sigma_terms",
    )


def edges_kernel(keep, got, turned, first, second):
    outer, height, _ = keep.shape
    odd = lax.rem(lax.axis_index("sec"), 2)
    for out, upward in ((first, odd == 0), (second, odd == 1)):
        edge = jnp.where(upward, outer - 1, 0)
        out[:height] = (keep[edge] + got[jnp.where(upward, 1, 0)].astype(F32)).astype(BF16)
        out[height:] = turned[jnp.where(upward, outer - 3, 0)]


def edges(token, keep, got, turned):
    _, height, width = keep.shape
    shape = (height + turned.shape[1], width)
    return kernel_call(
        edges_kernel,
        token,
        (keep, got, turned),
        [VMEM] * 3,
        [jax.ShapeDtypeStruct(shape, BF16)] * 2,
        [VMEM] * 2,
        mib=4,
        cost_estimate=estimate(0),
        name="edges",
    )


def split_kernel(bit, chunk, levels, first, held, *refs):
    if first:
        *core, one, two, send, keep = refs
    else:
        got, send, keep = refs
    sectors, height = send.shape[0], held.shape[1]
    own = lax.rem(lax.axis_index("op") // bit, 2)
    level = lax.axis_index("sec")
    odd = lax.rem(level, 2) == 1

    def total(s, rows):
        if not first:
            return held[s, rows] + got[s, rows].astype(F32)
        group, place = grouped(s + 1, sectors)
        value = held[s + 1, rows] + core[group][place, rows].astype(F32)
        if s == 0:
            below = jnp.where(odd, one[rows], two[rows]).astype(F32)
            value = value + jnp.where(level > 0, below, 0.0)
        if s == sectors - 1:
            above = jnp.where(odd, two[rows], one[rows]).astype(F32)
            value = value + jnp.where(level < levels - 1, above, 0.0)
        return value

    for q in range(height // chunk // 2):
        to = slice(q * chunk, (q + 1) * chunk)
        for s in range(sectors):
            send[s, to] = total(s, pl.ds((2 * q + 1 - own) * chunk, chunk)).astype(BF16)
            keep[s, to] = total(s, pl.ds((2 * q + own) * chunk, chunk))


def split(token, bit, chunk, levels, held, *got):
    first = len(got) > 1
    outer, height, width = held.shape
    sectors = outer - 2 if first else outer
    return kernel_call(
        functools.partial(split_kernel, bit, chunk, levels, first),
        token,
        (held, *got),
        [VMEM] * (1 + len(got)),
        [
            jax.ShapeDtypeStruct((sectors, height // 2, width), BF16),
            jax.ShapeDtypeStruct((sectors, height // 2, width), F32),
        ],
        [VMEM] * 2,
        mib=4,
        cost_estimate=estimate(0 if first else 1.3),
        name="split",
    )


def hold_kernel(*refs):
    pass


def hold(token, *values, cost=0):
    return kernel_call(
        hold_kernel,
        token,
        values,
        [ANY] * len(values),
        [jax.ShapeDtypeStruct(value.shape, value.dtype) for value in values],
        [ANY] * len(values),
        aliases={i: i for i in range(len(values))},
        mib=1,
        cost_estimate=estimate(cost),
        name="hold",
    )


def choose_kernel(half, parts, lead, front, rear, second, *outs):
    end = at_end(half)
    width = second.shape[1]

    @pl.when(end)
    def _():
        for out, (begin, stop) in zip(outs, parts):
            for s in range(begin, stop):
                source, at = (front, s) if s < lead else (rear, s - lead)
                out[(s - begin) * width : (s - begin + 1) * width] = source[
                    at * width : (at + 1) * width
                ]

    @pl.when(jnp.logical_not(end))
    def _():
        for out, (begin, stop) in zip(outs, parts):
            out[...] = second[begin * width : stop * width]


def choose(token, half, parts, lead, front, rear, second):
    width = second.shape[1]
    return kernel_call(
        functools.partial(choose_kernel, half, parts, lead),
        token,
        (front, rear, second),
        [VMEM] * 3,
        [pltpu.VMEM(((stop - begin) * width, width), BF16) for begin, stop in parts],
        [VMEM] * len(parts),
        mib=4,
        cost_estimate=estimate(0.9),
        name="choose",
    )


def frame_kernel(offset, turned, one, two, framed):
    sectors, width, _ = turned.shape
    raised = lax.rem(lax.axis_index("sec"), 2) == 1
    rows = pl.ds(offset, width)

    @pl.when(raised)
    def _():
        framed[0] = one[rows]
        framed[sectors + 1] = two[rows]

    @pl.when(jnp.logical_not(raised))
    def _():
        framed[0] = two[rows]
        framed[sectors + 1] = one[rows]

    for s in range(sectors):
        framed[s + 1] = turned[s]


def frame(token, offset, turned, one, two):
    sectors, width, _ = turned.shape
    return kernel_call(
        functools.partial(frame_kernel, offset),
        token,
        (turned, one, two),
        [VMEM] * 3,
        [pltpu.VMEM((sectors + 2, width, width), BF16)],
        [VMEM],
        mib=4,
        cost_estimate=estimate(0),
        name="frame",
    )


def renorm_kernel(items, zero, levels, half, scale, framed, rotations, *refs):
    if scale is not None:
        keep, got, *refs = refs
    buffers = refs[: 1 + max(buffer for came, told, *_ in items for buffer in (came[0], told[0]))]
    rest = refs[len(buffers) + (0 if zero else 1) :]
    if scale is not None:
        sigma, *rest, total = [rest[1], rest[0], *rest[2:]]
    out, results, done = rest
    sectors, width, _ = rotations.shape
    odd = lax.rem(lax.axis_index("op"), 2)
    end = at_end(half)
    level = lax.axis_index("sec")
    height = meta_rows(sectors)
    stores = []
    if scale is not None:
        total[...] = (keep[...] + got[...].astype(F32)) * scale
        copy = pltpu.make_async_copy(total, sigma, done)
        copy.start()
        stores.append(copy)
    if zero:
        results[len(items)] = jnp.zeros_like(results[len(items)])
        for place in range(CAPS):
            copy = pltpu.make_async_copy(results.at[len(items)], out.at[place], done)
            copy.start()
            stores.append(copy)
    kinds = {"core": 2 - odd, "side": 1 + odd, "half": 3}
    for i, ((buffer, base), (about, top, slot), targets, begin, stop) in enumerate(items):
        values = buffers[about][pl.ds(top, height)].astype(F32)
        values = values[slot * (height // 2) : (slot + 1) * (height // 2)]
        charge = jnp.max(values[:1]).astype(jnp.int32)
        kind, place = (kinds[targets[0][0]], targets[0][1])
        if len(targets) > 1:
            kind = jnp.where(end, kind, kinds[targets[1][0]])
            place = jnp.where(end, place, targets[1][1])
        weights = values[2 : 2 + sectors]
        named = jnp.where(values[1:2] == jnp.asarray(kind).astype(F32), weights, 0.0)
        weights = jnp.where(place == 1, named, weights)
        for s in range(begin, stop):
            at = s + charge
            whole = level * sectors + at
            inside = jnp.logical_and(whole >= 0, whole < levels * sectors)
            weight = jnp.where(inside, weights[s : s + 1], 0.0)
            block = buffers[buffer][pl.ds(base + (s - begin) * width, width)]
            rotated = jnp.dot(block, rotations[s], preferred_element_type=F32).astype(BF16)
            target = framed[jnp.clip(at + 1, 0, sectors + 1)]
            value = jnp.dot(target, rotated, preferred_element_type=F32) * weight
            results[i, s] = value.astype(BF16)
            copy = pltpu.make_async_copy(results.at[i, s], out.at[kind * CAPS + place, s], done)
            copy.start()
            stores.append(copy)
    for copy in stores:
        copy.wait()


def renorm(
    token, name, items, buffers, out, levels, half, framed, rotations, cost=0, sums=(), scale=None
):
    sectors, width, _ = rotations.shape
    zero = out is None
    operands = [framed, rotations, *sums, *buffers]
    in_specs = [VMEM] * len(operands)
    if not zero:
        operands.append(out)
        in_specs.append(HBM)
    count = len(items)
    block = (sectors, width, width)
    return kernel_call(
        functools.partial(renorm_kernel, items, zero, levels, half, scale),
        token,
        operands,
        in_specs,
        [
            jax.ShapeDtypeStruct((DIRS * CAPS, *block), BF16),
            *(jax.ShapeDtypeStruct(x.shape, F32) for x in sums[:1]),
        ],
        [HBM] * (1 + len(sums[:1])),
        aliases={} if zero else {len(operands) - 1: 0},
        scratch_shapes=[
            pltpu.VMEM((count + (1 if zero else 0), *block), BF16),
            pltpu.SemaphoreType.DMA,
            *(pltpu.VMEM(x.shape, F32) for x in sums[:1]),
        ],
        mib=10,
        cost_estimate=estimate(cost),
        name=name,
    )


def body(
    wavefunction, left_operators, right_operators, rotations, charges, present_blocks, directions
):
    sectors, width, _ = wavefunction.shape
    pairs = left_operators.shape[0]
    n = lax.axis_size("op")
    levels = lax.axis_size("sec")
    half = n // 2
    chunk = width // n
    halving = n >= 4 and n & (n - 1) == 0 and chunk % 16 == 0
    rows = sectors * width
    parts = [(0, 3 * sectors // 4), (3 * sectors // 4, sectors)] if sectors > 1 else [(0, 1)]

    def over_op(value, target):
        return lax.ppermute(value, "op", [(i, target(i)) for i in range(n)])

    def swapped(value, start):
        to = list(range(levels))
        for i in range(start, levels - 1, 2):
            to[i], to[i + 1] = i + 1, i
        return lax.ppermute(value, "sec", list(enumerate(to)))

    def side(i):
        return (i + 1) % n if i % 2 else (i - 1) % n

    def end(i):
        return i % half in (0, half - 1)

    def opposite(i):
        return (i + half) % n

    def relay(i):
        return i - i % half + half - 1 - i % half

    small = (directions[:, 0], charges, present_blocks)
    ahead_roles = (("extra", "side"), ("half", "extra"))
    behind_roles = (("side", "extra"), ("extra", "half"))
    core_roles = ("extra", "core")
    lead = min(2, sectors)
    whole = (0, sectors)
    token, (front, had) = staged(
        None, ((ahead_roles, (), 0, lead),), half, *small, left_operators
    )
    token, (rear, behind, last, first_core, left, wave, turn) = staged(
        token,
        (
            (ahead_roles, ahead_roles, lead, sectors),
            (behind_roles[:1], behind_roles, *whole),
            (("half",), (), *whole),
            (core_roles, core_roles, *whole),
        ),
        half,
        *small,
        left_operators,
        wavefunction,
        rotations,
        had=(had,),
    )
    got_front, got_rear = [
        over_op(x, lambda i: opposite(i) if end(i) else side(i)) for x in (front, rear)
    ]
    got_behind = over_op(behind, lambda i: side(i) if end(i) else opposite(i))
    from_core = over_op(first_core, lambda i: i ^ 1)
    token, (*terms, turned) = sigma_terms(
        token, halving, chunk, charges, present_blocks, left, right_operators, wave, turn
    )

    if halving:
        send_edges, send, keep = terms
        got_edges = over_op(send_edges, lambda i: i ^ 1)
        got = over_op(send, lambda i: i ^ 1)
        token, (got_front,) = hold(token, got_front, cost=1.75)
        token, (got,) = hold(token, got)
        token, (first, second) = edges(token, keep, got_edges, turned)
        one, two = swapped(first, 0), swapped(second, 1)
        offset = width // 2
        token, (one,) = hold(token, one, cost=0.6)
        bit = 2
        token, (send, keep) = split(token, bit, chunk, levels, keep, got_edges, got, one, two)
        got = over_op(send, lambda i: i ^ 2)
        token, (framed,) = frame(token, offset, turned, one, two)
        token, last = choose(token, half, parts, lead, got_front, got_rear, last)
        while 2 * bit < n:
            bit *= 2
            token, (send, keep) = split(token, bit, chunk, levels, keep, got)
            got = over_op(send, lambda i, bit=bit: i ^ bit)
    else:
        (terms,) = terms
        offset = width
        odd = lax.rem(lax.axis_index("sec"), 2) == 1
        level = lax.axis_index("sec")
        upward = jnp.concatenate([terms[sectors + 1].astype(BF16), turned[sectors - 1]])
        downward = jnp.concatenate([terms[0].astype(BF16), turned[0]])
        one = swapped(jnp.where(odd, downward, upward), 0)
        two = swapped(jnp.where(odd, upward, downward), 1)
        below = jnp.where(odd, one, two)[:width].astype(F32)
        above = jnp.where(odd, two, one)[:width].astype(F32)
        mid = terms[1 : sectors + 1]
        mid = mid.at[0].add(jnp.where(level > 0, below, 0.0))
        mid = mid.at[sectors - 1].add(jnp.where(level < levels - 1, above, 0.0))
        summed = lax.psum_scatter(mid, "op", scatter_dimension=1, tiled=True)
        token, (framed,) = frame(token, offset, turned, one, two)
        token, last = choose(token, half, parts, lead, got_front, got_rear, last)

    got_last = [over_op(x, lambda i: relay(i) if end(i) else opposite(i)) for x in last]
    fixed = (levels, half, framed, turn)
    tail = (sectors - lead) * width
    told = 2 * tail
    token, (out,) = renorm(
        token,
        "renorm_first",
        (
            ((0, 0), (0, 2 * rows, 0), (("core", 1),), *whole),
            ((0, rows), (0, 2 * rows, 1), (("core", 0),), *whole),
            ((1, 0), (2, told, 0), (("half", 1), ("side", 0)), 0, lead),
            ((2, 0), (2, told, 0), (("half", 1), ("side", 0)), lead, sectors),
            ((1, lead * width), (2, told, 1), (("half", 0), ("side", 1)), 0, lead),
            ((2, tail), (2, told, 1), (("half", 0), ("side", 1)), lead, sectors),
            ((3, 0), (3, rows, 0), (("side", 0), ("half", 1)), *whole),
        ),
        (from_core, got_front, got_rear, got_behind),
        None,
        *fixed,
        cost=1.75,
    )
    scale = 1.0 / math.sqrt(pairs * n)
    for i, (begin, stop) in enumerate(parts):
        token, (out, *sigma_vector) = renorm(
            token,
            "renorm_last",
            (((0, 0), (1, rows, 1), (("side", 1), ("half", 0)), begin, stop),),
            (got_last[i], got_behind),
            out,
            *fixed,
            sums=(keep, got) if halving and i == len(parts) - 1 else (),
            scale=scale if halving and i == len(parts) - 1 else None,
        )
    if not halving:
        sigma_vector = [summed * scale]
    return sigma_vector[0], out


def solution(mesh):
    placed = (
        P("sec", None, None),
        P("op", "sec", None, None),
        P("op", "sec", None, None),
        P("sec", None, None),
        P("op"),
        P("op", "sec"),
        P("op", None),
    )
    return jax.shard_map(
        body,
        mesh=mesh,
        in_specs=placed,
        out_specs=(P("sec", "op", None), P("op", "sec", None, None)),
        check_vma=False,
    )
```
